256 devices in a mesh: tm: 4 (over x_lo, core), space: 64 (over x_hi, y, z).
Axes of the slice: x: 4 (x_hi: 2, x_lo: 2; x = x_hi * 2 + x_lo), y: 4, z: 8, core: 2. Of those that a mesh axis runs over, the one named last changes fastest.
Arguments:
- tokens: bfloat16 [2, 4, 6144, 1152], P(None, 'tm', 'space'), may hold values from -6 to 6
- modulation: float32 [6, 1152], replicated, may hold values from -3 to 3
- spatial_qkv: bfloat16 [1152, 3456], P('space'), may hold values from -0.1875 to 0.1875
- spatial_out: bfloat16 [1152, 1152], P('space'), may hold values from -0.1875 to 0.1875
- temporal_qkv: bfloat16 [1152, 3456], P('space'), may hold values from -0.1875 to 0.1875
- temporal_out: bfloat16 [1152, 1152], P('space'), may hold values from -0.1875 to 0.1875
- norm_gains: float32 [4, 72], replicated, may hold values from 1 to 2.5
Outputs:
- block_out: bfloat16 [2, 4, 6144, 1152], P(None, 'tm', 'space')
The draws below stay inside these ranges and needn't reach their ends.
All inputs are finite; a program needn't handle non-finite values.
Results may differ from the reference program's by a relative error of at most 0.01.
Values may be sent and summed in bfloat16 or wider, within the bound.
No kernel may reach another device: no remote copies, remote signals or barrier semaphores. Data moves between devices by JAX's collectives and lax.ppermute only.
A program may use at most 128 MiB of HBM per device.

```python
import math
import jax
import jax.numpy as jnp
from jax import lax

D = 1152
HEADS = 16
CLIPS = 2
HEAD_DIM = 72
FRAME_TOKENS = 6144
FRAMES = 4


def block_levels(own_key, extent, shards, smallest, largest):
    def one(position, shards_of):
        steps = jax.random.uniform(jax.random.fold_in(jax.random.fold_in(own_key, 6), position), (shards_of,), jnp.float32, smallest / len(shards), largest / len(shards))
        return jnp.repeat(jnp.exp(steps), extent[position] // shards_of).reshape((-1,) + (1,) * (len(extent) - position - 1))

    loudness = one(*shards[0])
    for cut in shards[1:]:
        loudness = loudness * one(*cut)
    return loudness


def noise(own_key, extent, width, reach, pieces=(), dtype=jnp.bfloat16):
    level = block_levels(own_key, extent, pieces, -0.22, 0.18) if pieces else 1.0
    values = jax.random.normal(own_key, extent, jnp.float32) * width * level
    return jnp.minimum(jnp.maximum(values, -reach), reach).astype(dtype)


def setup_inputs(seed: int = 0) -> dict:
    streams_of = jax.random.split(jax.random.key(seed), 8)
    return {
        "tokens": noise(streams_of[0], (CLIPS, FRAMES, FRAME_TOKENS, D), 1.0, 6.0, ((1, 4), (2, 64))),
        "modulation": noise(streams_of[1], (6, D), 0.5, 3.0, (), jnp.float32),
        "spatial_qkv": noise(streams_of[2], (D, 3 * D), D ** -0.5, 0.1875, ((0, 64),)),
        "spatial_out": noise(streams_of[3], (D, D), D ** -0.5, 0.1875, ((0, 64),)),
        "temporal_qkv": noise(streams_of[4], (D, 3 * D), D ** -0.5, 0.1875, ((0, 64),)),
        "temporal_out": noise(streams_of[5], (D, D), D ** -0.5, 0.1875, ((0, 64),)),
        "norm_gains": jnp.clip(jnp.exp(jax.random.uniform(streams_of[6], (4, HEAD_DIM), jnp.float32, math.log(1.0), math.log(2.5))), 1.0, 2.5),
    }


def layer_norm(values):
    mean_val = lax.optimization_barrier(jnp.mean(values, -1, keepdims=True))
    centred = values - mean_val
    variance = lax.optimization_barrier(jnp.mean(centred * centred, -1, keepdims=True))
    return centred * lax.rsqrt(variance + 1e-06)

def rms_heads(values, gain):
    return values * lax.rsqrt(lax.optimization_barrier(jnp.mean(values * values, -1, keepdims=True)) + 1e-06) * gain

def attend(queries, keys, values):
    block_rows = math.gcd(queries.shape[0], 512)
    factor = 1.0 / math.sqrt(HEAD_DIM)

    def one_block(query_block):
        scores = jnp.dot(query_block, keys.T, preferred_element_type=jnp.float32) * factor
        expo = jnp.exp(scores)
        totals = lax.optimization_barrier(jnp.sum(expo, -1))
        result = jnp.dot(expo.astype(jnp.bfloat16), values, preferred_element_type=jnp.float32) / totals[:, None]
        return result.astype(jnp.bfloat16)
    blocks = lax.map(one_block, queries.reshape(-1, block_rows, HEAD_DIM))
    return blocks.reshape(-1, HEAD_DIM)

def attend_triple(triple):
    return attend(triple[0], triple[1], triple[2])

def one_clip(tokens, modulation, spatial_qkv, spatial_out, temporal_qkv, temporal_out, norm_gains):
    frames = tokens.shape[0]
    length = tokens.shape[1]
    factor = 1.0 / math.sqrt(HEAD_DIM)
    start = tokens.astype(jnp.float32)
    normed = (layer_norm(start) * (1.0 + modulation[1]) + modulation[0]).astype(jnp.bfloat16)
    projected = jnp.dot(normed.reshape(-1, D), spatial_qkv, preferred_element_type=jnp.float32)
    projected = projected.reshape(frames, length, 3, HEADS, HEAD_DIM)
    query_a = rms_heads(projected[:, :, 0], norm_gains[0]).astype(jnp.bfloat16)
    key_a = rms_heads(projected[:, :, 1], norm_gains[1]).astype(jnp.bfloat16)
    value_a = projected[:, :, 2].astype(jnp.bfloat16)

    def per_head(array):
        return array.transpose(0, 2, 1, 3).reshape(frames * HEADS, length, HEAD_DIM)
    attended = lax.map(attend_triple, (per_head(query_a), per_head(key_a), per_head(value_a)))
    attended = attended.reshape(frames, HEADS, length, HEAD_DIM).transpose(0, 2, 1, 3).reshape(frames * length, D)
    branch_a = jnp.dot(attended, spatial_out, preferred_element_type=jnp.float32)
    resid = start + modulation[2] * branch_a.reshape(frames, length, D)
    normed_b = (layer_norm(resid) * (1.0 + modulation[4]) + modulation[3]).astype(jnp.bfloat16)
    proj_b = jnp.dot(normed_b.reshape(-1, D), temporal_qkv, preferred_element_type=jnp.float32)
    proj_b = proj_b.reshape(frames, length, 3, HEADS, HEAD_DIM)
    query_b = rms_heads(proj_b[:, :, 0], norm_gains[2]).astype(jnp.bfloat16)
    key_b = rms_heads(proj_b[:, :, 1], norm_gains[3]).astype(jnp.bfloat16)
    value_b = proj_b[:, :, 2].astype(jnp.bfloat16)
    scores = jnp.einsum('flhd,glhd->lhfg', query_b.astype(jnp.float32), key_b.astype(jnp.float32)) * factor
    expo = jnp.exp(scores)
    totals = lax.optimization_barrier(jnp.sum(expo, -1))
    rounded = lax.optimization_barrier(expo.astype(jnp.bfloat16)).astype(jnp.float32)
    mixed = jnp.einsum('lhfg,glhd->flhd', rounded, value_b.astype(jnp.float32))
    mixed = (mixed / totals.transpose(2, 0, 1)[..., None]).astype(jnp.bfloat16)
    branch_b = jnp.dot(mixed.reshape(-1, D), temporal_out, preferred_element_type=jnp.float32)
    result = resid + modulation[5] * branch_b.reshape(frames, length, D)
    return result.astype(jnp.bfloat16)

def reference(tokens, modulation, spatial_qkv, spatial_out, temporal_qkv, temporal_out, norm_gains):
    outputs = []
    for clip in range(tokens.shape[0]):
        outputs.append(one_clip(tokens[clip], modulation, spatial_qkv, spatial_out, temporal_qkv, temporal_out, norm_gains))
    return jnp.stack(outputs, 0)
```

```python
import math

import jax
import jax.numpy as jnp
from jax import lax
from jax.experimental import pallas as pl
from jax.experimental.pallas import tpu as pltpu
from jax.sharding import Mesh
from jax.sharding import PartitionSpec as P

D = 1152
HEADS = 16
HD = 72
HP = 80
PATCH = 96
ROWS = 2 * PATCH
NZ, NY = 8, 4
PLANE = NZ * PATCH
BF = jnp.bfloat16
F32 = jnp.float32
FACTOR = 1.0 / math.sqrt(HD)
TN = (((0,), (0,)), ((), ()))
TT = (((0,), (1,)), ((), ()))
PARAMS = pltpu.CompilerParams(vmem_limit_bytes=48 * 1024 * 1024)


def normalise(values):
    mean_val = jnp.mean(values, -1, keepdims=True)
    centred = values - mean_val
    variance = jnp.mean(centred * centred, -1, keepdims=True)
    return centred * lax.rsqrt(variance + 1e-06)


def rms(values, gain):
    mean_sq = jnp.mean(values * values, 0, keepdims=True)
    return values * lax.rsqrt(mean_sq + 1e-06) * gain


def spatial_proj(tok_ref, mod_ref, w_ref, gain_ref, out_ref):
    cols = 4 * PATCH
    zeros = jnp.zeros((HP - HD, cols), F32)
    first = lax.broadcasted_iota(jnp.int32, (HP - HD, cols), 0) == 0
    ones = jnp.where(first, 1.0, 0.0)
    for clip in range(2):
        tok = tok_ref[:, clip * PATCH : (clip + 1) * PATCH, :].reshape(cols, D).astype(F32)
        normed = normalise(tok) * (1.0 + mod_ref[1:2, :]) + mod_ref[0:1, :]
        proj = lax.dot_general(w_ref[...], normed.astype(BF), TT, preferred_element_type=F32)
        for head in range(2):
            query, key, value = (
                proj[part * 2 * HD + head * HD : part * 2 * HD + (head + 1) * HD] for part in range(3)
            )
            query = rms(query, gain_ref[:, 0:1]) * (FACTOR * math.log2(math.e))
            key = rms(key, gain_ref[:, 1:2])
            place = clip * 2 + head
            parts = [key, zeros, value, ones, query, zeros]
            out_ref[place] = jnp.concatenate(parts, 0).astype(BF)


def attend_step(q_ref, kv_ref, keys, acc):
    query = jnp.concatenate([q_ref[0], jnp.zeros((128 - HP, PLANE), BF)], 0)
    total = None
    for part in range(PLANE // 256):
        here = slice(part * 256, (part + 1) * 256)
        score = jnp.dot(keys[here, :], query, preferred_element_type=F32)
        expo = jnp.exp2(score).astype(BF)
        add = jnp.dot(kv_ref[0, HP : 2 * HP, here], expo, preferred_element_type=F32)
        total = add if total is None else total + add
    return acc + total


def turn_keys(kv_ref, keys):
    wide = jnp.concatenate([kv_ref[0, :HP].astype(F32), jnp.zeros((128 - HP, PLANE), F32)], 0)
    keys[...] = wide.T.astype(BF)


def attend_own(q_ref, kv_ref, out_ref, keys, sums):
    step, block = pl.program_id(0), pl.program_id(1)

    @pl.when(block == 0)
    def _():
        turn_keys(kv_ref, keys)

    @pl.when(step == 0)
    def _():
        sums[block] = jnp.zeros((HP, PLANE), F32)

    sums[block] = attend_step(q_ref, kv_ref, keys, sums[block])

    @pl.when(step == NY - 1)
    def _():
        out_ref[0] = sums[block]


def attend_other(q_ref, kv_ref, part_ref, out_ref, keys, sums):
    step, block = pl.program_id(0), pl.program_id(1)

    @pl.when(block == 0)
    def _():
        turn_keys(kv_ref, keys)

    @pl.when(step == 0)
    def _():
        sums[block] = part_ref[0]

    sums[block] = attend_step(q_ref, kv_ref, keys, sums[block])

    @pl.when(step == NY - 1)
    def _():
        done = sums[block]
        done = done[:HD] / done[HD : HD + 1]
        for z in range(NZ):
            out_ref[0, z] = done[:, z * PATCH : (z + 1) * PATCH].astype(BF)


Q_SPEC = pl.BlockSpec((1, HP, PLANE), lambda k, q: (q, 2, 0))
KV_SPEC = pl.BlockSpec((1, 2 * HP, PLANE), lambda k, q: (k, 0, 0))
SCRATCH = [pltpu.VMEM((PLANE, 128), BF), pltpu.VMEM((NY, HP, PLANE), F32)]
COST = pl.CostEstimate(
    flops=4 * 128 * (NY * PLANE) ** 2, bytes_accessed=8_000_000, transcendentals=(NY * PLANE) ** 2
)


def last_only(k, q):
    return jnp.where(k == NY - 1, q, 0)


def first_only(k, q):
    return jnp.where(k == 0, q, NY - 1)


def attention_own(own):
    return pl.pallas_call(
        attend_own,
        grid=(NY, NY),
        in_specs=[Q_SPEC, KV_SPEC],
        out_specs=pl.BlockSpec((1, HP, PLANE), lambda k, q: (last_only(k, q), 0, 0)),
        out_shape=jax.ShapeDtypeStruct((NY, HP, PLANE), F32),
        scratch_shapes=SCRATCH,
        compiler_params=PARAMS,
        cost_estimate=COST,
        name="attend_own",
    )(own, own)


def attention_other(own, other, part):
    part_spec = pl.BlockSpec((1, HP, PLANE), lambda k, q: (first_only(k, q), 0, 0))
    return pl.pallas_call(
        attend_other,
        grid=(NY, NY),
        in_specs=[Q_SPEC, KV_SPEC, part_spec],
        out_specs=pl.BlockSpec((1, NZ, HD, PATCH), lambda k, q: (last_only(k, q), 0, 0, 0)),
        out_shape=jax.ShapeDtypeStruct((NY, NZ, HD, PATCH), BF),
        scratch_shapes=SCRATCH,
        compiler_params=PARAMS,
        cost_estimate=COST,
        name="attend_other",
    )(own, other, part)


def spatial_end(place_ref, att_ref, tok_ref, mod_ref, own, got, resid_ref, norm_ref):
    weight = jnp.where(place_ref[0] == 1, got[...], own[...])
    rows = []
    for clip in range(2):
        feats = [
            att_ref[clip * 2 + head, pair].astype(F32) for pair in range(NZ) for head in range(2)
        ]
        rows.append(jnp.concatenate(feats, 0).T.astype(BF))
    attended = jnp.concatenate(rows, 0)
    branch = jnp.dot(attended, weight, preferred_element_type=F32)
    resid = tok_ref[...].astype(F32) + mod_ref[2:3, :] * branch
    resid_ref[...] = resid
    norm_ref[...] = (normalise(resid) * (1.0 + mod_ref[4:5, :]) + mod_ref[3:4, :]).astype(BF)


def temporal(place_ref, n0, n1, n2, n3, weight, gain_ref, o0, o1, o2, o3):
    queries, keys, values = [], [], []
    for norm_ref in (n0, n1, n2, n3):
        proj = lax.dot_general(weight[...], norm_ref[...], TT, preferred_element_type=F32)
        heads = [proj[n * HD : (n + 1) * HD] for n in range(12)]
        queries.append([rms(v, gain_ref[:, 2:3]).astype(BF).astype(F32) for v in heads[:4]])
        keys.append([rms(v, gain_ref[:, 3:4]).astype(BF).astype(F32) for v in heads[4:8]])
        values.append([v.astype(BF).astype(F32) for v in heads[8:]])
    for f, out_ref in enumerate((o0, o1, o2, o3)):
        mixed = []
        for head in range(4):
            total, attended = 0.0, 0.0
            for g in range(4):
                score = jnp.sum(queries[f][head] * keys[g][head], 0, keepdims=True) * FACTOR
                expo = jnp.exp(score)
                total = total + expo
                attended = attended + expo.astype(BF).astype(F32) * values[g][head]
            mixed.append(attended / total)
        out_ref[...] = jnp.concatenate(mixed, 0).astype(BF)


def temporal_end(place_ref, m0, m1, m2, m3, resid_ref, mod_ref, own, got, out_ref):
    core = place_ref[0] == 1
    branch = None
    for step, att_ref in enumerate((m0, m1, m2, m3)):
        here = pl.ds(pl.multiple_of((place_ref[1] ^ step) * (4 * HD), 4 * HD), 4 * HD)
        rows = jnp.where(core, own[here, :], got[here, :])
        add = jnp.dot(att_ref[...].astype(F32).T.astype(BF), rows, preferred_element_type=F32)
        branch = add if branch is None else branch + add
    out_ref[...] = (resid_ref[...] + mod_ref[5:6, :] * branch).astype(BF)


def whole(shapes, kernel, name, *args):
    smem = pl.BlockSpec(memory_space=pltpu.SMEM)
    vmem = pl.BlockSpec(memory_space=pltpu.VMEM)
    return pl.pallas_call(
        kernel,
        in_specs=[smem] + [vmem] * (len(args) - 1),
        out_specs=[vmem] * len(shapes),
        out_shape=shapes,
        compiler_params=PARAMS,
        name=name,
    )(*args)


def per_device(tokens, modulation, spatial_qkv, spatial_out, temporal_qkv, temporal_out, norm_gains):
    core = lax.axis_index("c")
    frame = lax.axis_index("xl") * 2 + core
    place = jnp.stack([core, frame]).astype(jnp.int32)
    gains = norm_gains.T
    tok = tokens.reshape(ROWS, D)

    shard = spatial_qkv.reshape(18, 3, NZ, 2 * HD).transpose(2, 0, 1, 3).reshape(NZ, 18, 6 * HD)
    shard = jnp.pad(shard, ((0, 0), (0, 0), (0, 512 - 6 * HD)))
    part_b = lax.dynamic_slice_in_dim(temporal_qkv.reshape(18, 3, D), frame * 4 * HD, 4 * HD, 2)
    part_b = part_b.reshape(18, 12 * HD)
    bundle = jnp.concatenate([jnp.where(core == 0, spatial_out, temporal_out), part_b], 1)
    shard = jnp.concatenate([shard, jnp.broadcast_to(bundle, (NZ, 18, D + 12 * HD))], 2)
    shard = lax.all_to_all(shard, "z", 0, 0, tiled=True).reshape(NZ * 18, 512 + D + 12 * HD)
    weight_a = jnp.broadcast_to(shard[None, :, : 6 * HD], (8, NZ * 18, 6 * HD))
    weight_a = lax.all_to_all(weight_a, ("xh", "y"), 0, 0, tiled=True).reshape(D, 6 * HD)

    column = lax.all_gather(tok, "z", axis=0)
    projected = pl.pallas_call(
        spatial_proj,
        grid=(2,),
        in_specs=[
            pl.BlockSpec((4, ROWS, D), lambda i: (i, 0, 0)),
            pl.BlockSpec((6, D), lambda i: (0, 0)),
            pl.BlockSpec((D, 6 * HD), lambda i: (0, 0)),
            pl.BlockSpec((HD, 4), lambda i: (0, 0)),
        ],
        out_specs=pl.BlockSpec((4, 3 * HP, 4 * PATCH), lambda i: (0, 0, i)),
        out_shape=jax.ShapeDtypeStruct((4, 3 * HP, PLANE), BF),
        compiler_params=PARAMS,
        name="spatial_proj",
    )(column, modulation, weight_a, gains)

    swap = [(0, 1), (1, 0)]
    bundle, projected = lax.optimization_barrier((shard[:, 512:], projected))
    outs_own = lax.all_gather(bundle[:, :D], ("xh", "y"), axis=0, tiled=True)
    weight_b = lax.all_gather(bundle[:, D:], ("xh", "y"), axis=0, tiled=True)

    projected = lax.all_to_all(projected, "y", 0, 0, tiled=True)
    other = lax.ppermute(projected[:, : 2 * HP], "xh", swap)
    part = attention_own(projected)
    attended = attention_other(projected, other, part)
    attended, outs_own = lax.optimization_barrier((attended, outs_own))
    outs_got = lax.ppermute(outs_own, "c", swap)
    attended = attended.reshape(NY * NZ, HD, PATCH)
    attended = lax.all_to_all(attended, ("y", "z"), 0, 0, tiled=True)
    attended = attended.reshape(4, NZ, HD, PATCH)

    resid, normed_b = whole(
        [jax.ShapeDtypeStruct((ROWS, D), F32), jax.ShapeDtypeStruct((ROWS, D), BF)],
        spatial_end,
        "spatial_end",
        place, attended, tok, modulation, outs_own, outs_got,
    )
    norm_c = lax.ppermute(normed_b, "c", swap)
    norm_x = lax.ppermute(normed_b, "xl", swap)
    norm_cx = lax.ppermute(norm_x, "c", swap)
    mixed = whole(
        [jax.ShapeDtypeStruct((4 * HD, ROWS), BF)] * 4,
        temporal,
        "temporal",
        place, normed_b, norm_c, norm_x, norm_cx, weight_b, gains,
    )
    mixed = [
        mixed[0],
        lax.ppermute(mixed[1], "c", swap),
        lax.ppermute(mixed[2], "xl", swap),
        lax.ppermute(mixed[3], ("xl", "c"), [(0, 3), (3, 0), (1, 2), (2, 1)]),
    ]
    (result,) = whole(
        [jax.ShapeDtypeStruct((ROWS, D), BF)],
        temporal_end,
        "temporal_end",
        place, *mixed, resid, modulation, outs_own, outs_got,
    )
    return result.reshape(2, 1, PATCH, D)


def solution(mesh):
    fine = Mesh(mesh.devices.reshape(2, 2, 2, NY, NZ), ("xl", "c", "xh", "y", "z"))
    time, space = ("xl", "c"), ("xh", "y", "z")
    block = P(None, time, space, None)
    rows = P(space, None)
    return jax.shard_map(
        per_device,
        mesh=fine,
        in_specs=(block, P(), rows, rows, rows, rows, P()),
        out_specs=block,
        check_vma=False,
    )
```

```python
import functools
import math

import jax
import jax.numpy as jnp
from jax import lax
from jax.experimental import pallas as pl
from jax.experimental.pallas import tpu as pltpu
from jax.sharding import Mesh
from jax.sharding import PartitionSpec as P

D = 1152
HEADS = 16
HD = 72
HP = 80
PATCH = 96
ROWS = 2 * PATCH
NZ, NY = 8, 4
PLANE = NZ * PATCH
BF = jnp.bfloat16
F32 = jnp.float32
FACTOR = 1.0 / math.sqrt(HD)
TN = (((0,), (0,)), ((), ()))
NT = (((1,), (1,)), ((), ()))
TT = (((0,), (1,)), ((), ()))
PARAMS = pltpu.CompilerParams(vmem_limit_bytes=48 * 1024 * 1024)


def normalise(values):
    mean_val = jnp.mean(values, -1, keepdims=True)
    centred = values - mean_val
    variance = jnp.mean(centred * centred, -1, keepdims=True)
    return centred * lax.rsqrt(variance + 1e-06)


def rms(values, gain):
    mean_sq = jnp.mean(values * values, 0, keepdims=True)
    return values * lax.rsqrt(mean_sq + 1e-06) * gain


def spatial_proj(tok_ref, mod_ref, w_ref, gain_ref, out_ref, turned):
    cols = 4 * PATCH
    zeros = jnp.zeros((HP - HD, cols), F32)
    first = lax.broadcasted_iota(jnp.int32, (HP - HD, cols), 0) == 0
    ones = jnp.where(first, 1.0, 0.0)

    @pl.when(pl.program_id(0) == 0)
    def _():
        turned[...] = w_ref[...].astype(F32).T.astype(BF)

    clips = []
    for clip in range(2):
        tok = tok_ref[:, clip * PATCH : (clip + 1) * PATCH, :].reshape(cols, D).astype(F32)
        normed = normalise(tok) * (1.0 + mod_ref[1:2, :]) + mod_ref[0:1, :]
        clips.append(normed.astype(BF))
    normed = jnp.concatenate(clips, 0)
    both = lax.dot_general(turned[: 6 * HD], normed, NT, preferred_element_type=F32)
    for clip in range(2):
        proj = both[:, clip * cols : (clip + 1) * cols]
        for head in range(2):
            query, key, value = (
                proj[part * 2 * HD + head * HD : part * 2 * HD + (head + 1) * HD] for part in range(3)
            )
            query = rms(query, gain_ref[:, 0:1]) * (FACTOR * math.log2(math.e))
            key = rms(key, gain_ref[:, 1:2])
            place = clip * 2 + head
            parts = [key, zeros, value, ones, query, zeros]
            out_ref[place] = jnp.concatenate(parts, 0).astype(BF)


def attend_step(q_ref, kv_ref, keys, acc):
    query = jnp.concatenate([q_ref[0], jnp.zeros((128 - HP, PLANE), BF)], 0)
    total = None
    for part in range(PLANE // 256):
        here = slice(part * 256, (part + 1) * 256)
        score = jnp.dot(keys[here, :], query, preferred_element_type=F32)
        expo = jnp.exp2(score).astype(BF)
        add = jnp.dot(kv_ref[0, HP : 2 * HP, here], expo, preferred_element_type=F32)
        total = add if total is None else total + add
    return acc + total


def turn_keys(kv_ref, keys):
    wide = jnp.concatenate([kv_ref[0, :HP].astype(F32), jnp.zeros((128 - HP, PLANE), F32)], 0)
    keys[...] = wide.T.astype(BF)


def attend(steps, resume, finish, *refs):
    q_ref, kv_ref = refs[:2]
    out_ref, keys, sums = refs[-3:]
    step, block = pl.program_id(0), pl.program_id(1)

    @pl.when(block == 0)
    def _():
        turn_keys(kv_ref, keys)

    @pl.when(step == 0)
    def _():
        sums[block] = refs[2][0] if resume else jnp.zeros((HP, PLANE), F32)

    sums[block] = attend_step(q_ref, kv_ref, keys, sums[block])

    @pl.when(step == steps - 1)
    def _():
        done = sums[block]
        if not finish:
            out_ref[0] = done
            return
        done = done[:HD] / done[HD : HD + 1]
        for z in range(NZ):
            out_ref[0, z] = done[:, z * PATCH : (z + 1) * PATCH].astype(BF)


def attention(query, key_value, part, finish):
    steps = key_value.shape[0]
    last = lambda k, q: jnp.where(k == steps - 1, q, 0)
    first = lambda k, q: jnp.where(k == 0, q, NY - 1)
    q_spec = pl.BlockSpec((1, HP, PLANE), lambda k, q: (q, 2, 0))
    kv_spec = pl.BlockSpec((1, 2 * HP, PLANE), lambda k, q: (k, 0, 0))
    in_specs, args = [q_spec, kv_spec], [query, key_value]
    if part is not None:
        in_specs.append(pl.BlockSpec((1, HP, PLANE), lambda k, q: (first(k, q), 0, 0)))
        args.append(part)
    if finish:
        out_spec = pl.BlockSpec((1, NZ, HD, PATCH), lambda k, q: (last(k, q), 0, 0, 0))
        out_shape = jax.ShapeDtypeStruct((NY, NZ, HD, PATCH), BF)
    else:
        out_spec = pl.BlockSpec((1, HP, PLANE), lambda k, q: (last(k, q), 0, 0))
        out_shape = jax.ShapeDtypeStruct((NY, HP, PLANE), F32)
    pairs = steps * NY * PLANE * PLANE
    return pl.pallas_call(
        functools.partial(attend, steps, part is not None, finish),
        grid=(steps, NY),
        in_specs=in_specs,
        out_specs=out_spec,
        out_shape=out_shape,
        scratch_shapes=[pltpu.VMEM((PLANE, 128), BF), pltpu.VMEM((NY, HP, PLANE), F32)],
        compiler_params=PARAMS,
        cost_estimate=pl.CostEstimate(
            flops=4 * 256 * pairs, bytes_accessed=4_000_000, transcendentals=pairs
        ),
        name="attend",
    )(*args)


def choose(flag, yes, no, rows):
    chunks = [jnp.where(flag, yes[n, rows, :], no[n, rows, :]) for n in range(5)]
    return jnp.concatenate(chunks, 1)[:, :D]


def spatial_end(place_ref, att_ref, tok_ref, mod_ref, own, got, resid_ref, norm_ref):
    weight = choose(place_ref[0] == 1, got, own, slice(0, D))
    rows = []
    for clip in range(2):
        feats = [
            att_ref[clip * 2 + head, pair].astype(F32) for pair in range(NZ) for head in range(2)
        ]
        rows.append(jnp.concatenate(feats, 0).T.astype(BF))
    attended = jnp.concatenate(rows, 0)
    branch = jnp.dot(attended, weight, preferred_element_type=F32)
    resid = tok_ref[...].astype(F32) + mod_ref[2:3, :] * branch
    resid_ref[...] = resid
    norm_ref[...] = (normalise(resid) * (1.0 + mod_ref[4:5, :]) + mod_ref[3:4, :]).astype(BF)


def temporal(place_ref, n0, n1, n2, n3, weight, gain_ref, o0, o1, o2, o3):
    weight = jnp.concatenate([weight[0, :, 128:], weight[1], weight[2], weight[3]], 1)
    gap = jnp.zeros((256 - ROWS, D), BF)
    rows = jnp.concatenate([n0[...], gap, n1[...], gap, n2[...], gap, n3[...], gap], 0)
    proj = lax.dot_general(weight, rows, TT, preferred_element_type=F32)
    queries, keys, values = [], [], []
    for frame in range(4):
        here = slice(frame * 256, (frame + 1) * 256)
        heads = [proj[n * HD : (n + 1) * HD, here] for n in range(12)]
        queries.append([rms(v, gain_ref[:, 2:3]).astype(BF).astype(F32) for v in heads[:4]])
        keys.append([rms(v, gain_ref[:, 3:4]).astype(BF).astype(F32) for v in heads[4:8]])
        values.append([v.astype(BF).astype(F32) for v in heads[8:]])
    for f, out_ref in enumerate((o0, o1, o2, o3)):
        mixed = []
        for head in range(4):
            total, attended = 0.0, 0.0
            for g in range(4):
                score = jnp.sum(queries[f][head] * keys[g][head], 0, keepdims=True) * FACTOR
                expo = jnp.exp(score)
                total = total + expo
                attended = attended + expo.astype(BF).astype(F32) * values[g][head]
            mixed.append((attended / total)[:, :ROWS])
        out_ref[...] = jnp.concatenate(mixed, 0).astype(BF)


def temporal_end(place_ref, m0, m1, m2, m3, resid_ref, mod_ref, own, got, out_ref):
    core = place_ref[0] == 1
    branch = None
    for step, att_ref in enumerate((m0, m1, m2, m3)):
        here = pl.ds(pl.multiple_of((place_ref[1] ^ step) * (4 * HD), 4 * HD), 4 * HD)
        rows = choose(core, own, got, here)
        add = jnp.dot(att_ref[...].astype(F32).T.astype(BF), rows, preferred_element_type=F32)
        branch = add if branch is None else branch + add
    out_ref[...] = (resid_ref[...] + mod_ref[5:6, :] * branch).astype(BF)


def whole(shapes, kernel, name, *args):
    specs, arrays = [pl.BlockSpec(memory_space=pltpu.SMEM)], [args[0]]
    for arg in args[1:]:
        array, count, n = arg if isinstance(arg, tuple) else (arg, arg.shape[0], 0)
        place = (n,) + (0,) * (array.ndim - 1)
        specs.append(pl.BlockSpec((count,) + array.shape[1:], lambda i, place=place: place))
        arrays.append(array)
    return pl.pallas_call(
        kernel,
        grid=(1,),
        in_specs=specs,
        out_specs=[pl.BlockSpec(s.shape, lambda i: (0, 0)) for s in shapes],
        out_shape=shapes,
        compiler_params=PARAMS,
        name=name,
    )(*arrays)


def per_device(tokens, modulation, spatial_qkv, spatial_out, temporal_qkv, temporal_out, norm_gains):
    core = lax.axis_index("c")
    frame = lax.axis_index("xl") * 2 + core
    place = jnp.stack([core, frame]).astype(jnp.int32)
    gains = norm_gains.T
    tok = tokens.reshape(ROWS, D)

    part_a = spatial_qkv.reshape(18, 3, NZ, 2 * HD).transpose(2, 0, 1, 3).reshape(NZ, 18, 6 * HD)
    part_a = jnp.pad(part_a, ((0, 0), (0, 0), (0, 512 - 6 * HD)))
    part_b = lax.dynamic_slice_in_dim(temporal_qkv.reshape(18, 3, D), frame * 4 * HD, 4 * HD, 2)
    rest = [jnp.where(core == 0, spatial_out, temporal_out), part_b.reshape(18, 12 * HD)]
    rest = jnp.pad(jnp.concatenate(rest, 1), ((0, 0), (0, 256 * NZ - D - 12 * HD)))
    rest = rest.reshape(18, NZ, 256).transpose(1, 0, 2)
    shard = jnp.concatenate([part_a, rest], 2)
    shard = lax.all_to_all(shard, "z", 0, 0, tiled=True).reshape(1, NZ * 18, 768)
    shard = jnp.broadcast_to(shard, (8, NZ * 18, 768))
    shard = lax.all_to_all(shard, ("xh", "y"), 0, 0, tiled=True).reshape(D, 768)

    column = lax.all_gather(tok, "z", axis=0)

    rest, column = lax.optimization_barrier((shard[:, 512:], column))
    rest = lax.all_gather(rest, "z", axis=0)

    projected = pl.pallas_call(
        spatial_proj,
        grid=(2,),
        in_specs=[
            pl.BlockSpec((4, ROWS, D), lambda i: (i, 0, 0)),
            pl.BlockSpec((6, D), lambda i: (0, 0)),
            pl.BlockSpec((D, 512), lambda i: (0, 0)),
            pl.BlockSpec((HD, 4), lambda i: (0, 0)),
        ],
        out_specs=pl.BlockSpec((4, 3 * HP, 4 * PATCH), lambda i: (0, 0, i)),
        out_shape=jax.ShapeDtypeStruct((4, 3 * HP, PLANE), BF),
        scratch_shapes=[pltpu.VMEM((512, D), BF)],
        compiler_params=PARAMS,
        name="spatial_proj",
    )(column, modulation, shard, gains)

    swap = [(0, 1), (1, 0)]
    projected = lax.all_to_all(projected, "y", 0, 0, tiled=True)
    other_a = lax.ppermute(projected[:2, : 2 * HP], "xh", swap)
    other_b = lax.ppermute(projected[2:, : 2 * HP], "xh", swap)
    part = attention(projected, projected, None, False)
    part = attention(projected, other_a, part, False)
    attended = attention(projected, other_b, part, True)
    attended, rest = lax.optimization_barrier((attended, rest))
    rest_got = lax.ppermute(rest, "c", swap)
    attended = attended.reshape(NY * NZ, HD, PATCH)
    attended = lax.all_to_all(attended, ("y", "z"), 0, 0, tiled=True)
    attended = attended.reshape(4, NZ, HD, PATCH)

    resid, normed_b = whole(
        [jax.ShapeDtypeStruct((ROWS, D), F32), jax.ShapeDtypeStruct((ROWS, D), BF)],
        spatial_end,
        "spatial_end",
        place, attended, tok, modulation, (rest, 5, 0), (rest_got, 5, 0),
    )
    norm_c = lax.ppermute(normed_b, "c", swap)
    norm_x = lax.ppermute(normed_b, "xl", swap)
    norm_cx = lax.ppermute(norm_x, "c", swap)
    mixed = whole(
        [jax.ShapeDtypeStruct((4 * HD, ROWS), BF)] * 4,
        temporal,
        "temporal",
        place, normed_b, norm_c, norm_x, norm_cx, (rest, 4, 1), gains,
    )
    mixed = [
        mixed[0],
        lax.ppermute(mixed[1], "c", swap),
        lax.ppermute(mixed[2], "xl", swap),
        lax.ppermute(mixed[3], ("xl", "c"), [(0, 3), (3, 0), (1, 2), (2, 1)]),
    ]
    (result,) = whole(
        [jax.ShapeDtypeStruct((ROWS, D), BF)],
        temporal_end,
        "temporal_end",
        place, *mixed, resid, modulation, (rest, 5, 0), (rest_got, 5, 0),
    )
    return result.reshape(2, 1, PATCH, D)


def solution(mesh):
    fine = Mesh(mesh.devices.reshape(2, 2, 2, NY, NZ), ("xl", "c", "xh", "y", "z"))
    time, space = ("xl", "c"), ("xh", "y", "z")
    block = P(None, time, space, None)
    rows = P(space, None)
    return jax.shard_map(
        per_device,
        mesh=fine,
        in_specs=(block, P(), rows, rows, rows, rows, P()),
        out_specs=block,
        check_vma=False,
    )
```

```python
import functools
import math

import jax
import jax.numpy as jnp
from jax import lax
from jax.experimental import pallas as pl
from jax.experimental.pallas import tpu as pltpu
from jax.sharding import Mesh
from jax.sharding import PartitionSpec as P

D = 1152
HEADS = 16
HD = 72
HP = 80
PATCH = 96
ROWS = 2 * PATCH
NZ, NY = 8, 4
PLANE = NZ * PATCH
BF = jnp.bfloat16
F32 = jnp.float32
FACTOR = 1.0 / math.sqrt(HD)
TN = (((0,), (0,)), ((), ()))
NT = (((1,), (1,)), ((), ()))
PARAMS = pltpu.CompilerParams(vmem_limit_bytes=48 * 1024 * 1024)


def normalise(values):
    mean_val = jnp.mean(values, -1, keepdims=True)
    centred = values - mean_val
    variance = jnp.mean(centred * centred, -1, keepdims=True)
    return centred * lax.rsqrt(variance + 1e-06)


def rms(values, gain):
    mean_sq = jnp.mean(values * values, 0, keepdims=True)
    return values * lax.rsqrt(mean_sq + 1e-06) * gain


def spatial_proj(tok_ref, mod_ref, w_ref, gain_ref, out_ref, turned):
    cols = 4 * PATCH
    zeros = jnp.zeros((HP - HD, cols), F32)
    first = lax.broadcasted_iota(jnp.int32, (HP - HD, cols), 0) == 0
    ones = jnp.where(first, 1.0, 0.0)

    @pl.when(pl.program_id(0) == 0)
    def _():
        turned[...] = w_ref[...].astype(F32).T.astype(BF)

    clips = []
    for clip in range(2):
        tok = tok_ref[:, clip * PATCH : (clip + 1) * PATCH, :].reshape(cols, D).astype(F32)
        normed = normalise(tok) * (1.0 + mod_ref[1:2, :]) + mod_ref[0:1, :]
        clips.append(normed.astype(BF))
    normed = jnp.concatenate(clips, 0)
    both = lax.dot_general(turned[: 6 * HD], normed, NT, preferred_element_type=F32)
    for clip in range(2):
        proj = both[:, clip * cols : (clip + 1) * cols]
        for head in range(2):
            query, key, value = (
                proj[part * 2 * HD + head * HD : part * 2 * HD + (head + 1) * HD] for part in range(3)
            )
            query = rms(query, gain_ref[:, 0:1]) * (FACTOR * math.log2(math.e))
            key = rms(key, gain_ref[:, 1:2])
            place = clip * 2 + head
            parts = [key, zeros, value, ones, query, zeros]
            out_ref[place] = jnp.concatenate(parts, 0).astype(BF)


def attend(steps, resume, finish, *refs):
    q_ref, kv_ref = refs[:2]
    out_ref, keys = refs[-2:]

    @pl.when(pl.program_id(0) == 0)
    def _():
        gap = jnp.zeros((128 - HP, PLANE), F32)
        for n in range(steps):
            keys[n] = jnp.concatenate([kv_ref[n, :HP].astype(F32), gap], 0).T.astype(BF)

    query = jnp.concatenate([q_ref[0], jnp.zeros((128 - HP, PLANE), BF)], 0)
    parts = [(n, slice(p, p + 256)) for n in range(steps) for p in range(0, PLANE, 256)]

    def scores(n, here):
        return jnp.dot(keys[n, here, :], query, preferred_element_type=F32)

    done = refs[2][0] if resume else None
    ahead = scores(*parts[0])
    for place, (n, here) in enumerate(parts):
        score = ahead
        if place + 1 < len(parts):
            ahead = scores(*parts[place + 1])
        expo = jnp.exp2(score).astype(BF)
        add = jnp.dot(kv_ref[n, HP : 2 * HP, here], expo, preferred_element_type=F32)
        done = add if done is None else done + add
    if not finish:
        out_ref[0] = done
        return
    done = done[:HD] / done[HD : HD + 1]
    for z in range(NZ):
        out_ref[0, z] = done[:, z * PATCH : (z + 1) * PATCH].astype(BF)


def attention(query, key_value, part, finish):
    steps = key_value.shape[0]
    sums = pl.BlockSpec((1, HP, PLANE), lambda q: (q, 0, 0))
    in_specs = [
        pl.BlockSpec((1, HP, PLANE), lambda q: (q, 2, 0)),
        pl.BlockSpec((steps, 2 * HP, PLANE), lambda q: (0, 0, 0)),
    ]
    args = [query, key_value]
    if part is not None:
        in_specs.append(sums)
        args.append(part)
    if finish:
        out_spec = pl.BlockSpec((1, NZ, HD, PATCH), lambda q: (q, 0, 0, 0))
        out_shape = jax.ShapeDtypeStruct((NY, NZ, HD, PATCH), BF)
    else:
        out_spec = sums
        out_shape = jax.ShapeDtypeStruct((NY, HP, PLANE), F32)
    pairs = steps * NY * PLANE * PLANE
    return pl.pallas_call(
        functools.partial(attend, steps, part is not None, finish),
        grid=(NY,),
        in_specs=in_specs,
        out_specs=out_spec,
        out_shape=out_shape,
        scratch_shapes=[pltpu.VMEM((steps, PLANE, 128), BF)],
        compiler_params=PARAMS,
        cost_estimate=pl.CostEstimate(
            flops=4 * 256 * pairs, bytes_accessed=4_000_000, transcendentals=pairs
        ),
        name="attend",
    )(*args)


def prepare(place_ref, own, got, out_a, out_b, turned):
    second = place_ref[0] == 1
    for n in range(5):
        width = min(256, D - n * 256)
        here = slice(n * 256, n * 256 + width)
        out_a[:, here] = jnp.where(second, got[n, :, :width], own[n, :, :width])
        out_b[:, here] = jnp.where(second, own[n, :, :width], got[n, :, :width])
    turned[:128] = own[4, :, 128:].astype(F32).T.astype(BF)
    for n in range(3):
        turned[128 + n * 256 : 384 + n * 256] = own[5 + n].astype(F32).T.astype(BF)


def spatial_end(att_ref, tok_ref, mod_ref, weight, resid_ref, norm_ref):
    feats = [att_ref[head, pair].astype(F32) for pair in range(NZ) for head in range(2)]
    attended = jnp.concatenate(feats, 0).T.astype(BF)
    branch = jnp.dot(attended, weight[...], preferred_element_type=F32)
    resid = tok_ref[...].astype(F32) + mod_ref[2:3, :] * branch
    resid_ref[...] = resid
    norm_ref[...] = (normalise(resid) * (1.0 + mod_ref[4:5, :]) + mod_ref[3:4, :]).astype(BF)


def temporal(n0, n1, n2, n3, weight, gain_ref, *out_refs):
    gap = jnp.zeros((128 - PATCH, D), BF)
    rows = jnp.concatenate([n0[...], gap, n1[...], gap, n2[...], gap, n3[...], gap], 0)
    proj = lax.dot_general(weight[...], rows, NT, preferred_element_type=F32)
    queries, keys, values = [], [], []
    for frame in range(4):
        here = slice(frame * 128, (frame + 1) * 128)
        heads = [proj[n * HD : (n + 1) * HD, here] for n in range(12)]
        queries.append([rms(v, gain_ref[:, 2:3]).astype(BF).astype(F32) for v in heads[:4]])
        keys.append([rms(v, gain_ref[:, 3:4]).astype(BF).astype(F32) for v in heads[4:8]])
        values.append([v.astype(BF).astype(F32) for v in heads[8:]])
    for f, out_ref in enumerate(out_refs):
        mixed = []
        for head in range(4):
            total, attended = 0.0, 0.0
            for g in range(4):
                score = jnp.sum(queries[f][head] * keys[g][head], 0, keepdims=True) * FACTOR
                expo = jnp.exp(score)
                total = total + expo
                attended = attended + expo.astype(BF).astype(F32) * values[g][head]
            mixed.append(attended / total)
        tail = [mixed[3][:, n * 32 : (n + 1) * 32] for n in range(3)]
        body = jnp.concatenate([m[:, :PATCH] for m in mixed[:3]], 0)
        out_ref[...] = jnp.concatenate([body, jnp.concatenate(tail, 0)], 1).astype(BF)


def temporal_end(place_ref, m0, m1, m2, m3, resid_ref, mod_ref, weight, *out_refs):
    branch = None
    for step, att_ref in enumerate((m0, m1, m2, m3)):
        packed = att_ref[...].astype(F32)
        tail = [packed[n * HD : (n + 1) * HD, PATCH:] for n in range(3)]
        feats = jnp.concatenate([packed[:, :PATCH], jnp.concatenate(tail, 1)], 0)
        here = pl.ds(pl.multiple_of((place_ref[1] ^ step) * (4 * HD), 4 * HD), 4 * HD)
        add = jnp.dot(feats.T.astype(BF), weight[here, :], preferred_element_type=F32)
        branch = add if branch is None else branch + add
    out_refs[-1][...] = (resid_ref[...] + mod_ref[5:6, :] * branch).astype(BF)


SMEM = pl.BlockSpec(memory_space=pltpu.SMEM)


def full(array, lead=None, n=0):
    block = array.shape if lead is None else (lead,) + array.shape[1:]
    place = (n,) + (0,) * (array.ndim - 1)
    return pl.BlockSpec(block, lambda i: place)


def once(kernel, args, specs, shapes, out_specs=None, aliases=None):
    return pl.pallas_call(
        kernel,
        grid=(1,),
        in_specs=specs,
        out_specs=out_specs or [full(s) for s in shapes],
        out_shape=shapes,
        input_output_aliases=aliases or {},
        compiler_params=PARAMS,
        cost_estimate=pl.CostEstimate(
            flops=2_000_000_000, bytes_accessed=8_000_000, transcendentals=0
        ),
        name=kernel.__name__,
    )(*args)


def shape(dtype, *sizes):
    return jax.ShapeDtypeStruct(sizes, dtype)


def per_device(tokens, modulation, spatial_qkv, spatial_out, temporal_qkv, temporal_out, norm_gains):
    core = lax.axis_index("c")
    frame = lax.axis_index("xl") * 2 + core
    place = jnp.stack([core, frame]).astype(jnp.int32)
    gains = norm_gains.T
    tok = tokens.reshape(ROWS, D)

    part_a = spatial_qkv.reshape(18, 3, NZ, 2 * HD).transpose(2, 0, 1, 3).reshape(NZ, 18, 6 * HD)
    part_a = jnp.pad(part_a, ((0, 0), (0, 0), (0, 512 - 6 * HD)))
    part_b = lax.dynamic_slice_in_dim(temporal_qkv.reshape(18, 3, D), frame * 4 * HD, 4 * HD, 2)
    rest = [jnp.where(core == 0, spatial_out, temporal_out), part_b.reshape(18, 12 * HD)]
    rest = jnp.pad(jnp.concatenate(rest, 1), ((0, 0), (0, 256 * NZ - D - 12 * HD)))
    rest = rest.reshape(18, NZ, 256).transpose(1, 0, 2)
    shard = jnp.concatenate([part_a, rest], 2)
    shard = lax.all_to_all(shard, "z", 0, 0, tiled=True).reshape(1, NZ * 18, 768)
    shard = jnp.broadcast_to(shard, (8, NZ * 18, 768))
    shard = lax.all_to_all(shard, ("xh", "y"), 0, 0, tiled=True).reshape(D, 768)

    column = lax.all_gather(tok, "z", axis=0)

    rest, column = lax.optimization_barrier((shard[:, 512:], column))
    rest = lax.all_gather(rest, "z", axis=0)

    projected = pl.pallas_call(
        spatial_proj,
        grid=(2,),
        in_specs=[
            pl.BlockSpec((4, ROWS, D), lambda i: (i, 0, 0)),
            pl.BlockSpec((6, D), lambda i: (0, 0)),
            pl.BlockSpec((D, 512), lambda i: (0, 0)),
            pl.BlockSpec((HD, 4), lambda i: (0, 0)),
        ],
        out_specs=pl.BlockSpec((4, 3 * HP, 4 * PATCH), lambda i: (0, 0, i)),
        out_shape=jax.ShapeDtypeStruct((4, 3 * HP, PLANE), BF),
        scratch_shapes=[pltpu.VMEM((512, D), BF)],
        compiler_params=PARAMS,
        name="spatial_proj",
    )(column, modulation, shard, gains)

    swap = [(0, 1), (1, 0)]
    projected = lax.all_to_all(projected, "y", 0, 0, tiled=True)
    other_a = lax.ppermute(projected[:2, : 2 * HP], "xh", swap)
    other_b = lax.ppermute(projected[2:, : 2 * HP], "xh", swap)
    part = attention(projected, projected, None, False)
    part = attention(projected, other_a, part, False)
    attended = attention(projected, other_b, part, True)
    attended, rest = lax.optimization_barrier((attended, rest))
    rest_got = lax.ppermute(rest, "c", swap)
    attended = attended.reshape(NY * NZ, HD, PATCH)
    attended = lax.all_to_all(attended, ("y", "z"), 0, 0, tiled=True)
    attended = attended.reshape(4, NZ, HD, PATCH)
    out_a, out_b, turned = once(
        prepare,
        [place, rest, rest_got],
        [SMEM, full(rest), full(rest, 5)],
        [shape(BF, D, D), shape(BF, D, D), shape(BF, 896, D)],
    )

    steps = []
    for clip in range(2):
        args = [attended, tok, modulation, out_a]
        specs = [full(attended, 2, clip), full(tok, PATCH, clip), full(modulation), full(out_a)]
        steps.append(once(spatial_end, args, specs, [shape(F32, PATCH, D), shape(BF, PATCH, D)]))
    diagonal = [(0, 3), (3, 0), (1, 2), (2, 1)]
    sent = []
    moved = [lax.ppermute(norm, "xl", swap) for _, norm in steps]
    moved[0], _ = lax.optimization_barrier((moved[0], steps[1][1]))
    for (_, norm), norm_x in zip(steps, moved):
        if sent:
            norm_x, sent[0][0] = lax.optimization_barrier((norm_x, sent[0][0]))
        args = [norm, lax.ppermute(norm, "c", swap), norm_x, lax.ppermute(norm_x, "c", swap)]
        args += [turned, gains]
        mixed = once(temporal, args, [full(a) for a in args], [shape(BF, 3 * HD, 128)] * 4)
        sent.append(
            [
                mixed[0],
                lax.ppermute(mixed[1], "c", swap),
                lax.ppermute(mixed[2], "xl", swap),
                lax.ppermute(mixed[3], ("xl", "c"), diagonal),
            ]
        )
    result = None
    for clip in range(2):
        args = sent[clip] + [steps[clip][0], modulation, out_b]
        specs = [SMEM] + [full(a) for a in args]
        aliases = None
        if result is not None:
            args, specs = args + [result], specs + [pl.BlockSpec(memory_space=pl.ANY)]
            aliases = {len(args): 0}
        whole = shape(BF, ROWS, D)
        out_specs = [full(whole, PATCH, clip)]
        (result,) = once(temporal_end, [place] + args, specs, [whole], out_specs, aliases)
    return result.reshape(2, 1, PATCH, D)


def solution(mesh):
    fine = Mesh(mesh.devices.reshape(2, 2, 2, NY, NZ), ("xl", "c", "xh", "y", "z"))
    time, space = ("xl", "c"), ("xh", "y", "z")
    block = P(None, time, space, None)
    rows = P(space, None)
    return jax.shard_map(
        per_device,
        mesh=fine,
        in_specs=(block, P(), rows, rows, rows, rows, P()),
        out_specs=block,
        check_vma=False,
    )
```

```python
import functools
import math

import jax
import jax.numpy as jnp
from jax import lax
from jax.experimental import pallas as pl
from jax.experimental.pallas import tpu as pltpu
from jax.sharding import Mesh
from jax.sharding import PartitionSpec as P

D = 1152
HEADS = 16
HD = 72
HP = 80
PATCH = 96
ROWS = 2 * PATCH
NZ, NY = 8, 4
PLANE = NZ * PATCH
BF = jnp.bfloat16
F32 = jnp.float32
PIECES = (slice(0, 2), slice(2, 3), slice(3, 4))
FACTOR = 1.0 / math.sqrt(HD)
TN = (((0,), (0,)), ((), ()))
NT = (((1,), (1,)), ((), ()))
PARAMS = pltpu.CompilerParams(vmem_limit_bytes=48 * 1024 * 1024)


def normalise(values):
    mean_val = jnp.mean(values, -1, keepdims=True)
    centred = values - mean_val
    variance = jnp.mean(centred * centred, -1, keepdims=True)
    return centred * lax.rsqrt(variance + 1e-06)


def rms(values, gain):
    mean_sq = jnp.mean(values * values, 0, keepdims=True)
    return values * lax.rsqrt(mean_sq + 1e-06) * gain


def spatial_proj(tok_ref, mod_ref, w_ref, gain_ref, out_ref, turned):
    cols = 4 * PATCH
    zeros = jnp.zeros((HP - HD, cols), F32)

    @pl.when(pl.program_id(0) == 0)
    def _():
        turned[...] = w_ref[...].astype(F32).T.astype(BF)

    clips = []
    for clip in range(2):
        tok = tok_ref[:, clip * PATCH : (clip + 1) * PATCH, :].reshape(cols, D).astype(F32)
        normed = normalise(tok) * (1.0 + mod_ref[1:2, :]) + mod_ref[0:1, :]
        clips.append(normed.astype(BF))
    normed = jnp.concatenate(clips, 0)
    both = lax.dot_general(turned[: 6 * HD], normed, NT, preferred_element_type=F32)
    for clip in range(2):
        proj = both[:, clip * cols : (clip + 1) * cols]
        for head in range(2):
            query, key, value = (
                proj[part * 2 * HD + head * HD : part * 2 * HD + (head + 1) * HD] for part in range(3)
            )
            query = rms(query, gain_ref[:, 0:1]) * (FACTOR * math.log2(math.e))
            key = rms(key, gain_ref[:, 1:2])
            place = clip * 2 + head
            parts = [key, value, query, zeros]
            out_ref[place] = jnp.concatenate(parts, 0).astype(BF)


def pack(block, rows):
    strips = [block[rows:, n * 32 : (n + 1) * 32] for n in range(3)]
    spare = rows - 3 * strips[0].shape[0]
    if spare:
        strips.append(jnp.zeros((spare, 32), block.dtype))
    return jnp.concatenate([block[:rows], jnp.concatenate(strips, 0)], 1)


def unpack(packed, tall):
    strips = [packed[n * tall : (n + 1) * tall, PATCH:] for n in range(3)]
    return jnp.concatenate([packed[:, :PATCH], jnp.concatenate(strips, 1)], 0)


def attend(steps, resume, finish, *refs):
    q_ref, kv_ref = refs[:2]
    out_ref, keys, values = refs[-3:]

    @pl.when(pl.program_id(0) == 0)
    def _():
        gap = jnp.zeros((128 - HD, PLANE), F32)
        first = lax.broadcasted_iota(jnp.int32, (HP - HD, PLANE), 0) == 0
        ones = jnp.where(first, 1.0, 0.0)
        for n in range(steps):
            both = kv_ref[n, : 2 * HD].astype(F32)
            keys[n] = jnp.concatenate([both[:HD], gap], 0).T.astype(BF)
            values[n] = jnp.concatenate([both[HD:], ones], 0).astype(BF)

    query = jnp.concatenate([q_ref[0, 2 * HD :], jnp.zeros((128 - HP, PLANE), BF)], 0)
    parts = [(n, slice(p, p + 256)) for n in range(steps) for p in range(0, PLANE, 256)]

    def scores(n, here):
        return jnp.dot(keys[n, here, :], query, preferred_element_type=F32)

    done = refs[2][0] if resume else None
    ahead = scores(*parts[0])
    for place, (n, here) in enumerate(parts):
        score = ahead
        if place + 1 < len(parts):
            ahead = scores(*parts[place + 1])
        expo = jnp.exp2(score).astype(BF)
        add = jnp.dot(values[n, :, here], expo, preferred_element_type=F32)
        done = add if done is None else done + add
    if not finish:
        out_ref[0] = done
        return
    done = done[:HD] / done[HD : HD + 1]
    for z in range(NZ):
        out_ref[0, z] = pack(done[:, z * PATCH : (z + 1) * PATCH], 56).astype(BF)


def attention(query, key_value, part, finish):
    steps = key_value.shape[0]
    sums = pl.BlockSpec((1, HP, PLANE), lambda q: (q, 0, 0))
    in_specs = [
        pl.BlockSpec((1, 3 * HD + 8, PLANE), lambda q: (q, 0, 0)),
        pl.BlockSpec((steps,) + key_value.shape[1:], lambda q: (0, 0, 0)),
    ]
    args = [query, key_value]
    if part is not None:
        in_specs.append(sums)
        args.append(part)
    if finish:
        out_spec = pl.BlockSpec((1, NZ, 56, 128), lambda q: (q, 0, 0, 0))
        out_shape = shape(BF, NY, NZ, 56, 128)
    else:
        out_spec = sums
        out_shape = shape(F32, NY, HP, PLANE)
    pairs = steps * NY * PLANE * PLANE
    return pl.pallas_call(
        functools.partial(attend, steps, part is not None, finish),
        grid=(NY,),
        in_specs=in_specs,
        out_specs=out_spec,
        out_shape=out_shape,
        scratch_shapes=[pltpu.VMEM((steps, PLANE, 128), BF), pltpu.VMEM((steps, HP, PLANE), BF)],
        compiler_params=PARAMS,
        cost_estimate=pl.CostEstimate(
            flops=4 * pairs, bytes_accessed=1_000_000, transcendentals=0
        ),
        name="attend",
    )(*args)


def prepare(place_ref, own, got, out_a, out_b, turned):
    second = place_ref[0] == 1
    for n in range(5):
        width = min(256, D - n * 256)
        here = slice(n * 256, n * 256 + width)
        out_a[:, here] = jnp.where(second, got[n, :, :width], own[n, :, :width])
        out_b[:, here] = jnp.where(second, own[n, :, :width], got[n, :, :width])
    turned[:128] = own[4, :, 128:].astype(F32).T.astype(BF)
    for n in range(3):
        turned[128 + n * 256 : 384 + n * 256] = own[5 + n].astype(F32).T.astype(BF)


def spatial_end(att_ref, tok_ref, mod_ref, weight, resid_ref, norm_ref):
    feats = [unpack(att_ref[n % 2, n // 2].astype(F32), 16) for n in range(HEADS)]
    attended = jnp.concatenate(feats, 0).T.astype(BF)
    branch = jnp.dot(attended, weight[...], preferred_element_type=F32)
    resid = tok_ref[...].astype(F32) + mod_ref[2:3, :] * branch
    resid_ref[...] = resid
    norm_ref[...] = (normalise(resid) * (1.0 + mod_ref[4:5, :]) + mod_ref[3:4, :]).astype(BF)


def temporal(n0, n1, n2, n3, weight, gain_ref, *out_refs):
    gap = jnp.zeros((128 - PATCH, D), BF)
    rows = jnp.concatenate([n0[...], gap, n1[...], gap, n2[...], gap, n3[...], gap], 0)
    proj = lax.dot_general(weight[...], rows, NT, preferred_element_type=F32)
    queries, keys, values = [], [], []
    for frame in range(4):
        here = slice(frame * 128, (frame + 1) * 128)
        heads = [proj[n * HD : (n + 1) * HD, here] for n in range(12)]
        queries.append([rms(v, gain_ref[:, 2:3]).astype(BF).astype(F32) for v in heads[:4]])
        keys.append([rms(v, gain_ref[:, 3:4]).astype(BF).astype(F32) for v in heads[4:8]])
        values.append([v.astype(BF).astype(F32) for v in heads[8:]])
    for f, out_ref in enumerate(out_refs):
        mixed = []
        for head in range(4):
            total, attended = 0.0, 0.0
            for g in range(4):
                score = jnp.sum(queries[f][head] * keys[g][head], 0, keepdims=True) * FACTOR
                expo = jnp.exp(score)
                total = total + expo
                attended = attended + expo.astype(BF).astype(F32) * values[g][head]
            mixed.append(attended / total)
        out_ref[...] = pack(jnp.concatenate(mixed, 0)[:, :PATCH], 3 * HD).astype(BF)


def temporal_end(place_ref, m0, m1, m2, m3, resid_ref, mod_ref, weight, *out_refs):
    branch = None
    for step, att_ref in enumerate((m0, m1, m2, m3)):
        feats = unpack(att_ref[...].astype(F32), HD)
        here = pl.ds(pl.multiple_of((place_ref[1] ^ step) * (4 * HD), 4 * HD), 4 * HD)
        add = jnp.dot(feats.T.astype(BF), weight[here, :], preferred_element_type=F32)
        branch = add if branch is None else branch + add
    out_refs[-1][...] = (resid_ref[...] + mod_ref[5:6, :] * branch).astype(BF)


SMEM = pl.BlockSpec(memory_space=pltpu.SMEM)


def full(array, lead=None, n=0):
    block = array.shape if lead is None else (lead,) + array.shape[1:]
    place = (n,) + (0,) * (array.ndim - 1)
    return pl.BlockSpec(block, lambda i: place)


def once(kernel, args, specs, shapes, out_specs=None, aliases=None):
    return pl.pallas_call(
        kernel,
        grid=(1,),
        in_specs=specs,
        out_specs=out_specs or [full(s) for s in shapes],
        out_shape=shapes,
        input_output_aliases=aliases or {},
        compiler_params=PARAMS,
        cost_estimate=pl.CostEstimate(
            flops=2_000_000_000, bytes_accessed=8_000_000, transcendentals=0
        ),
        name=kernel.__name__,
    )(*args)


def shape(dtype, *sizes):
    return jax.ShapeDtypeStruct(sizes, dtype)


def per_device(tokens, modulation, spatial_qkv, spatial_out, temporal_qkv, temporal_out, norm_gains):
    core = lax.axis_index("c")
    frame = lax.axis_index("xl") * 2 + core
    place = jnp.stack([core, frame]).astype(jnp.int32)
    gains = norm_gains.T
    tok = tokens.reshape(ROWS, D)

    part_a = spatial_qkv.reshape(18, 3, NZ, 2 * HD).transpose(2, 0, 1, 3).reshape(NZ, 18, 6 * HD)
    part_a = jnp.pad(part_a, ((0, 0), (0, 0), (0, 512 - 6 * HD)))
    part_b = lax.dynamic_slice_in_dim(temporal_qkv.reshape(18, 3, D), frame * 4 * HD, 4 * HD, 2)
    rest = [jnp.where(core == 0, spatial_out, temporal_out), part_b.reshape(18, 12 * HD)]
    rest = jnp.pad(jnp.concatenate(rest, 1), ((0, 0), (0, 256 * NZ - D - 12 * HD)))
    rest = rest.reshape(18, NZ, 256).transpose(1, 0, 2)
    shard = jnp.concatenate([part_a, rest], 2)
    shard = lax.all_to_all(shard, "z", 0, 0, tiled=True).reshape(1, NZ * 18, 768)
    shard = jnp.broadcast_to(shard, (8, NZ * 18, 768))
    shard = lax.all_to_all(shard, ("xh", "y"), 0, 0, tiled=True).reshape(D, 768)

    column = lax.all_gather(tok, "z", axis=0)

    rest, column = lax.optimization_barrier((shard[:, 512:], column))
    rest = lax.all_gather(rest, "z", axis=0)

    projected = pl.pallas_call(
        spatial_proj,
        grid=(2,),
        in_specs=[
            pl.BlockSpec((4, ROWS, D), lambda i: (i, 0, 0)),
            pl.BlockSpec((6, D), lambda i: (0, 0)),
            pl.BlockSpec((D, 512), lambda i: (0, 0)),
            pl.BlockSpec((HD, 4), lambda i: (0, 0)),
        ],
        out_specs=pl.BlockSpec((4, 3 * HD + 8, 4 * PATCH), lambda i: (0, 0, i)),
        out_shape=shape(BF, 4, 3 * HD + 8, PLANE),
        scratch_shapes=[pltpu.VMEM((512, D), BF)],
        compiler_params=PARAMS,
        name="spatial_proj",
    )(column, modulation, shard, gains)

    swap = [(0, 1), (1, 0)]
    projected = lax.all_to_all(projected, "y", 0, 0, tiled=True)
    others = [lax.ppermute(projected[n, : 2 * HD], "xh", swap) for n in PIECES]
    part = attention(projected, projected, None, False)
    part = attention(projected, others[0], part, False)
    part = attention(projected, others[1], part, False)
    attended = attention(projected, others[2], part, True)
    attended, rest = lax.optimization_barrier((attended, rest))
    rest_got = lax.ppermute(rest, "c", swap)
    attended = attended.reshape(NY * NZ, 56, 128)
    attended = lax.all_to_all(attended, ("y", "z"), 0, 0, tiled=True)
    attended = attended.reshape(4, NZ, 56, 128)
    out_a, out_b, turned = once(
        prepare,
        [place, rest, rest_got],
        [SMEM, full(rest), full(rest, 5)],
        [shape(BF, D, D), shape(BF, D, D), shape(BF, 896, D)],
    )

    steps = []
    for clip in range(2):
        args = [attended, tok, modulation, out_a]
        specs = [full(attended, 2, clip), full(tok, PATCH, clip), full(modulation), full(out_a)]
        steps.append(once(spatial_end, args, specs, [shape(F32, PATCH, D), shape(BF, PATCH, D)]))
    diagonal = [(0, 3), (3, 0), (1, 2), (2, 1)]
    sent = []
    moved = [lax.ppermute(norm, "xl", swap) for _, norm in steps]
    moved[0], _ = lax.optimization_barrier((moved[0], steps[1][1]))
    for (_, norm), norm_x in zip(steps, moved):
        if sent:
            norm_x, sent[0][0] = lax.optimization_barrier((norm_x, sent[0][0]))
        args = [norm, lax.ppermute(norm, "c", swap), norm_x, lax.ppermute(norm_x, "c", swap)]
        args += [turned, gains]
        mixed = once(temporal, args, [full(a) for a in args], [shape(BF, 3 * HD, 128)] * 4)
        sent.append(
            [
                mixed[0],
                lax.ppermute(mixed[1], "c", swap),
                lax.ppermute(mixed[2], "xl", swap),
                lax.ppermute(mixed[3], ("xl", "c"), diagonal),
            ]
        )
    result = None
    for clip in range(2):
        args = sent[clip] + [steps[clip][0], modulation, out_b]
        specs = [SMEM] + [full(a) for a in args]
        aliases = None
        if result is not None:
            args, specs = args + [result], specs + [pl.BlockSpec(memory_space=pl.ANY)]
            aliases = {len(args): 0}
        whole = shape(BF, ROWS, D)
        out_specs = [full(whole, PATCH, clip)]
        (result,) = once(temporal_end, [place] + args, specs, [whole], out_specs, aliases)
    return result.reshape(2, 1, PATCH, D)


def solution(mesh):
    fine = Mesh(mesh.devices.reshape(2, 2, 2, NY, NZ), ("xl", "c", "xh", "y", "z"))
    time, space = ("xl", "c"), ("xh", "y", "z")
    block = P(None, time, space, None)
    rows = P(space, None)
    return jax.shard_map(
        per_device,
        mesh=fine,
        in_specs=(block, P(), rows, rows, rows, rows, P()),
        out_specs=block,
        check_vma=False,
    )
```

```python
import functools
import math

import jax
import jax.numpy as jnp
from jax import lax
from jax.experimental import pallas as pl
from jax.experimental.pallas import tpu as pltpu
from jax.sharding import Mesh
from jax.sharding import PartitionSpec as P

D = 1152
HEADS = 16
HD = 72
HP = 80
PATCH = 96
ROWS = 2 * PATCH
NZ, NY = 8, 4
PLANE = NZ * PATCH
BF = jnp.bfloat16
F32 = jnp.float32
PIECES = (slice(0, 2), slice(2, 3), slice(3, 4))
FACTOR = 1.0 / math.sqrt(HD)
TN = (((0,), (0,)), ((), ()))
NT = (((1,), (1,)), ((), ()))
PARAMS = pltpu.CompilerParams(vmem_limit_bytes=48 * 1024 * 1024)


def normalise(values):
    mean_val = jnp.mean(values, -1, keepdims=True)
    centred = values - mean_val
    variance = jnp.mean(centred * centred, -1, keepdims=True)
    return centred * lax.rsqrt(variance + 1e-06)


def rms(values, gain):
    mean_sq = jnp.mean(values * values, 0, keepdims=True)
    return values * lax.rsqrt(mean_sq + 1e-06) * gain


def spatial_proj(tok_ref, mod_ref, w_ref, gain_ref, out_ref, outs_ref, part_ref, turned):
    cols = 4 * PATCH
    zeros = jnp.zeros((HP - HD, cols), F32)

    @pl.when((pl.program_id(0) == 0) & (pl.program_id(1) == 0))
    def _():
        turned[...] = w_ref[:, :512].astype(F32).T.astype(BF)
        rest = w_ref[:, 512:].astype(F32).T
        outs_ref[...] = rest[: 2 * HD].astype(BF)
        part_ref[...] = rest[2 * HD :].astype(BF)

    tok = tok_ref[...].reshape(cols, D).astype(F32)
    normed = normalise(tok) * (1.0 + mod_ref[1:2, :]) + mod_ref[0:1, :]
    proj = lax.dot_general(turned[: 6 * HD], normed.astype(BF), NT, preferred_element_type=F32)
    for head in range(2):
        query, key, value = (
            proj[part * 2 * HD + head * HD : part * 2 * HD + (head + 1) * HD] for part in range(3)
        )
        query = rms(query, gain_ref[:, 0:1]) * (FACTOR * math.log2(math.e))
        key = rms(key, gain_ref[:, 1:2])
        out_ref[head] = jnp.concatenate([key, value, query, zeros], 0).astype(BF)


def pack(block, rows):
    strips = [block[rows:, n * 32 : (n + 1) * 32] for n in range(3)]
    spare = rows - 3 * strips[0].shape[0]
    if spare:
        strips.append(jnp.zeros((spare, 32), block.dtype))
    return jnp.concatenate([block[:rows], jnp.concatenate(strips, 0)], 1)


def unpack(packed, tall):
    strips = [packed[n * tall : (n + 1) * tall, PATCH:] for n in range(3)]
    return jnp.concatenate([packed[:, :PATCH], jnp.concatenate(strips, 1)], 0)


def attend(steps, resume, finish, *refs):
    q_ref, kv_ref = refs[:2]
    out_ref, keys, values = refs[-3:]

    @pl.when(pl.program_id(0) == 0)
    def _():
        gap = jnp.zeros((128 - HD, PLANE), F32)
        first = lax.broadcasted_iota(jnp.int32, (HP - HD, PLANE), 0) == 0
        ones = jnp.where(first, 1.0, 0.0)
        for n in range(steps):
            both = kv_ref[n, : 2 * HD].astype(F32)
            keys[n] = jnp.concatenate([both[:HD], gap], 0).T.astype(BF)
            values[n] = jnp.concatenate([both[HD:], ones], 0).astype(BF)

    query = jnp.concatenate([q_ref[0, 2 * HD :], jnp.zeros((128 - HP, PLANE), BF)], 0)
    parts = [(n, slice(p, p + 256)) for n in range(steps) for p in range(0, PLANE, 256)]

    def scores(n, here):
        return jnp.dot(keys[n, here, :], query, preferred_element_type=F32)

    done = refs[2][0] if resume else None
    ahead = scores(*parts[0])
    for place, (n, here) in enumerate(parts):
        score = ahead
        if place + 1 < len(parts):
            ahead = scores(*parts[place + 1])
        expo = jnp.exp2(score).astype(BF)
        add = jnp.dot(values[n, :, here], expo, preferred_element_type=F32)
        done = add if done is None else done + add
    if not finish:
        out_ref[0] = done
        return
    done = done[:HD] / done[HD : HD + 1]
    for z in range(NZ):
        out_ref[0, z] = pack(done[:, z * PATCH : (z + 1) * PATCH], 56).astype(BF)


def attention(query, key_value, part, finish):
    steps = key_value.shape[0]
    sums = pl.BlockSpec((1, HP, PLANE), lambda q: (q, 0, 0))
    in_specs = [
        pl.BlockSpec((1, 3 * HD + 8, PLANE), lambda q: (q, 0, 0)),
        pl.BlockSpec((steps,) + key_value.shape[1:], lambda q: (0, 0, 0)),
    ]
    args = [query, key_value]
    if part is not None:
        in_specs.append(sums)
        args.append(part)
    if finish:
        out_spec = pl.BlockSpec((1, NZ, 56, 128), lambda q: (q, 0, 0, 0))
        out_shape = shape(BF, NY, NZ, 56, 128)
    else:
        out_spec = sums
        out_shape = shape(F32, NY, HP, PLANE)
    pairs = steps * NY * PLANE * PLANE
    return pl.pallas_call(
        functools.partial(attend, steps, part is not None, finish),
        grid=(NY,),
        in_specs=in_specs,
        out_specs=out_spec,
        out_shape=out_shape,
        scratch_shapes=[pltpu.VMEM((steps, PLANE, 128), BF), pltpu.VMEM((steps, HP, PLANE), BF)],
        compiler_params=PARAMS,
        cost_estimate=pl.CostEstimate(
            flops=4 * pairs, bytes_accessed=1_000_000, transcendentals=0
        ),
        name="attend",
    )(*args)


def spatial_end(att_ref, tok_ref, mod_ref, weight, resid_ref, norm_ref):
    feats = [unpack(att_ref[n % 2, n // 2].astype(F32), 16) for n in range(HEADS)]
    attended = jnp.concatenate(feats, 0).T.astype(BF)
    branch = lax.dot_general(attended, weight[...], NT, preferred_element_type=F32)
    resid = tok_ref[...].astype(F32) + mod_ref[2:3, :] * branch
    resid_ref[...] = resid
    norm_ref[...] = (normalise(resid) * (1.0 + mod_ref[4:5, :]) + mod_ref[3:4, :]).astype(BF)


def temporal(n0, n1, n2, n3, weight, gain_ref, *out_refs):
    gap = jnp.zeros((128 - PATCH, D), BF)
    rows = jnp.concatenate([n0[...], gap, n1[...], gap, n2[...], gap, n3[...], gap], 0)
    proj = lax.dot_general(weight[...], rows, NT, preferred_element_type=F32)
    queries, keys, values = [], [], []
    for frame in range(4):
        here = slice(frame * 128, (frame + 1) * 128)
        heads = [proj[n * HD : (n + 1) * HD, here] for n in range(12)]
        queries.append([rms(v, gain_ref[:, 2:3]).astype(BF).astype(F32) for v in heads[:4]])
        keys.append([rms(v, gain_ref[:, 3:4]).astype(BF).astype(F32) for v in heads[4:8]])
        values.append([v.astype(BF).astype(F32) for v in heads[8:]])
    for f, out_ref in enumerate(out_refs):
        mixed = []
        for head in range(4):
            total, attended = 0.0, 0.0
            for g in range(4):
                score = jnp.sum(queries[f][head] * keys[g][head], 0, keepdims=True) * FACTOR
                expo = jnp.exp(score)
                total = total + expo
                attended = attended + expo.astype(BF).astype(F32) * values[g][head]
            mixed.append(attended / total)
        out_ref[...] = pack(jnp.concatenate(mixed, 0)[:, :PATCH], 3 * HD).astype(BF)


def temporal_end(place_ref, m0, m1, m2, m3, resid_ref, mod_ref, weight, *refs):
    out_ref, feats = refs[-2:]
    for step, att_ref in enumerate((m0, m1, m2, m3)):
        here = pl.ds(pl.multiple_of((place_ref[0] ^ step) * (4 * HD), 4 * HD), 4 * HD)
        feats[here, :] = unpack(att_ref[...].astype(F32), HD)
    attended = feats[...].T.astype(BF)
    branch = lax.dot_general(attended, weight[...], NT, preferred_element_type=F32)
    out_ref[...] = (resid_ref[...] + mod_ref[5:6, :] * branch).astype(BF)


SMEM = pl.BlockSpec(memory_space=pltpu.SMEM)


def full(array, lead=None, n=0):
    block = array.shape if lead is None else (lead,) + array.shape[1:]
    place = (n,) + (0,) * (array.ndim - 1)
    return pl.BlockSpec(block, lambda i: place)


def once(kernel, args, specs, shapes, out_specs=None, aliases=None, scratch=()):
    return pl.pallas_call(
        kernel,
        grid=(1,),
        in_specs=specs,
        out_specs=out_specs or [full(s) for s in shapes],
        out_shape=shapes,
        input_output_aliases=aliases or {},
        scratch_shapes=scratch,
        compiler_params=pltpu.CompilerParams(vmem_limit_bytes=20 * 1024 * 1024),
        cost_estimate=pl.CostEstimate(
            flops=20_000_000, bytes_accessed=100_000, transcendentals=0
        ),
        name=kernel.__name__,
    )(*args)


def shape(dtype, *sizes):
    return jax.ShapeDtypeStruct(sizes, dtype)


def per_device(tokens, modulation, spatial_qkv, spatial_out, temporal_qkv, temporal_out, norm_gains):
    core = lax.axis_index("c")
    frame = lax.axis_index("xl") * 2 + core
    place = frame.astype(jnp.int32).reshape(1)
    gains = norm_gains.T
    tok = tokens.reshape(ROWS, D)

    part_a = spatial_qkv.reshape(18, 3, NZ, 2 * HD).transpose(2, 0, 1, 3).reshape(NZ, 18, 6 * HD)
    part_a = jnp.pad(part_a, ((0, 0), (0, 0), (0, 512 - 6 * HD)))
    part_b = lax.dynamic_slice_in_dim(temporal_qkv.reshape(18, 3, D), frame * 4 * HD, 4 * HD, 2)
    part_b = jnp.pad(part_b.reshape(18, 12 * HD), ((0, 0), (0, 32))).reshape(18, NZ, 112)
    outs = jnp.where(core == 0, spatial_out, temporal_out).reshape(18, NZ, 2 * HD)
    rest = jnp.concatenate([outs, part_b], 2).transpose(1, 0, 2)
    shard = jnp.concatenate([part_a, rest], 2)
    shard = lax.all_to_all(shard, "z", 0, 0, tiled=True).reshape(1, NZ * 18, 768)
    shard = jnp.broadcast_to(shard, (8, NZ * 18, 768))
    shard = lax.all_to_all(shard, ("xh", "y"), 0, 0, tiled=True).reshape(D, 768)

    column = lax.all_gather(tok, "z", axis=0)

    projected, outs, part_b = pl.pallas_call(
        spatial_proj,
        grid=(2, 2),
        in_specs=[
            pl.BlockSpec((4, PATCH, D), lambda i, clip: (i, clip, 0)),
            pl.BlockSpec((6, D), lambda i, clip: (0, 0)),
            pl.BlockSpec((D, 768), lambda i, clip: (0, 0)),
            pl.BlockSpec((HD, 4), lambda i, clip: (0, 0)),
        ],
        out_specs=[
            pl.BlockSpec((2, 3 * HD + 8, 4 * PATCH), lambda i, clip: (clip, 0, i)),
            pl.BlockSpec((2 * HD, D), lambda i, clip: (0, 0)),
            pl.BlockSpec((112, D), lambda i, clip: (0, 0)),
        ],
        out_shape=[
            shape(BF, 4, 3 * HD + 8, PLANE),
            shape(BF, 2 * HD, D),
            shape(BF, 112, D),
        ],
        scratch_shapes=[pltpu.VMEM((512, D), BF)],
        compiler_params=PARAMS,
        name="spatial_proj",
    )(column, modulation, shard, gains)

    swap = [(0, 1), (1, 0)]
    outs = lax.all_gather(outs, "z", axis=0, tiled=True)
    turned = lax.all_gather(part_b, "z", axis=0, tiled=True)

    projected = lax.all_to_all(projected, "y", 0, 0, tiled=True)
    others = [lax.ppermute(projected[n, : 2 * HD], "xh", swap) for n in PIECES]
    part = attention(projected, projected, None, False)
    part = attention(projected, others[0], part, False)
    part = attention(projected, others[1], part, False)
    part, others[2], outs = lax.optimization_barrier((part, others[2], outs))
    attended = attention(projected, others[2], part, True)
    outs_got = lax.ppermute(outs, "c", swap)
    attended = attended.reshape(NY * NZ, 56, 128)
    attended = lax.all_to_all(attended, ("y", "z"), 0, 0, tiled=True)
    attended = attended.reshape(4, NZ, 56, 128)
    out_a = jnp.where(core == 0, outs, outs_got)
    out_b = jnp.where(core == 0, outs_got, outs)

    steps = []
    for clip in range(2):
        args = [attended, tok, modulation, out_a]
        specs = [full(attended, 2, clip), full(tok, PATCH, clip), full(modulation), full(out_a)]
        steps.append(once(spatial_end, args, specs, [shape(F32, PATCH, D), shape(BF, PATCH, D)]))
    diagonal = [(0, 3), (3, 0), (1, 2), (2, 1)]
    sent = []
    moved = [lax.ppermute(norm, "xl", swap) for _, norm in steps]
    moved[0], _ = lax.optimization_barrier((moved[0], steps[1][1]))
    for (_, norm), norm_x in zip(steps, moved):
        if sent:
            norm_x, sent[0][0] = lax.optimization_barrier((norm_x, sent[0][0]))
        args = [norm, lax.ppermute(norm, "c", swap), norm_x, lax.ppermute(norm_x, "c", swap)]
        args += [turned, gains]
        mixed = once(temporal, args, [full(a) for a in args], [shape(BF, 3 * HD, 128)] * 4)
        sent.append(
            [
                mixed[0],
                lax.ppermute(mixed[1], "c", swap),
                lax.ppermute(mixed[2], "xl", swap),
                lax.ppermute(mixed[3], ("xl", "c"), diagonal),
            ]
        )
    result = None
    for clip in range(2):
        args = sent[clip] + [steps[clip][0], modulation, out_b]
        specs = [SMEM] + [full(a) for a in args]
        aliases = None
        if result is not None:
            args, specs = args + [result], specs + [pl.BlockSpec(memory_space=pl.ANY)]
            aliases = {len(args): 0}
        whole = shape(BF, ROWS, D)
        out_specs = [full(whole, PATCH, clip)]
        scratch = [pltpu.VMEM((D, PATCH), F32)]
        args = [place] + args
        (result,) = once(temporal_end, args, specs, [whole], out_specs, aliases, scratch)
    return result.reshape(2, 1, PATCH, D)


def solution(mesh):
    fine = Mesh(mesh.devices.reshape(2, 2, 2, NY, NZ), ("xl", "c", "xh", "y", "z"))
    time, space = ("xl", "c"), ("xh", "y", "z")
    block = P(None, time, space, None)
    rows = P(space, None)
    return jax.shard_map(
        per_device,
        mesh=fine,
        in_specs=(block, P(), rows, rows, rows, rows, P()),
        out_specs=block,
        check_vma=False,
    )
```

```python
import functools
import math

import jax
import jax.numpy as jnp
from jax import lax
from jax.experimental import pallas as pl
from jax.experimental.pallas import tpu as pltpu
from jax.sharding import Mesh
from jax.sharding import PartitionSpec as P

D = 1152
HEADS = 16
HD = 72
HP = 80
PATCH = 96
ROWS = 2 * PATCH
NZ, NY = 8, 4
PLANE = NZ * PATCH
BF = jnp.bfloat16
F32 = jnp.float32
FACTOR = 1.0 / math.sqrt(HD)
TN = (((0,), (0,)), ((), ()))
NT = (((1,), (1,)), ((), ()))
SMEM = pl.BlockSpec(memory_space=pltpu.SMEM)
PARAMS = pltpu.CompilerParams(vmem_limit_bytes=48 * 1024 * 1024)


def normalise(values):
    mean_val = jnp.mean(values, -1, keepdims=True)
    centred = values - mean_val
    variance = jnp.mean(centred * centred, -1, keepdims=True)
    return centred * lax.rsqrt(variance + 1e-06)


def rms(values, gain):
    mean_sq = jnp.mean(values * values, 0, keepdims=True)
    return values * lax.rsqrt(mean_sq + 1e-06) * gain


def spatial_proj(y_ref, tok_ref, mod_ref, w_ref, gain_ref, s0, s1, s2, s3, turned):
    cols = 4 * PATCH
    zeros = jnp.zeros((HP - HD, cols), F32)

    @pl.when(pl.program_id(0) == 0)
    def _():
        turned[...] = w_ref[...].astype(F32).T.astype(BF)

    clips = []
    for clip in range(2):
        tok = tok_ref[:, clip * PATCH : (clip + 1) * PATCH, :].reshape(cols, D).astype(F32)
        normed = normalise(tok) * (1.0 + mod_ref[1:2, :]) + mod_ref[0:1, :]
        clips.append(normed.astype(BF))
    normed = jnp.concatenate(clips, 0)
    both = lax.dot_general(turned[: 6 * HD], normed, NT, preferred_element_type=F32)
    for clip in range(2):
        proj = both[:, clip * cols : (clip + 1) * cols]
        for head in range(2):
            query, key, value = (
                proj[part * 2 * HD + head * HD : part * 2 * HD + (head + 1) * HD] for part in range(3)
            )
            query = rms(query, gain_ref[:, 0:1]) * (FACTOR * math.log2(math.e))
            key = rms(key, gain_ref[:, 1:2])
            place = clip * 2 + head
            parts = [key, value, query, zeros]
            block = jnp.concatenate(parts, 0).astype(BF)
            slot = (place + NY - y_ref[0]) % NY
            for n, out_ref in enumerate((s0, s1, s2, s3)):

                @pl.when(slot == n)
                def _(out_ref=out_ref, block=block):
                    out_ref[0] = block


def pack(block, rows):
    strips = [block[rows:, n * 32 : (n + 1) * 32] for n in range(3)]
    spare = rows - 3 * strips[0].shape[0]
    if spare:
        strips.append(jnp.zeros((spare, 32), block.dtype))
    return jnp.concatenate([block[:rows], jnp.concatenate(strips, 0)], 1)


def unpack(packed, tall):
    strips = [packed[n * tall : (n + 1) * tall, PATCH:] for n in range(3)]
    return jnp.concatenate([packed[:, :PATCH], jnp.concatenate(strips, 1)], 0)


def attend(count, resume, finish, y_ref, *refs):
    q_refs, kv_refs = refs[:NY], refs[NY : NY + count]
    out_ref, query, keys, values = refs[-4:]
    place = pl.program_id(0)

    @pl.when(place == 0)
    def _():
        gap = jnp.zeros((128 - HD, PLANE), F32)
        first = lax.broadcasted_iota(jnp.int32, (HP - HD, PLANE), 0) == 0
        ones = jnp.where(first, 1.0, 0.0)
        for n, kv_ref in enumerate(kv_refs):
            both = kv_ref[0, : 2 * HD].astype(F32)
            keys[n] = jnp.concatenate([both[:HD], gap], 0).T.astype(BF)
            values[n] = jnp.concatenate([both[HD:], ones], 0).astype(BF)
        query[HP:] = jnp.zeros((128 - HP, PLANE), BF)

    for n, q_ref in enumerate(q_refs):

        @pl.when(place == n)
        def _(q_ref=q_ref):
            query[:HP] = q_ref[0, 2 * HD :]

    parts = [(n, slice(p, p + 256)) for n in range(count) for p in range(0, PLANE, 256)]

    def scores(n, here):
        return jnp.dot(keys[n, here, :], query[...], preferred_element_type=F32)

    done = refs[NY + count][0] if resume else None
    ahead = scores(*parts[0])
    for index, (n, here) in enumerate(parts):
        score = ahead
        if index + 1 < len(parts):
            ahead = scores(*parts[index + 1])
        expo = jnp.exp2(score).astype(BF)
        add = jnp.dot(values[n, :, here], expo, preferred_element_type=F32)
        done = add if done is None else done + add
    if not finish:
        out_ref[0] = done
        return
    done = done[:HD] / done[HD : HD + 1]
    home = (y_ref[0] + NY - place) % NY
    for z in range(NZ):
        out_ref[home, z] = pack(done[:, z * PATCH : (z + 1) * PATCH], 56).astype(BF)


def attention(y_place, queries, key_values, part, finish):
    count = len(key_values)
    sums = pl.BlockSpec((1, HP, PLANE), lambda q: (q, 0, 0))
    args = [y_place, *queries, *key_values]
    in_specs = [SMEM] + [pl.BlockSpec(a.shape, lambda q: (0, 0, 0)) for a in args[1:]]
    if part is not None:
        in_specs.append(sums)
        args.append(part)
    if finish:
        out_spec = pl.BlockSpec((NY, NZ, 56, 128), lambda q: (0, 0, 0, 0))
        out_shape = shape(BF, NY, NZ, 56, 128)
    else:
        out_spec = sums
        out_shape = shape(F32, NY, HP, PLANE)
    pairs = count * NY * PLANE * PLANE
    return pl.pallas_call(
        functools.partial(attend, count, part is not None, finish),
        grid=(NY,),
        in_specs=in_specs,
        out_specs=out_spec,
        out_shape=out_shape,
        scratch_shapes=[
            pltpu.VMEM((128, PLANE), BF),
            pltpu.VMEM((count, PLANE, 128), BF),
            pltpu.VMEM((count, HP, PLANE), BF),
        ],
        compiler_params=PARAMS,
        cost_estimate=pl.CostEstimate(
            flops=4 * pairs, bytes_accessed=1_000_000, transcendentals=0
        ),
        name="attend",
    )(*args)


def prepare(rest, own, turned):
    for n in range(5):
        width = min(256, D - n * 256)
        own[:, n * 256 : n * 256 + width] = rest[n, :, :width]
    turned[:128] = rest[4, :, 128:].astype(F32).T.astype(BF)
    for n in range(3):
        turned[128 + n * 256 : 384 + n * 256] = rest[5 + n].astype(F32).T.astype(BF)


def spatial_end(place_ref, att_ref, tok_ref, mod_ref, own, got, resid_ref, norm_ref):
    feats = [unpack(att_ref[n % 2, n // 2].astype(F32), 16) for n in range(HEADS)]
    attended = jnp.concatenate(feats, 0).T.astype(BF)
    weight = jnp.where(place_ref[0] == 1, got[...], own[...])
    branch = jnp.dot(attended, weight, preferred_element_type=F32)
    resid = tok_ref[...].astype(F32) + mod_ref[2:3, :] * branch
    resid_ref[...] = resid
    norm_ref[...] = (normalise(resid) * (1.0 + mod_ref[4:5, :]) + mod_ref[3:4, :]).astype(BF)


def temporal(n0, n1, n2, n3, weight, gain_ref, *out_refs):
    gap = jnp.zeros((128 - PATCH, D), BF)
    rows = jnp.concatenate([n0[...], gap, n1[...], gap, n2[...], gap, n3[...], gap], 0)
    proj = lax.dot_general(weight[...], rows, NT, preferred_element_type=F32)
    queries, keys, values = [], [], []
    for frame in range(4):
        here = slice(frame * 128, (frame + 1) * 128)
        heads = [proj[n * HD : (n + 1) * HD, here] for n in range(12)]
        queries.append([rms(v, gain_ref[:, 2:3]).astype(BF).astype(F32) for v in heads[:4]])
        keys.append([rms(v, gain_ref[:, 3:4]).astype(BF).astype(F32) for v in heads[4:8]])
        values.append([v.astype(BF).astype(F32) for v in heads[8:]])
    for f, out_ref in enumerate(out_refs):
        mixed = []
        for head in range(4):
            total, attended = 0.0, 0.0
            for g in range(4):
                score = jnp.sum(queries[f][head] * keys[g][head], 0, keepdims=True) * FACTOR
                expo = jnp.exp(score)
                total = total + expo
                attended = attended + expo.astype(BF).astype(F32) * values[g][head]
            mixed.append(attended / total)
        out_ref[...] = pack(jnp.concatenate(mixed, 0)[:, :PATCH], 3 * HD).astype(BF)


def temporal_end(place_ref, m0, m1, m2, m3, resid_ref, mod_ref, own, got, *out_refs):
    second, branch = place_ref[0] == 1, None
    for step, att_ref in enumerate((m0, m1, m2, m3)):
        feats = unpack(att_ref[...].astype(F32), HD)
        here = pl.ds(pl.multiple_of((place_ref[1] ^ step) * (4 * HD), 4 * HD), 4 * HD)
        rows = jnp.where(second, own[here, :], got[here, :])
        add = jnp.dot(feats.T.astype(BF), rows, preferred_element_type=F32)
        branch = add if branch is None else branch + add
    out_refs[-1][...] = (resid_ref[...] + mod_ref[5:6, :] * branch).astype(BF)


def full(array, lead=None, n=0):
    block = array.shape if lead is None else (lead,) + array.shape[1:]
    place = (n,) + (0,) * (array.ndim - 1)
    return pl.BlockSpec(block, lambda i: place)


def once(kernel, args, specs, shapes, out_specs=None, aliases=None):
    return pl.pallas_call(
        kernel,
        grid=(1,),
        in_specs=specs,
        out_specs=out_specs or [full(s) for s in shapes],
        out_shape=shapes,
        input_output_aliases=aliases or {},
        compiler_params=PARAMS,
        cost_estimate=pl.CostEstimate(
            flops=2_000_000_000, bytes_accessed=8_000_000, transcendentals=0
        ),
        name=kernel.__name__,
    )(*args)


def shape(dtype, *sizes):
    return jax.ShapeDtypeStruct(sizes, dtype)


def per_device(tokens, modulation, spatial_qkv, spatial_out, temporal_qkv, temporal_out, norm_gains):
    core = lax.axis_index("c")
    frame = lax.axis_index("xl") * 2 + core
    place = jnp.stack([core, frame]).astype(jnp.int32)
    gains = norm_gains.T
    tok = tokens.reshape(ROWS, D)

    part_a = spatial_qkv.reshape(18, 3, NZ, 2 * HD).transpose(2, 0, 1, 3).reshape(NZ, 18, 6 * HD)
    part_a = jnp.pad(part_a, ((0, 0), (0, 0), (0, 512 - 6 * HD)))
    part_b = lax.dynamic_slice_in_dim(temporal_qkv.reshape(18, 3, D), frame * 4 * HD, 4 * HD, 2)
    rest = [jnp.where(core == 0, spatial_out, temporal_out), part_b.reshape(18, 12 * HD)]
    rest = jnp.pad(jnp.concatenate(rest, 1), ((0, 0), (0, 256 * NZ - D - 12 * HD)))
    rest = rest.reshape(18, NZ, 256).transpose(1, 0, 2)
    shard = jnp.concatenate([part_a, rest], 2)
    shard = lax.all_to_all(shard, "z", 0, 0, tiled=True).reshape(1, NZ * 18, 768)
    shard = jnp.broadcast_to(shard, (8, NZ * 18, 768))
    shard = lax.all_to_all(shard, ("xh", "y"), 0, 0, tiled=True).reshape(D, 768)

    column = lax.all_gather(tok, "z", axis=0)

    rest, column = lax.optimization_barrier((shard[:, 512:], column))
    rest = lax.all_gather(rest, "z", axis=0)

    y_place = lax.axis_index("y").astype(jnp.int32).reshape(1)
    slots = pl.pallas_call(
        spatial_proj,
        grid=(2,),
        in_specs=[
            SMEM,
            pl.BlockSpec((4, ROWS, D), lambda i: (i, 0, 0)),
            pl.BlockSpec((6, D), lambda i: (0, 0)),
            pl.BlockSpec((D, 512), lambda i: (0, 0)),
            pl.BlockSpec((HD, 4), lambda i: (0, 0)),
        ],
        out_specs=[pl.BlockSpec((1, 3 * HD + 8, 4 * PATCH), lambda i: (0, 0, i))] * NY,
        out_shape=[shape(BF, 1, 3 * HD + 8, PLANE)] * NY,
        scratch_shapes=[pltpu.VMEM((512, D), BF)],
        compiler_params=PARAMS,
        name="spatial_proj",
    )(y_place, column, modulation, shard, gains)

    swap = [(0, 1), (1, 0)]
    blocks = list(slots)
    for n in (1, 3, 2):
        blocks[n] = lax.ppermute(slots[n], "y", [(i, (i + n) % NY) for i in range(NY)])
    others = [lax.ppermute(block[:, : 2 * HD], "xh", swap) for block in blocks]
    part = attention(y_place, blocks, blocks, None, False)
    part = attention(y_place, blocks, [others[n] for n in (0, 1, 3)], part, False)
    attended = attention(y_place, blocks, [others[2]], part, True)
    attended = attended.reshape(NY * NZ, 56, 128)
    attended = lax.all_to_all(attended, ("y", "z"), 0, 0, tiled=True)
    attended = attended.reshape(4, NZ, 56, 128)
    own, turned = once(prepare, [rest], [full(rest)], [shape(BF, D, D), shape(BF, 896, D)])
    swapped, _ = lax.optimization_barrier((own, attended))
    got = lax.ppermute(swapped, "c", swap)

    steps = []
    for clip in range(2):
        args = [place, attended, tok, modulation, own, got]
        specs = [SMEM, full(attended, 2, clip), full(tok, PATCH, clip)]
        specs += [full(a) for a in args[3:]]
        steps.append(once(spatial_end, args, specs, [shape(F32, PATCH, D), shape(BF, PATCH, D)]))
    diagonal = [(0, 3), (3, 0), (1, 2), (2, 1)]
    sent = []
    moved = [lax.ppermute(norm, "xl", swap) for _, norm in steps]
    moved[0], _ = lax.optimization_barrier((moved[0], steps[1][1]))
    for (_, norm), norm_x in zip(steps, moved):
        if sent:
            norm_x, sent[0][0] = lax.optimization_barrier((norm_x, sent[0][0]))
        args = [norm, lax.ppermute(norm, "c", swap), norm_x, lax.ppermute(norm_x, "c", swap)]
        args += [turned, gains]
        mixed = once(temporal, args, [full(a) for a in args], [shape(BF, 3 * HD, 128)] * 4)
        sent.append(
            [
                mixed[0],
                lax.ppermute(mixed[1], "c", swap),
                lax.ppermute(mixed[2], "xl", swap),
                lax.ppermute(mixed[3], ("xl", "c"), diagonal),
            ]
        )
    result = None
    for clip in range(2):
        args = sent[clip] + [steps[clip][0], modulation, own, got]
        specs = [SMEM] + [full(a) for a in args]
        aliases = None
        if result is not None:
            args, specs = args + [result], specs + [pl.BlockSpec(memory_space=pl.ANY)]
            aliases = {len(args): 0}
        whole = shape(BF, ROWS, D)
        out_specs = [full(whole, PATCH, clip)]
        (result,) = once(temporal_end, [place] + args, specs, [whole], out_specs, aliases)
    return result.reshape(2, 1, PATCH, D)


def solution(mesh):
    fine = Mesh(mesh.devices.reshape(2, 2, 2, NY, NZ), ("xl", "c", "xh", "y", "z"))
    time, space = ("xl", "c"), ("xh", "y", "z")
    block = P(None, time, space, None)
    rows = P(space, None)
    return jax.shard_map(
        per_device,
        mesh=fine,
        in_specs=(block, P(), rows, rows, rows, rows, P()),
        out_specs=block,
        check_vma=False,
    )
```

```python
import functools
import math

import jax
import jax.numpy as jnp
from jax import lax
from jax.experimental import pallas as pl
from jax.experimental.pallas import tpu as pltpu
from jax.sharding import Mesh
from jax.sharding import PartitionSpec as P

D = 1152
HEADS = 16
HD = 72
HP = 80
PATCH = 96
ROWS = 2 * PATCH
NZ, NY = 8, 4
PLANE = NZ * PATCH
BF = jnp.bfloat16
F32 = jnp.float32
FACTOR = 1.0 / math.sqrt(HD)
TN = (((0,), (0,)), ((), ()))
NT = (((1,), (1,)), ((), ()))
SMEM = pl.BlockSpec(memory_space=pltpu.SMEM)
PARAMS = pltpu.CompilerParams(vmem_limit_bytes=48 * 1024 * 1024)


def normalise(values):
    mean_val = jnp.mean(values, -1, keepdims=True)
    centred = values - mean_val
    variance = jnp.mean(centred * centred, -1, keepdims=True)
    return centred * lax.rsqrt(variance + 1e-06)


def rms(values, gain):
    mean_sq = jnp.mean(values * values, 0, keepdims=True)
    return values * lax.rsqrt(mean_sq + 1e-06) * gain


def spatial_proj(y_ref, tok_ref, mod_ref, w_ref, gain_ref, s0, s1, s2, s3, turned):
    cols = 4 * PATCH
    zeros = jnp.zeros((HP - HD, cols), F32)

    @pl.when(pl.program_id(0) == 0)
    def _():
        turned[...] = w_ref[...].astype(F32).T.astype(BF)

    clips = []
    for clip in range(2):
        tok = tok_ref[:, clip * PATCH : (clip + 1) * PATCH, :].reshape(cols, D).astype(F32)
        normed = normalise(tok) * (1.0 + mod_ref[1:2, :]) + mod_ref[0:1, :]
        clips.append(normed.astype(BF))
    normed = jnp.concatenate(clips, 0)
    both = lax.dot_general(turned[: 6 * HD], normed, NT, preferred_element_type=F32)
    for clip in range(2):
        proj = both[:, clip * cols : (clip + 1) * cols]
        for head in range(2):
            query, key, value = (
                proj[part * 2 * HD + head * HD : part * 2 * HD + (head + 1) * HD] for part in range(3)
            )
            query = rms(query, gain_ref[:, 0:1]) * (FACTOR * math.log2(math.e))
            key = rms(key, gain_ref[:, 1:2])
            place = clip * 2 + head
            parts = [key, value, query, zeros]
            block = jnp.concatenate(parts, 0).astype(BF)
            slot = (place + NY - y_ref[0]) % NY
            for n, out_ref in enumerate((s0, s1, s2, s3)):

                @pl.when(slot == n)
                def _(out_ref=out_ref, block=block):
                    out_ref[0] = block


def pack(block, rows):
    strips = [block[rows:, n * 32 : (n + 1) * 32] for n in range(3)]
    spare = rows - 3 * strips[0].shape[0]
    if spare:
        strips.append(jnp.zeros((spare, 32), block.dtype))
    return jnp.concatenate([block[:rows], jnp.concatenate(strips, 0)], 1)


def unpack(packed, tall):
    strips = [packed[n * tall : (n + 1) * tall, PATCH:] for n in range(3)]
    return jnp.concatenate([packed[:, :PATCH], jnp.concatenate(strips, 1)], 0)


def attend(count, resume, finish, y_ref, *refs):
    q_refs, kv_refs = refs[:NY], refs[NY : NY + count]
    out_ref, query, keys, values = refs[-4:]
    place = pl.program_id(0)

    @pl.when(place == 0)
    def _():
        gap = jnp.zeros((128 - HD, PLANE), F32)
        first = lax.broadcasted_iota(jnp.int32, (HP - HD, PLANE), 0) == 0
        ones = jnp.where(first, 1.0, 0.0)
        for n, kv_ref in enumerate(kv_refs):
            both = kv_ref[0, : 2 * HD].astype(F32)
            keys[n] = jnp.concatenate([both[:HD], gap], 0).T.astype(BF)
            values[n] = jnp.concatenate([both[HD:], ones], 0).astype(BF)
        query[HP:] = jnp.zeros((128 - HP, PLANE), BF)

    for n, q_ref in enumerate(q_refs):

        @pl.when(place == n)
        def _(q_ref=q_ref):
            query[:HP] = q_ref[0, 2 * HD :]

    parts = [(n, slice(p, p + 256)) for n in range(count) for p in range(0, PLANE, 256)]

    def scores(n, here):
        return jnp.dot(keys[n, here, :], query[...], preferred_element_type=F32)

    done = refs[NY + count][0] if resume else None
    ahead = scores(*parts[0])
    for index, (n, here) in enumerate(parts):
        score = ahead
        if index + 1 < len(parts):
            ahead = scores(*parts[index + 1])
        expo = jnp.exp2(score).astype(BF)
        add = jnp.dot(values[n, :, here], expo, preferred_element_type=F32)
        done = add if done is None else done + add
    if not finish:
        out_ref[0] = done
        return
    done = done[:HD] / done[HD : HD + 1]
    home = (y_ref[0] + NY - place) % NY
    for z in range(NZ):
        out_ref[home, z] = pack(done[:, z * PATCH : (z + 1) * PATCH], 56).astype(BF)


def attention(y_place, queries, key_values, part, finish):
    count = len(key_values)
    sums = pl.BlockSpec((1, HP, PLANE), lambda q: (q, 0, 0))
    args = [y_place, *queries, *key_values]
    in_specs = [SMEM] + [pl.BlockSpec(a.shape, lambda q: (0, 0, 0)) for a in args[1:]]
    if part is not None:
        in_specs.append(sums)
        args.append(part)
    if finish:
        out_spec = pl.BlockSpec((NY, NZ, 56, 128), lambda q: (0, 0, 0, 0))
        out_shape = shape(BF, NY, NZ, 56, 128)
    else:
        out_spec = sums
        out_shape = shape(F32, NY, HP, PLANE)
    pairs = count * NY * PLANE * PLANE
    return pl.pallas_call(
        functools.partial(attend, count, part is not None, finish),
        grid=(NY,),
        in_specs=in_specs,
        out_specs=out_spec,
        out_shape=out_shape,
        scratch_shapes=[
            pltpu.VMEM((128, PLANE), BF),
            pltpu.VMEM((count, PLANE, 128), BF),
            pltpu.VMEM((count, HP, PLANE), BF),
        ],
        compiler_params=PARAMS,
        cost_estimate=pl.CostEstimate(
            flops=4 * pairs, bytes_accessed=1_000_000, transcendentals=0
        ),
        name="attend",
    )(*args)


def prepare(rest, out_a, turned, out_b):
    half, last = D // 2, D // 2 + 12 * HD
    for n in range(NZ):
        chunk = rest[n].astype(F32).T.astype(BF)
        low, high = n * 256, (n + 1) * 256
        for ref, begin, end in ((out_a, 0, half), (turned, half, last), (out_b, last, last + half)):
            first, stop = max(low, begin), min(high, end)
            if first < stop:
                ref[first - begin : stop - begin] = chunk[first - low : stop - low]


def both_halves(second, own, got):
    return jnp.where(second, jnp.concatenate([got, own], 1), jnp.concatenate([own, got], 1))


def spatial_end(place_ref, att_ref, tok_ref, mod_ref, own, got, resid_ref, norm_ref):
    feats = [unpack(att_ref[n % 2, n // 2].astype(F32), 16) for n in range(HEADS)]
    attended = jnp.concatenate(feats, 0).T.astype(BF)
    halves = [
        lax.dot_general(attended, w[...], NT, preferred_element_type=F32) for w in (own, got)
    ]
    branch = both_halves(place_ref[0] == 1, *halves)
    resid = tok_ref[...].astype(F32) + mod_ref[2:3, :] * branch
    resid_ref[...] = resid
    norm_ref[...] = (normalise(resid) * (1.0 + mod_ref[4:5, :]) + mod_ref[3:4, :]).astype(BF)


def temporal(n0, n1, n2, n3, weight, gain_ref, *out_refs):
    gap = jnp.zeros((128 - PATCH, D), BF)
    rows = jnp.concatenate([n0[...], gap, n1[...], gap, n2[...], gap, n3[...], gap], 0)
    proj = lax.dot_general(weight[...], rows, NT, preferred_element_type=F32)
    queries, keys, values = [], [], []
    for frame in range(4):
        here = slice(frame * 128, (frame + 1) * 128)
        heads = [proj[n * HD : (n + 1) * HD, here] for n in range(12)]
        queries.append([rms(v, gain_ref[:, 2:3]).astype(BF).astype(F32) for v in heads[:4]])
        keys.append([rms(v, gain_ref[:, 3:4]).astype(BF).astype(F32) for v in heads[4:8]])
        values.append([v.astype(BF).astype(F32) for v in heads[8:]])
    for f, out_ref in enumerate(out_refs):
        mixed = []
        for head in range(4):
            total, attended = 0.0, 0.0
            for g in range(4):
                score = jnp.sum(queries[f][head] * keys[g][head], 0, keepdims=True) * FACTOR
                expo = jnp.exp(score)
                total = total + expo
                attended = attended + expo.astype(BF).astype(F32) * values[g][head]
            mixed.append(attended / total)
        out_ref[...] = pack(jnp.concatenate(mixed, 0)[:, :PATCH], 3 * HD).astype(BF)


def temporal_end(place_ref, m0, m1, m2, m3, resid_ref, mod_ref, own, got, *refs):
    out_ref, feats = refs[-2:]
    for step, att_ref in enumerate((m0, m1, m2, m3)):
        here = pl.ds(pl.multiple_of((place_ref[1] ^ step) * (4 * HD), 4 * HD), 4 * HD)
        feats[here, :] = unpack(att_ref[...].astype(F32), HD)
    attended = feats[...].T.astype(BF)
    halves = [
        lax.dot_general(attended, w[...], NT, preferred_element_type=F32) for w in (own, got)
    ]
    branch = both_halves(place_ref[0] == 1, *halves)
    out_ref[...] = (resid_ref[...] + mod_ref[5:6, :] * branch).astype(BF)


def full(array, lead=None, n=0):
    block = array.shape if lead is None else (lead,) + array.shape[1:]
    place = (n,) + (0,) * (array.ndim - 1)
    return pl.BlockSpec(block, lambda i: place)


def once(kernel, args, specs, shapes, out_specs=None, aliases=None, scratch=()):
    return pl.pallas_call(
        kernel,
        grid=(1,),
        in_specs=specs,
        out_specs=out_specs or [full(s) for s in shapes],
        out_shape=shapes,
        input_output_aliases=aliases or {},
        scratch_shapes=scratch,
        compiler_params=pltpu.CompilerParams(vmem_limit_bytes=24 * 1024 * 1024),
        cost_estimate=pl.CostEstimate(
            flops=2_000_000_000, bytes_accessed=8_000_000, transcendentals=0
        ),
        name=kernel.__name__,
    )(*args)


def shape(dtype, *sizes):
    return jax.ShapeDtypeStruct(sizes, dtype)


def per_device(tokens, modulation, spatial_qkv, spatial_out, temporal_qkv, temporal_out, norm_gains):
    core = lax.axis_index("c")
    frame = lax.axis_index("xl") * 2 + core
    place = jnp.stack([core, frame]).astype(jnp.int32)
    gains = norm_gains.T
    tok = tokens.reshape(ROWS, D)

    half = D // 2
    part_a = spatial_qkv.reshape(18, 3, NZ, 2 * HD).transpose(2, 0, 1, 3).reshape(NZ, 18, 6 * HD)
    part_a = jnp.pad(part_a, ((0, 0), (0, 0), (0, 512 - 6 * HD)))
    part_b = lax.dynamic_slice_in_dim(temporal_qkv.reshape(18, 3, D), frame * 4 * HD, 4 * HD, 2)
    rest = [
        jnp.where(core == 0, spatial_out[:, :half], spatial_out[:, half:]),
        part_b.reshape(18, 12 * HD),
        jnp.where(core == 0, temporal_out[:, :half], temporal_out[:, half:]),
    ]
    rest = jnp.pad(jnp.concatenate(rest, 1), ((0, 0), (0, 256 * NZ - D - 12 * HD)))
    rest = rest.reshape(18, NZ, 256).transpose(1, 0, 2)
    shard = jnp.concatenate([part_a, rest], 2)
    shard = lax.all_to_all(shard, "z", 0, 0, tiled=True).reshape(1, NZ * 18, 768)
    shard = jnp.broadcast_to(shard, (8, NZ * 18, 768))
    shard = lax.all_to_all(shard, ("xh", "y"), 0, 0, tiled=True).reshape(D, 768)

    column = lax.all_gather(tok, "z", axis=0)

    rest, column = lax.optimization_barrier((shard[:, 512:], column))
    rest = lax.all_gather(rest, "z", axis=0)

    y_place = lax.axis_index("y").astype(jnp.int32).reshape(1)
    slots = pl.pallas_call(
        spatial_proj,
        grid=(2,),
        in_specs=[
            SMEM,
            pl.BlockSpec((4, ROWS, D), lambda i: (i, 0, 0)),
            pl.BlockSpec((6, D), lambda i: (0, 0)),
            pl.BlockSpec((D, 512), lambda i: (0, 0)),
            pl.BlockSpec((HD, 4), lambda i: (0, 0)),
        ],
        out_specs=[pl.BlockSpec((1, 3 * HD + 8, 4 * PATCH), lambda i: (0, 0, i))] * NY,
        out_shape=[shape(BF, 1, 3 * HD + 8, PLANE)] * NY,
        scratch_shapes=[pltpu.VMEM((512, D), BF)],
        compiler_params=PARAMS,
        name="spatial_proj",
    )(y_place, column, modulation, shard, gains)

    swap = [(0, 1), (1, 0)]
    blocks = list(slots)
    for n in (1, 3, 2):
        blocks[n] = lax.ppermute(slots[n], "y", [(i, (i + n) % NY) for i in range(NY)])
    others = [lax.ppermute(block[:, : 2 * HD], "xh", swap) for block in blocks]
    part = attention(y_place, blocks, blocks, None, False)
    part = attention(y_place, blocks, [others[n] for n in (0, 1, 3)], part, False)
    attended = attention(y_place, blocks, [others[2]], part, True)
    attended = attended.reshape(NY * NZ, 56, 128)
    attended = lax.all_to_all(attended, ("y", "z"), 0, 0, tiled=True)
    attended = attended.reshape(4, NZ, 56, 128)
    shapes = [shape(BF, half, D), shape(BF, 12 * HD, D), shape(BF, half, D)]
    out_a, turned, out_b = once(prepare, [rest], [full(rest)], shapes)
    swapped, _ = lax.optimization_barrier((out_a, attended))
    got_a = lax.ppermute(swapped, "c", swap)

    steps = []
    for clip in range(2):
        args = [place, attended, tok, modulation, out_a, got_a]
        specs = [SMEM, full(attended, 2, clip), full(tok, PATCH, clip)]
        specs += [full(a) for a in args[3:]]
        steps.append(once(spatial_end, args, specs, [shape(F32, PATCH, D), shape(BF, PATCH, D)]))
    swapped, _ = lax.optimization_barrier((out_b, steps[1][1]))
    got_b = lax.ppermute(swapped, "c", swap)
    diagonal = [(0, 3), (3, 0), (1, 2), (2, 1)]
    sent = []
    moved = [lax.ppermute(norm, "xl", swap) for _, norm in steps]
    moved[0], _ = lax.optimization_barrier((moved[0], steps[1][1]))
    for (_, norm), norm_x in zip(steps, moved):
        if sent:
            norm_x, sent[0][0] = lax.optimization_barrier((norm_x, sent[0][0]))
        args = [norm, lax.ppermute(norm, "c", swap), norm_x, lax.ppermute(norm_x, "c", swap)]
        args += [turned, gains]
        mixed = once(temporal, args, [full(a) for a in args], [shape(BF, 3 * HD, 128)] * 4)
        sent.append(
            [
                mixed[0],
                lax.ppermute(mixed[1], "c", swap),
                lax.ppermute(mixed[2], "xl", swap),
                lax.ppermute(mixed[3], ("xl", "c"), diagonal),
            ]
        )
    result = None
    for clip in range(2):
        args = sent[clip] + [steps[clip][0], modulation, out_b, got_b]
        specs = [SMEM] + [full(a) for a in args]
        aliases = None
        if result is not None:
            args, specs = args + [result], specs + [pl.BlockSpec(memory_space=pl.ANY)]
            aliases = {len(args): 0}
        whole = shape(BF, ROWS, D)
        out_specs = [full(whole, PATCH, clip)]
        scratch = [pltpu.VMEM((D, PATCH), F32)]
        args = [place] + args
        (result,) = once(temporal_end, args, specs, [whole], out_specs, aliases, scratch)
    return result.reshape(2, 1, PATCH, D)


def solution(mesh):
    fine = Mesh(mesh.devices.reshape(2, 2, 2, NY, NZ), ("xl", "c", "xh", "y", "z"))
    time, space = ("xl", "c"), ("xh", "y", "z")
    block = P(None, time, space, None)
    rows = P(space, None)
    return jax.shard_map(
        per_device,
        mesh=fine,
        in_specs=(block, P(), rows, rows, rows, rows, P()),
        out_specs=block,
        check_vma=False,
    )
```

```python
import functools
import math

import jax
import jax.numpy as jnp
from jax import lax
from jax.experimental import pallas as pl
from jax.experimental.pallas import tpu as pltpu
from jax.sharding import Mesh
from jax.sharding import PartitionSpec as P

D = 1152
HEADS = 16
HD = 72
HP = 80
PATCH = 96
ROWS = 2 * PATCH
NZ, NY = 8, 4
PLANE = NZ * PATCH
BF = jnp.bfloat16
F32 = jnp.float32
FACTOR = 1.0 / math.sqrt(HD)
TN = (((0,), (0,)), ((), ()))
NT = (((1,), (1,)), ((), ()))
SMEM = pl.BlockSpec(memory_space=pltpu.SMEM)
PARAMS = pltpu.CompilerParams(vmem_limit_bytes=32 * 1024 * 1024)


def normalise(values):
    mean_val = jnp.mean(values, -1, keepdims=True)
    centred = values - mean_val
    variance = jnp.mean(centred * centred, -1, keepdims=True)
    return centred * lax.rsqrt(variance + 1e-06)


def rms(values, gain):
    mean_sq = jnp.mean(values * values, 0, keepdims=True)
    return values * lax.rsqrt(mean_sq + 1e-06) * gain


def spatial_proj(y_ref, tok_ref, mod_ref, w_ref, gain_ref, s0, s1, s2, s3, turned):
    cols = 4 * PATCH
    zeros = jnp.zeros((HP - HD, cols), F32)

    @pl.when(pl.program_id(0) == 0)
    def _():
        turned[...] = w_ref[...].astype(F32).T.astype(BF)

    clips = []
    for clip in range(2):
        tok = tok_ref[:, clip * PATCH : (clip + 1) * PATCH, :].reshape(cols, D).astype(F32)
        normed = normalise(tok) * (1.0 + mod_ref[1:2, :]) + mod_ref[0:1, :]
        clips.append(normed.astype(BF))
    normed = jnp.concatenate(clips, 0)
    both = lax.dot_general(turned[: 6 * HD], normed, NT, preferred_element_type=F32)
    for clip in range(2):
        proj = both[:, clip * cols : (clip + 1) * cols]
        for head in range(2):
            query, key, value = (
                proj[part * 2 * HD + head * HD : part * 2 * HD + (head + 1) * HD] for part in range(3)
            )
            query = rms(query, gain_ref[:, 0:1]) * (FACTOR * math.log2(math.e))
            key = rms(key, gain_ref[:, 1:2])
            place = clip * 2 + head
            parts = [key, value, query, zeros]
            block = jnp.concatenate(parts, 0).astype(BF)
            slot = (place + NY - y_ref[0]) % NY
            for n, out_ref in enumerate((s0, s1, s2, s3)):

                @pl.when(slot == n)
                def _(out_ref=out_ref, block=block):
                    out_ref[0] = block


def pack(block, rows):
    strips = [block[rows:, n * 32 : (n + 1) * 32] for n in range(3)]
    spare = rows - 3 * strips[0].shape[0]
    if spare:
        strips.append(jnp.zeros((spare, 32), block.dtype))
    return jnp.concatenate([block[:rows], jnp.concatenate(strips, 0)], 1)


def unpack(packed, tall):
    strips = [packed[n * tall : (n + 1) * tall, PATCH:] for n in range(3)]
    return jnp.concatenate([packed[:, :PATCH], jnp.concatenate(strips, 1)], 0)


def attend(count, resume, finish, y_ref, *refs):
    q_refs, kv_refs = refs[:NY], refs[NY : NY + count]
    out_ref, query, keys, values = refs[-4:]
    place = pl.program_id(0)

    @pl.when(place == 0)
    def _():
        gap = jnp.zeros((128 - HD, PLANE), F32)
        first = lax.broadcasted_iota(jnp.int32, (HP - HD, PLANE), 0) == 0
        ones = jnp.where(first, 1.0, 0.0)
        for n, kv_ref in enumerate(kv_refs):
            both = kv_ref[0, : 2 * HD].astype(F32)
            keys[n] = jnp.concatenate([both[:HD], gap], 0).T.astype(BF)
            values[n] = jnp.concatenate([both[HD:], ones], 0).astype(BF)
        query[HP:] = jnp.zeros((128 - HP, PLANE), BF)

    for n, q_ref in enumerate(q_refs):

        @pl.when(place == n)
        def _(q_ref=q_ref):
            query[:HP] = q_ref[0, 2 * HD :]

    parts = [(n, slice(p, p + 256)) for n in range(count) for p in range(0, PLANE, 256)]

    def scores(n, here):
        return jnp.dot(keys[n, here, :], query[...], preferred_element_type=F32)

    done = refs[NY + count][0] if resume else None
    ahead = scores(*parts[0])
    for index, (n, here) in enumerate(parts):
        score = ahead
        if index + 1 < len(parts):
            ahead = scores(*parts[index + 1])
        expo = jnp.exp2(score).astype(BF)
        add = jnp.dot(values[n, :, here], expo, preferred_element_type=F32)
        done = add if done is None else done + add
    if not finish:
        out_ref[0] = done
        return
    done = done[:HD] / done[HD : HD + 1]
    home = (y_ref[0] + NY - place) % NY
    for z in range(NZ):
        out_ref[home, z] = pack(done[:, z * PATCH : (z + 1) * PATCH], 56).astype(BF)


def attention(y_place, queries, key_values, part, finish):
    count = len(key_values)
    sums = pl.BlockSpec((1, HP, PLANE), lambda q: (q, 0, 0))
    args = [y_place, *queries, *key_values]
    in_specs = [SMEM] + [pl.BlockSpec(a.shape, lambda q: (0, 0, 0)) for a in args[1:]]
    if part is not None:
        in_specs.append(sums)
        args.append(part)
    if finish:
        out_spec = pl.BlockSpec((NY, NZ, 56, 128), lambda q: (0, 0, 0, 0))
        out_shape = shape(BF, NY, NZ, 56, 128)
    else:
        out_spec = sums
        out_shape = shape(F32, NY, HP, PLANE)
    pairs = count * NY * PLANE * PLANE
    return pl.pallas_call(
        functools.partial(attend, count, part is not None, finish),
        grid=(NY,),
        in_specs=in_specs,
        out_specs=out_spec,
        out_shape=out_shape,
        scratch_shapes=[
            pltpu.VMEM((128, PLANE), BF),
            pltpu.VMEM((count, PLANE, 128), BF),
            pltpu.VMEM((count, HP, PLANE), BF),
        ],
        compiler_params=PARAMS,
        cost_estimate=pl.CostEstimate(
            flops=4 * pairs, bytes_accessed=1_000_000, transcendentals=0
        ),
        name="attend",
    )(*args)


def prepare(rest, out_a, turned, out_b):
    half, last = D // 2, D // 2 + 12 * HD
    out_a[:, :256] = rest[0]
    out_a[:, 256:512] = rest[1]
    out_a[:, 512:] = rest[2, :, :128]
    for n in range(2, NZ):
        chunk = rest[n].astype(F32).T.astype(BF)
        low, high = n * 256, (n + 1) * 256
        for ref, begin, end in ((turned, half, last), (out_b, last, last + half)):
            first, stop = max(low, begin), min(high, end)
            if first < stop:
                ref[first - begin : stop - begin] = chunk[first - low : stop - low]


def both_halves(second, own, got):
    return jnp.where(second, jnp.concatenate([got, own], 1), jnp.concatenate([own, got], 1))


def spatial_end(place_ref, att_ref, tok_ref, mod_ref, own, got, resid_ref, norm_ref):
    feats = [unpack(att_ref[n % 2, n // 2].astype(F32), 16) for n in range(HEADS)]
    attended = jnp.concatenate(feats, 0).T.astype(BF)
    halves = [jnp.dot(attended, w[...], preferred_element_type=F32) for w in (own, got)]
    branch = both_halves(place_ref[0] == 1, *(h[:, : D // 2] for h in halves))
    resid = tok_ref[...].astype(F32) + mod_ref[2:3, :] * branch
    resid_ref[...] = resid
    norm_ref[...] = (normalise(resid) * (1.0 + mod_ref[4:5, :]) + mod_ref[3:4, :]).astype(BF)


def temporal(n0, n1, n2, n3, weight, gain_ref, *out_refs):
    gap = jnp.zeros((128 - PATCH, D), BF)
    rows = jnp.concatenate([n0[...], gap, n1[...], gap, n2[...], gap, n3[...], gap], 0)
    proj = lax.dot_general(weight[...], rows, NT, preferred_element_type=F32)
    queries, keys, values = [], [], []
    for frame in range(4):
        here = slice(frame * 128, (frame + 1) * 128)
        heads = [proj[n * HD : (n + 1) * HD, here] for n in range(12)]
        queries.append([rms(v, gain_ref[:, 2:3]).astype(BF).astype(F32) for v in heads[:4]])
        keys.append([rms(v, gain_ref[:, 3:4]).astype(BF).astype(F32) for v in heads[4:8]])
        values.append([v.astype(BF).astype(F32) for v in heads[8:]])
    for f, out_ref in enumerate(out_refs):
        mixed = []
        for head in range(4):
            total, attended = 0.0, 0.0
            for g in range(4):
                score = jnp.sum(queries[f][head] * keys[g][head], 0, keepdims=True) * FACTOR
                expo = jnp.exp(score)
                total = total + expo
                attended = attended + expo.astype(BF).astype(F32) * values[g][head]
            mixed.append(attended / total)
        out_ref[...] = pack(jnp.concatenate(mixed, 0)[:, :PATCH], 3 * HD).astype(BF)


def temporal_end(place_ref, m0, m1, m2, m3, resid_ref, mod_ref, own, got, *refs):
    out_ref, feats = refs[-2:]
    for step, att_ref in enumerate((m0, m1, m2, m3)):
        here = pl.ds(pl.multiple_of((place_ref[1] ^ step) * (4 * HD), 4 * HD), 4 * HD)
        feats[here, :] = unpack(att_ref[...].astype(F32), HD)
    attended = feats[...].T.astype(BF)
    halves = [
        lax.dot_general(attended, w[...], NT, preferred_element_type=F32) for w in (own, got)
    ]
    branch = both_halves(place_ref[0] == 1, *halves)
    out_ref[...] = (resid_ref[...] + mod_ref[5:6, :] * branch).astype(BF)


def full(array, lead=None, n=0):
    block = array.shape if lead is None else (lead,) + array.shape[1:]
    place = (n,) + (0,) * (array.ndim - 1)
    return pl.BlockSpec(block, lambda i: place)


def once(kernel, args, specs, shapes, out_specs=None, aliases=None, scratch=(), grant=16):
    return pl.pallas_call(
        kernel,
        grid=(1,),
        in_specs=specs,
        out_specs=out_specs or [full(s) for s in shapes],
        out_shape=shapes,
        input_output_aliases=aliases or {},
        scratch_shapes=scratch,
        compiler_params=pltpu.CompilerParams(vmem_limit_bytes=grant * 1024 * 1024),
        cost_estimate=pl.CostEstimate(
            flops=2_000_000_000, bytes_accessed=8_000_000, transcendentals=0
        ),
        name=kernel.__name__,
    )(*args)


def shape(dtype, *sizes):
    return jax.ShapeDtypeStruct(sizes, dtype)


def per_device(tokens, modulation, spatial_qkv, spatial_out, temporal_qkv, temporal_out, norm_gains):
    core = lax.axis_index("c")
    frame = lax.axis_index("xl") * 2 + core
    place = jnp.stack([core, frame]).astype(jnp.int32)
    gains = norm_gains.T
    tok = tokens.reshape(ROWS, D)

    half = D // 2
    part_a = spatial_qkv.reshape(18, 3, NZ, 2 * HD).transpose(2, 0, 1, 3).reshape(NZ, 18, 6 * HD)
    part_a = jnp.pad(part_a, ((0, 0), (0, 0), (0, 512 - 6 * HD)))
    part_b = lax.dynamic_slice_in_dim(temporal_qkv.reshape(18, 3, D), frame * 4 * HD, 4 * HD, 2)
    rest = [
        jnp.where(core == 0, spatial_out[:, :half], spatial_out[:, half:]),
        part_b.reshape(18, 12 * HD),
        jnp.where(core == 0, temporal_out[:, :half], temporal_out[:, half:]),
    ]
    rest = jnp.pad(jnp.concatenate(rest, 1), ((0, 0), (0, 256 * NZ - D - 12 * HD)))
    rest = rest.reshape(18, NZ, 256).transpose(1, 0, 2)
    shard = jnp.concatenate([part_a, rest], 2)
    shard = lax.all_to_all(shard, "z", 0, 0, tiled=True).reshape(1, NZ * 18, 768)
    shard = jnp.broadcast_to(shard, (8, NZ * 18, 768))
    shard = lax.all_to_all(shard, ("xh", "y"), 0, 0, tiled=True).reshape(D, 768)

    column = lax.all_gather(tok, "z", axis=0)

    rest, column = lax.optimization_barrier((shard[:, 512:], column))
    rest = lax.all_gather(rest, "z", axis=0)

    y_place = lax.axis_index("y").astype(jnp.int32).reshape(1)
    slots = pl.pallas_call(
        spatial_proj,
        grid=(2,),
        in_specs=[
            SMEM,
            pl.BlockSpec((4, ROWS, D), lambda i: (i, 0, 0)),
            pl.BlockSpec((6, D), lambda i: (0, 0)),
            pl.BlockSpec((D, 512), lambda i: (0, 0)),
            pl.BlockSpec((HD, 4), lambda i: (0, 0)),
        ],
        out_specs=[pl.BlockSpec((1, 3 * HD + 8, 4 * PATCH), lambda i: (0, 0, i))] * NY,
        out_shape=[shape(BF, 1, 3 * HD + 8, PLANE)] * NY,
        scratch_shapes=[pltpu.VMEM((512, D), BF)],
        compiler_params=PARAMS,
        name="spatial_proj",
    )(y_place, column, modulation, shard, gains)

    swap = [(0, 1), (1, 0)]
    blocks = list(slots)
    for n in (1, 3, 2):
        blocks[n] = lax.ppermute(slots[n], "y", [(i, (i + n) % NY) for i in range(NY)])
    others = [lax.ppermute(block[:, : 2 * HD], "xh", swap) for block in blocks]
    part = attention(y_place, blocks, blocks, None, False)
    part = attention(y_place, blocks, [others[n] for n in (0, 1, 3)], part, False)
    attended = attention(y_place, blocks, [others[2]], part, True)
    attended = attended.reshape(NY * NZ, 56, 128)
    attended = lax.all_to_all(attended, ("y", "z"), 0, 0, tiled=True)
    attended = attended.reshape(4, NZ, 56, 128)
    shapes = [shape(BF, D, 640), shape(BF, 12 * HD, D), shape(BF, half, D)]
    out_a, turned, out_b = once(prepare, [rest], [full(rest)], shapes, grant=24)
    swapped, _ = lax.optimization_barrier((out_a, attended))
    got_a = lax.ppermute(swapped, "c", swap)

    steps = []
    for clip in range(2):
        args = [place, attended, tok, modulation, out_a, got_a]
        specs = [SMEM, full(attended, 2, clip), full(tok, PATCH, clip)]
        specs += [full(a) for a in args[3:]]
        steps.append(once(spatial_end, args, specs, [shape(F32, PATCH, D), shape(BF, PATCH, D)]))
    diagonal = [(0, 3), (3, 0), (1, 2), (2, 1)]
    sent = []
    moved = [lax.ppermute(norm, "xl", swap) for _, norm in steps]
    moved[0], _ = lax.optimization_barrier((moved[0], steps[1][1]))
    for (_, norm), norm_x in zip(steps, moved):
        if sent:
            norm_x, sent[0][0] = lax.optimization_barrier((norm_x, sent[0][0]))
        args = [norm, lax.ppermute(norm, "c", swap), norm_x, lax.ppermute(norm_x, "c", swap)]
        args += [turned, gains]
        mixed = once(temporal, args, [full(a) for a in args], [shape(BF, 3 * HD, 128)] * 4)
        if not sent:
            swapped, _ = lax.optimization_barrier((out_b, mixed[0]))
            got_b = lax.ppermute(swapped, "c", swap)
        sent.append(
            [
                mixed[0],
                lax.ppermute(mixed[1], "c", swap),
                lax.ppermute(mixed[2], "xl", swap),
                lax.ppermute(mixed[3], ("xl", "c"), diagonal),
            ]
        )
    result = None
    for clip in range(2):
        args = sent[clip] + [steps[clip][0], modulation, out_b, got_b]
        specs = [SMEM] + [full(a) for a in args]
        aliases = None
        if result is not None:
            args, specs = args + [result], specs + [pl.BlockSpec(memory_space=pl.ANY)]
            aliases = {len(args): 0}
        whole = shape(BF, ROWS, D)
        out_specs = [full(whole, PATCH, clip)]
        scratch = [pltpu.VMEM((D, PATCH), F32)]
        args = [place] + args
        (result,) = once(temporal_end, args, specs, [whole], out_specs, aliases, scratch)
    return result.reshape(2, 1, PATCH, D)


def solution(mesh):
    fine = Mesh(mesh.devices.reshape(2, 2, 2, NY, NZ), ("xl", "c", "xh", "y", "z"))
    time, space = ("xl", "c"), ("xh", "y", "z")
    block = P(None, time, space, None)
    rows = P(space, None)
    return jax.shard_map(
        per_device,
        mesh=fine,
        in_specs=(block, P(), rows, rows, rows, rows, P()),
        out_specs=block,
        check_vma=False,
    )
```

```python
import functools
import math

import jax
import jax.numpy as jnp
from jax import lax
from jax.experimental import pallas as pl
from jax.experimental.pallas import tpu as pltpu
from jax.sharding import Mesh
from jax.sharding import PartitionSpec as P

D = 1152
HEADS = 16
HD = 72
HP = 80
PATCH = 96
ROWS = 2 * PATCH
NZ, NY = 8, 4
PLANE = NZ * PATCH
BF = jnp.bfloat16
F32 = jnp.float32
FACTOR = 1.0 / math.sqrt(HD)
TN = (((0,), (0,)), ((), ()))
NT = (((1,), (1,)), ((), ()))
SMEM = pl.BlockSpec(memory_space=pltpu.SMEM)
PARAMS = pltpu.CompilerParams(vmem_limit_bytes=32 * 1024 * 1024)


def normalise(values):
    mean_val = jnp.mean(values, -1, keepdims=True)
    centred = values - mean_val
    variance = jnp.mean(centred * centred, -1, keepdims=True)
    return centred * lax.rsqrt(variance + 1e-06)


def rms(values, gain):
    mean_sq = jnp.mean(values * values, 0, keepdims=True)
    return values * lax.rsqrt(mean_sq + 1e-06) * gain


def spatial_proj(y_ref, tok_ref, mod_ref, w_ref, gain_ref, s0, s1, s2, s3, turned):
    cols = 4 * PATCH
    zeros = jnp.zeros((HP - HD, cols), F32)

    @pl.when(pl.program_id(0) == 0)
    def _():
        turned[...] = w_ref[...].astype(F32).T.astype(BF)

    clips = []
    for clip in range(2):
        tok = tok_ref[:, clip * PATCH : (clip + 1) * PATCH, :].reshape(cols, D).astype(F32)
        normed = normalise(tok) * (1.0 + mod_ref[1:2, :]) + mod_ref[0:1, :]
        clips.append(normed.astype(BF))
    normed = jnp.concatenate(clips, 0)
    both = lax.dot_general(turned[: 6 * HD], normed, NT, preferred_element_type=F32)
    for clip in range(2):
        proj = both[:, clip * cols : (clip + 1) * cols]
        for head in range(2):
            query, key, value = (
                proj[part * 2 * HD + head * HD : part * 2 * HD + (head + 1) * HD] for part in range(3)
            )
            query = rms(query, gain_ref[:, 0:1]) * (FACTOR * math.log2(math.e))
            key = rms(key, gain_ref[:, 1:2])
            place = clip * 2 + head
            parts = [key, value, query, zeros]
            block = jnp.concatenate(parts, 0).astype(BF)
            slot = (place + NY - y_ref[0]) % NY
            for n, out_ref in enumerate((s0, s1, s2, s3)):

                @pl.when(slot == n)
                def _(out_ref=out_ref, block=block):
                    out_ref[0] = block


def pack(block, rows):
    strips = [block[rows:, n * 32 : (n + 1) * 32] for n in range(3)]
    spare = rows - 3 * strips[0].shape[0]
    if spare:
        strips.append(jnp.zeros((spare, 32), block.dtype))
    return jnp.concatenate([block[:rows], jnp.concatenate(strips, 0)], 1)


def unpack(packed, tall):
    strips = [packed[n * tall : (n + 1) * tall, PATCH:] for n in range(3)]
    return jnp.concatenate([packed[:, :PATCH], jnp.concatenate(strips, 1)], 0)


def attend(count, resume, finish, y_ref, *refs):
    q_refs, kv_refs = refs[:NY], refs[NY : NY + count]
    out_ref, query, keys, values = refs[-4:]
    place = pl.program_id(0)

    @pl.when(place == 0)
    def _():
        gap = jnp.zeros((128 - HD, PLANE), F32)
        first = lax.broadcasted_iota(jnp.int32, (HP - HD, PLANE), 0) == 0
        ones = jnp.where(first, 1.0, 0.0)
        for n, kv_ref in enumerate(kv_refs):
            both = kv_ref[0, : 2 * HD].astype(F32)
            keys[n] = jnp.concatenate([both[:HD], gap], 0).T.astype(BF)
            values[n] = jnp.concatenate([both[HD:], ones], 0).astype(BF)
        query[HP:] = jnp.zeros((128 - HP, PLANE), BF)

    for n, q_ref in enumerate(q_refs):

        @pl.when(place == n)
        def _(q_ref=q_ref):
            query[:HP] = q_ref[0, 2 * HD :]

    parts = [(n, slice(p, p + 256)) for n in range(count) for p in range(0, PLANE, 256)]

    def scores(n, here):
        return jnp.dot(keys[n, here, :], query[...], preferred_element_type=F32)

    done = refs[NY + count][0] if resume else None
    ahead = scores(*parts[0])
    for index, (n, here) in enumerate(parts):
        score = ahead
        if index + 1 < len(parts):
            ahead = scores(*parts[index + 1])
        expo = jnp.exp2(score).astype(BF)
        add = jnp.dot(values[n, :, here], expo, preferred_element_type=F32)
        done = add if done is None else done + add
    if not finish:
        out_ref[0] = done
        return
    done = done[:HD] * (1.0 / done[HD : HD + 1])
    home = (y_ref[0] + NY - place) % NY
    for z in range(NZ):
        out_ref[home, z] = pack(done[:, z * PATCH : (z + 1) * PATCH], 56).astype(BF)


def attention(y_place, queries, key_values, part, finish):
    count = len(key_values)
    sums = pl.BlockSpec((1, HP, PLANE), lambda q: (q, 0, 0))
    args = [y_place, *queries, *key_values]
    in_specs = [SMEM] + [pl.BlockSpec(a.shape, lambda q: (0, 0, 0)) for a in args[1:]]
    if part is not None:
        in_specs.append(sums)
        args.append(part)
    if finish:
        out_spec = pl.BlockSpec((NY, NZ, 56, 128), lambda q: (0, 0, 0, 0))
        out_shape = shape(BF, NY, NZ, 56, 128)
    else:
        out_spec = sums
        out_shape = shape(F32, NY, HP, PLANE)
    pairs = count * NY * PLANE * PLANE
    return pl.pallas_call(
        functools.partial(attend, count, part is not None, finish),
        grid=(NY,),
        in_specs=in_specs,
        out_specs=out_spec,
        out_shape=out_shape,
        scratch_shapes=[
            pltpu.VMEM((128, PLANE), BF),
            pltpu.VMEM((count, PLANE, 128), BF),
            pltpu.VMEM((count, HP, PLANE), BF),
        ],
        compiler_params=PARAMS,
        cost_estimate=pl.CostEstimate(
            flops=4 * pairs, bytes_accessed=1_000_000, transcendentals=0
        ),
        name="attend",
    )(*args)


def prepare(rest, out_a, turned, out_b):
    half, last = D // 2, D // 2 + 12 * HD
    out_a[:, :256] = rest[0]
    out_a[:, 256:512] = rest[1]
    out_a[:, 512:] = rest[2, :, :128]
    for n in range(2, NZ):
        chunk = rest[n].astype(F32).T.astype(BF)
        low, high = n * 256, (n + 1) * 256
        for ref, begin, end in ((turned, half, last), (out_b, last, last + half)):
            first, stop = max(low, begin), min(high, end)
            if first < stop:
                ref[first - begin : stop - begin] = chunk[first - low : stop - low]


def both_halves(second, own, got):
    return jnp.where(second, jnp.concatenate([got, own], 1), jnp.concatenate([own, got], 1))


def spatial_end(place_ref, att_ref, tok_ref, mod_ref, own, got, resid_ref, norm_ref):
    feats = [unpack(att_ref[n % 2, n // 2].astype(F32), 16) for n in range(HEADS)]
    attended = jnp.concatenate(feats, 0).T.astype(BF)
    halves = [jnp.dot(attended, w[...], preferred_element_type=F32) for w in (own, got)]
    branch = both_halves(place_ref[0] == 1, *(h[:, : D // 2] for h in halves))
    resid = tok_ref[...].astype(F32) + mod_ref[2:3, :] * branch
    resid_ref[...] = resid
    norm_ref[...] = (normalise(resid) * (1.0 + mod_ref[4:5, :]) + mod_ref[3:4, :]).astype(BF)


def temporal(n0, n1, n2, n3, weight, gain_ref, *out_refs):
    gap = jnp.zeros((128 - PATCH, D), BF)
    rows = jnp.concatenate([n0[...], gap, n1[...], gap, n2[...], gap, n3[...], gap], 0)
    proj = lax.dot_general(weight[...], rows, NT, preferred_element_type=F32)
    queries, keys, values = [], [], []
    for frame in range(4):
        here = slice(frame * 128, (frame + 1) * 128)
        heads = [proj[n * HD : (n + 1) * HD, here] for n in range(12)]
        queries.append([rms(v, gain_ref[:, 2:3]).astype(BF).astype(F32) for v in heads[:4]])
        keys.append([rms(v, gain_ref[:, 3:4]).astype(BF).astype(F32) for v in heads[4:8]])
        values.append([v.astype(BF).astype(F32) for v in heads[8:]])
    for f, out_ref in enumerate(out_refs):
        mixed = []
        for head in range(4):
            total, attended = 0.0, 0.0
            for g in range(4):
                score = jnp.sum(queries[f][head] * keys[g][head], 0, keepdims=True) * FACTOR
                expo = jnp.exp(score)
                total = total + expo
                attended = attended + expo.astype(BF).astype(F32) * values[g][head]
            mixed.append(attended / total)
        out_ref[...] = pack(jnp.concatenate(mixed, 0)[:, :PATCH], 3 * HD).astype(BF)


def temporal_end(place_ref, m0, m1, m2, m3, resid_ref, mod_ref, own, got, *refs):
    out_ref, feats = refs[-2:]
    for step, att_ref in enumerate((m0, m1, m2, m3)):
        here = pl.ds(pl.multiple_of((place_ref[1] ^ step) * (4 * HD), 4 * HD), 4 * HD)
        feats[here, :] = unpack(att_ref[...].astype(F32), HD)
    attended = feats[...].T.astype(BF)
    halves = [
        lax.dot_general(attended, w[...], NT, preferred_element_type=F32) for w in (own, got)
    ]
    branch = both_halves(place_ref[0] == 1, *halves)
    out_ref[...] = (resid_ref[...] + mod_ref[5:6, :] * branch).astype(BF)


def full(array, lead=None, n=0):
    block = array.shape if lead is None else (lead,) + array.shape[1:]
    place = (n,) + (0,) * (array.ndim - 1)
    return pl.BlockSpec(block, lambda i: place)


def once(kernel, args, specs, shapes, out_specs=None, aliases=None, scratch=(), grant=16):
    return pl.pallas_call(
        kernel,
        grid=(1,),
        in_specs=specs,
        out_specs=out_specs or [full(s) for s in shapes],
        out_shape=shapes,
        input_output_aliases=aliases or {},
        scratch_shapes=scratch,
        compiler_params=pltpu.CompilerParams(vmem_limit_bytes=grant * 1024 * 1024),
        cost_estimate=pl.CostEstimate(
            flops=2_000_000_000, bytes_accessed=8_000_000, transcendentals=0
        ),
        name=kernel.__name__,
    )(*args)


def shape(dtype, *sizes):
    return jax.ShapeDtypeStruct(sizes, dtype)


def per_device(tokens, modulation, spatial_qkv, spatial_out, temporal_qkv, temporal_out, norm_gains):
    core = lax.axis_index("c")
    frame = lax.axis_index("xl") * 2 + core
    place = jnp.stack([core, frame]).astype(jnp.int32)
    gains = norm_gains.T
    tok = tokens.reshape(ROWS, D)

    half = D // 2
    part_a = spatial_qkv.reshape(18, 3, NZ, 2 * HD).transpose(2, 0, 1, 3).reshape(NZ, 18, 6 * HD)
    part_a = jnp.pad(part_a, ((0, 0), (0, 0), (0, 512 - 6 * HD)))
    part_b = lax.dynamic_slice_in_dim(temporal_qkv.reshape(18, 3, D), frame * 4 * HD, 4 * HD, 2)
    rest = [
        jnp.where(core == 0, spatial_out[:, :half], spatial_out[:, half:]),
        part_b.reshape(18, 12 * HD),
        jnp.where(core == 0, temporal_out[:, :half], temporal_out[:, half:]),
    ]
    rest = jnp.pad(jnp.concatenate(rest, 1), ((0, 0), (0, 256 * NZ - D - 12 * HD)))
    rest = rest.reshape(18, NZ, 256).transpose(1, 0, 2)
    shard = jnp.concatenate([part_a, rest], 2)
    shard = lax.all_to_all(shard, "z", 0, 0, tiled=True).reshape(1, NZ * 18, 768)
    shard = jnp.broadcast_to(shard, (8, NZ * 18, 768))
    shard = lax.all_to_all(shard, ("xh", "y"), 0, 0, tiled=True).reshape(D, 768)

    column = lax.all_gather(tok, "z", axis=0)

    rest, column = lax.optimization_barrier((shard[:, 512:], column))
    rest = lax.all_gather(rest, "z", axis=0)

    y_place = lax.axis_index("y").astype(jnp.int32).reshape(1)
    slots = pl.pallas_call(
        spatial_proj,
        grid=(2,),
        in_specs=[
            SMEM,
            pl.BlockSpec((4, ROWS, D), lambda i: (i, 0, 0)),
            pl.BlockSpec((6, D), lambda i: (0, 0)),
            pl.BlockSpec((D, 512), lambda i: (0, 0)),
            pl.BlockSpec((HD, 4), lambda i: (0, 0)),
        ],
        out_specs=[pl.BlockSpec((1, 3 * HD + 8, 4 * PATCH), lambda i: (0, 0, i))] * NY,
        out_shape=[shape(BF, 1, 3 * HD + 8, PLANE)] * NY,
        scratch_shapes=[pltpu.VMEM((512, D), BF)],
        compiler_params=pltpu.CompilerParams(vmem_limit_bytes=48 * 1024 * 1024),
        name="spatial_proj",
    )(y_place, column, modulation, shard, gains)

    swap = [(0, 1), (1, 0)]
    blocks = list(slots)
    for n in (1, 3, 2):
        blocks[n] = lax.ppermute(slots[n], "y", [(i, (i + n) % NY) for i in range(NY)])
    others = [lax.ppermute(block[:, : 2 * HD], "xh", swap) for block in blocks]
    part = attention(y_place, blocks, [blocks[n] for n in (0, 1, 3, 2)], None, False)
    attended = attention(y_place, blocks, [others[n] for n in (0, 1, 3, 2)], part, True)
    attended = attended.reshape(NY * NZ, 56, 128)
    attended = lax.all_to_all(attended, ("y", "z"), 0, 0, tiled=True)
    attended = attended.reshape(4, NZ, 56, 128)
    shapes = [shape(BF, D, 640), shape(BF, 12 * HD, D), shape(BF, half, D)]
    out_a, turned, out_b = once(prepare, [rest], [full(rest)], shapes, grant=24)
    swapped, _ = lax.optimization_barrier((out_a, attended))
    got_a = lax.ppermute(swapped, "c", swap)
    swapped, _ = lax.optimization_barrier((out_b, got_a))
    got_b = lax.ppermute(swapped, "c", swap)

    steps = []
    for clip in range(2):
        args = [place, attended, tok, modulation, out_a, got_a]
        specs = [SMEM, full(attended, 2, clip), full(tok, PATCH, clip)]
        specs += [full(a) for a in args[3:]]
        steps.append(once(spatial_end, args, specs, [shape(F32, PATCH, D), shape(BF, PATCH, D)]))
    diagonal = [(0, 3), (3, 0), (1, 2), (2, 1)]
    sent = []
    moved = [lax.ppermute(norm, "xl", swap) for _, norm in steps]
    moved[0], _ = lax.optimization_barrier((moved[0], steps[1][1]))
    for (_, norm), norm_x in zip(steps, moved):
        if sent:
            norm_x, sent[0][0] = lax.optimization_barrier((norm_x, sent[0][0]))
        args = [norm, lax.ppermute(norm, "c", swap), norm_x, lax.ppermute(norm_x, "c", swap)]
        args += [turned, gains]
        mixed = once(temporal, args, [full(a) for a in args], [shape(BF, 3 * HD, 128)] * 4)
        sent.append(
            [
                mixed[0],
                lax.ppermute(mixed[1], "c", swap),
                lax.ppermute(mixed[2], "xl", swap),
                lax.ppermute(mixed[3], ("xl", "c"), diagonal),
            ]
        )
    result = None
    for clip in range(2):
        args = sent[clip] + [steps[clip][0], modulation, out_b, got_b]
        specs = [SMEM] + [full(a) for a in args]
        aliases = None
        if result is not None:
            args, specs = args + [result], specs + [pl.BlockSpec(memory_space=pl.ANY)]
            aliases = {len(args): 0}
        whole = shape(BF, ROWS, D)
        out_specs = [full(whole, PATCH, clip)]
        scratch = [pltpu.VMEM((D, PATCH), F32)]
        args = [place] + args
        (result,) = once(temporal_end, args, specs, [whole], out_specs, aliases, scratch)
    return result.reshape(2, 1, PATCH, D)


def solution(mesh):
    fine = Mesh(mesh.devices.reshape(2, 2, 2, NY, NZ), ("xl", "c", "xh", "y", "z"))
    time, space = ("xl", "c"), ("xh", "y", "z")
    block = P(None, time, space, None)
    rows = P(space, None)
    return jax.shard_map(
        per_device,
        mesh=fine,
        in_specs=(block, P(), rows, rows, rows, rows, P()),
        out_specs=block,
        check_vma=False,
    )
```

```python
import functools
import math

import jax
import jax.numpy as jnp
from jax import lax
from jax.experimental import pallas as pl
from jax.experimental.pallas import tpu as pltpu
from jax.sharding import Mesh
from jax.sharding import PartitionSpec as P

D = 1152
HEADS = 16
HD = 72
HP = 80
PATCH = 96
ROWS = 2 * PATCH
NZ, NY = 8, 4
PLANE = NZ * PATCH
BF = jnp.bfloat16
F32 = jnp.float32
FACTOR = 1.0 / math.sqrt(HD)
TN = (((0,), (0,)), ((), ()))
NT = (((1,), (1,)), ((), ()))
SMEM = pl.BlockSpec(memory_space=pltpu.SMEM)
PARAMS = pltpu.CompilerParams(vmem_limit_bytes=32 * 1024 * 1024)


def normalise(values):
    mean_val = jnp.mean(values, -1, keepdims=True)
    centred = values - mean_val
    variance = jnp.mean(centred * centred, -1, keepdims=True)
    return centred * lax.rsqrt(variance + 1e-06)


def rms(values, gain):
    mean_sq = jnp.mean(values * values, 0, keepdims=True)
    return values * lax.rsqrt(mean_sq + 1e-06) * gain


def spatial_proj(y_ref, tok_ref, mod_ref, w_ref, gain_ref, s0, s1, s2, s3, turned):
    cols = 4 * PATCH
    zeros = jnp.zeros((HP - HD, cols), F32)

    @pl.when(pl.program_id(0) == 0)
    def _():
        turned[...] = w_ref[...].astype(F32).T.astype(BF)

    clips = []
    for clip in range(2):
        tok = tok_ref[:, clip * PATCH : (clip + 1) * PATCH, :].reshape(cols, D).astype(F32)
        normed = normalise(tok) * (1.0 + mod_ref[1:2, :]) + mod_ref[0:1, :]
        clips.append(normed.astype(BF))
    normed = jnp.concatenate(clips, 0)
    both = lax.dot_general(turned[: 6 * HD], normed, NT, preferred_element_type=F32)
    for clip in range(2):
        proj = both[:, clip * cols : (clip + 1) * cols]
        for head in range(2):
            query, key, value = (
                proj[part * 2 * HD + head * HD : part * 2 * HD + (head + 1) * HD] for part in range(3)
            )
            query = rms(query, gain_ref[:, 0:1]) * (FACTOR * math.log2(math.e))
            key = rms(key, gain_ref[:, 1:2])
            place = clip * 2 + head
            parts = [key, value, query, zeros]
            block = jnp.concatenate(parts, 0).astype(BF)
            slot = (place + NY - y_ref[0]) % NY
            for n, out_ref in enumerate((s0, s1, s2, s3)):

                @pl.when(slot == n)
                def _(out_ref=out_ref, block=block):
                    out_ref[0] = block


def pack(block, rows):
    strips = [block[rows:, n * 32 : (n + 1) * 32] for n in range(3)]
    spare = rows - 3 * strips[0].shape[0]
    if spare:
        strips.append(jnp.zeros((spare, 32), block.dtype))
    return jnp.concatenate([block[:rows], jnp.concatenate(strips, 0)], 1)


def unpack(packed, tall):
    strips = [packed[n * tall : (n + 1) * tall, PATCH:] for n in range(3)]
    return jnp.concatenate([packed[:, :PATCH], jnp.concatenate(strips, 1)], 0)


def attend(count, resume, finish, y_ref, *refs):
    q_refs, kv_refs = refs[:NY], refs[NY : NY + count]
    out_ref, query, keys, values = refs[-4:]
    place = pl.program_id(0)

    @pl.when(place == 0)
    def _():
        gap = jnp.zeros((128 - HD, PLANE), F32)
        first = lax.broadcasted_iota(jnp.int32, (HP - HD, PLANE), 0) == 0
        ones = jnp.where(first, 1.0, 0.0)
        for n, kv_ref in enumerate(kv_refs):
            both = kv_ref[0, : 2 * HD].astype(F32)
            keys[n] = jnp.concatenate([both[:HD], gap], 0).T.astype(BF)
            values[n] = jnp.concatenate([both[HD:], ones], 0).astype(BF)
        query[HP:] = jnp.zeros((128 - HP, PLANE), BF)

    for n, q_ref in enumerate(q_refs):

        @pl.when(place == n)
        def _(q_ref=q_ref):
            query[:HP] = q_ref[0, 2 * HD :]

    parts = [(n, slice(p, p + 256)) for n in range(count) for p in range(0, PLANE, 256)]

    def scores(n, here):
        return jnp.dot(keys[n, here, :], query[...], preferred_element_type=F32)

    done = refs[NY + count][0] if resume else None
    ahead = scores(*parts[0])
    for index, (n, here) in enumerate(parts):
        score = ahead
        if index + 1 < len(parts):
            ahead = scores(*parts[index + 1])
        expo = jnp.exp2(score).astype(BF)
        add = jnp.dot(values[n, :, here], expo, preferred_element_type=F32)
        done = add if done is None else done + add
    if not finish:
        out_ref[0] = done
        return
    done = done[:HD] * (1.0 / done[HD : HD + 1])
    home = (y_ref[0] + NY - place) % NY
    for z in range(NZ):
        out_ref[home, z] = pack(done[:, z * PATCH : (z + 1) * PATCH], 56).astype(BF)


def attention(y_place, queries, key_values, part, finish):
    count = len(key_values)
    sums = pl.BlockSpec((1, HP, PLANE), lambda q: (q, 0, 0))
    args = [y_place, *queries, *key_values]
    in_specs = [SMEM] + [pl.BlockSpec(a.shape, lambda q: (0, 0, 0)) for a in args[1:]]
    if part is not None:
        in_specs.append(sums)
        args.append(part)
    if finish:
        out_spec = pl.BlockSpec((NY, NZ, 56, 128), lambda q: (0, 0, 0, 0))
        out_shape = shape(BF, NY, NZ, 56, 128)
    else:
        out_spec = sums
        out_shape = shape(F32, NY, HP, PLANE)
    pairs = count * NY * PLANE * PLANE
    return pl.pallas_call(
        functools.partial(attend, count, part is not None, finish),
        grid=(NY,),
        in_specs=in_specs,
        out_specs=out_spec,
        out_shape=out_shape,
        scratch_shapes=[
            pltpu.VMEM((128, PLANE), BF),
            pltpu.VMEM((count, PLANE, 128), BF),
            pltpu.VMEM((count, HP, PLANE), BF),
        ],
        compiler_params=PARAMS,
        cost_estimate=pl.CostEstimate(
            flops=4 * pairs, bytes_accessed=1_000_000, transcendentals=0
        ),
        name="attend",
    )(*args)


def prepare(rest, out_a, turned, out_b):
    half, last = D // 2, D // 2 + 12 * HD
    out_a[:, :256] = rest[0]
    out_a[:, 256:512] = rest[1]
    out_a[:, 512:] = rest[2, :, :128]
    for n in range(2, NZ):
        chunk = rest[n].astype(F32).T.astype(BF)
        low, high = n * 256, (n + 1) * 256
        for ref, begin, end in ((turned, half, last), (out_b, last, last + half)):
            first, stop = max(low, begin), min(high, end)
            if first < stop:
                ref[first - begin : stop - begin] = chunk[first - low : stop - low]


def both_halves(second, own, got):
    return jnp.where(second, jnp.concatenate([got, own], 1), jnp.concatenate([own, got], 1))


def spatial_end(place_ref, att_ref, tok_ref, mod_ref, own, got, resid_ref, norm_ref):
    feats = [unpack(att_ref[n % 2, n // 2].astype(F32), 16) for n in range(HEADS)]
    attended = jnp.concatenate(feats, 0).T.astype(BF)
    halves = [jnp.dot(attended, w[...], preferred_element_type=F32) for w in (own, got)]
    branch = both_halves(place_ref[0] == 1, *(h[:, : D // 2] for h in halves))
    resid = tok_ref[...].astype(F32) + mod_ref[2:3, :] * branch
    resid_ref[...] = resid
    norm_ref[...] = (normalise(resid) * (1.0 + mod_ref[4:5, :]) + mod_ref[3:4, :]).astype(BF)


def temporal(n0, n1, n2, n3, weight, gain_ref, *out_refs):
    gap = jnp.zeros((128 - PATCH, D), BF)
    rows = jnp.concatenate([n0[...], gap, n1[...], gap, n2[...], gap, n3[...], gap], 0)
    proj = lax.dot_general(weight[...], rows, NT, preferred_element_type=F32)
    queries, keys, values = [], [], []
    for frame in range(4):
        here = slice(frame * 128, (frame + 1) * 128)
        heads = [proj[n * HD : (n + 1) * HD, here] for n in range(12)]
        queries.append([rms(v, gain_ref[:, 2:3]).astype(BF).astype(F32) for v in heads[:4]])
        keys.append([rms(v, gain_ref[:, 3:4]).astype(BF).astype(F32) for v in heads[4:8]])
        values.append([v.astype(BF).astype(F32) for v in heads[8:]])
    for f, out_ref in enumerate(out_refs):
        mixed = []
        for head in range(4):
            total, attended = 0.0, 0.0
            for g in range(4):
                score = jnp.sum(queries[f][head] * keys[g][head], 0, keepdims=True) * FACTOR
                expo = jnp.exp(score)
                total = total + expo
                attended = attended + expo.astype(BF).astype(F32) * values[g][head]
            mixed.append(attended / total)
        out_ref[...] = pack(jnp.concatenate(mixed, 0)[:, :PATCH], 3 * HD).astype(BF)


def temporal_end(place_ref, m0, m1, m2, m3, resid_ref, mod_ref, own, got, *refs):
    out_ref, feats = refs[-2:]
    for step, att_ref in enumerate((m0, m1, m2, m3)):
        here = pl.ds(pl.multiple_of((place_ref[1] ^ step) * (4 * HD), 4 * HD), 4 * HD)
        feats[here, :] = unpack(att_ref[...].astype(F32), HD)
    attended = feats[...].T.astype(BF)
    halves = [
        lax.dot_general(attended, w[...], NT, preferred_element_type=F32) for w in (own, got)
    ]
    branch = both_halves(place_ref[0] == 1, *halves)
    out_ref[...] = (resid_ref[...] + mod_ref[5:6, :] * branch).astype(BF)


def full(array, lead=None, n=0):
    block = array.shape if lead is None else (lead,) + array.shape[1:]
    place = (n,) + (0,) * (array.ndim - 1)
    return pl.BlockSpec(block, lambda i: place)


def once(kernel, args, specs, shapes, out_specs=None, aliases=None, scratch=(), grant=16):
    return pl.pallas_call(
        kernel,
        grid=(1,),
        in_specs=specs,
        out_specs=out_specs or [full(s) for s in shapes],
        out_shape=shapes,
        input_output_aliases=aliases or {},
        scratch_shapes=scratch,
        compiler_params=pltpu.CompilerParams(vmem_limit_bytes=grant * 1024 * 1024),
        cost_estimate=pl.CostEstimate(
            flops=2_000_000_000, bytes_accessed=8_000_000, transcendentals=0
        ),
        name=kernel.__name__,
    )(*args)


def shape(dtype, *sizes):
    return jax.ShapeDtypeStruct(sizes, dtype)


def per_device(tokens, modulation, spatial_qkv, spatial_out, temporal_qkv, temporal_out, norm_gains):
    core = lax.axis_index("c")
    frame = lax.axis_index("xl") * 2 + core
    place = jnp.stack([core, frame]).astype(jnp.int32)
    gains = norm_gains.T
    tok = tokens.reshape(ROWS, D)

    half = D // 2
    part_a = spatial_qkv.reshape(18, 3, NZ, 2 * HD).transpose(2, 0, 1, 3).reshape(NZ, 18, 6 * HD)
    part_a = jnp.pad(part_a, ((0, 0), (0, 0), (0, 512 - 6 * HD)))
    part_b = lax.dynamic_slice_in_dim(temporal_qkv.reshape(18, 3, D), frame * 4 * HD, 4 * HD, 2)
    rest = [
        jnp.where(core == 0, spatial_out[:, :half], spatial_out[:, half:]),
        part_b.reshape(18, 12 * HD),
        jnp.where(core == 0, temporal_out[:, :half], temporal_out[:, half:]),
    ]
    rest = jnp.pad(jnp.concatenate(rest, 1), ((0, 0), (0, 256 * NZ - D - 12 * HD)))
    rest = rest.reshape(18, NZ, 256).transpose(1, 0, 2)
    shard = jnp.concatenate([part_a, rest], 2)
    shard = lax.all_to_all(shard, "z", 0, 0, tiled=True).reshape(1, NZ * 18, 768)
    shard = jnp.broadcast_to(shard, (8, NZ * 18, 768))
    shard = lax.all_to_all(shard, ("xh", "y"), 0, 0, tiled=True).reshape(D, 768)

    column = lax.all_gather(tok, "z", axis=0)

    rest, column = lax.optimization_barrier((shard[:, 512:], column))
    rest = lax.all_gather(rest, "z", axis=0)

    y_place = lax.axis_index("y").astype(jnp.int32).reshape(1)
    slots = pl.pallas_call(
        spatial_proj,
        grid=(2,),
        in_specs=[
            SMEM,
            pl.BlockSpec((4, ROWS, D), lambda i: (i, 0, 0)),
            pl.BlockSpec((6, D), lambda i: (0, 0)),
            pl.BlockSpec((D, 512), lambda i: (0, 0)),
            pl.BlockSpec((HD, 4), lambda i: (0, 0)),
        ],
        out_specs=[pl.BlockSpec((1, 3 * HD + 8, 4 * PATCH), lambda i: (0, 0, i))] * NY,
        out_shape=[shape(BF, 1, 3 * HD + 8, PLANE)] * NY,
        scratch_shapes=[pltpu.VMEM((512, D), BF)],
        compiler_params=pltpu.CompilerParams(vmem_limit_bytes=48 * 1024 * 1024),
        name="spatial_proj",
    )(y_place, column, modulation, shard, gains)

    swap = [(0, 1), (1, 0)]
    blocks = list(slots)
    for n in (1, 3, 2):
        blocks[n] = lax.ppermute(slots[n], "y", [(i, (i + n) % NY) for i in range(NY)])
    others = [lax.ppermute(block[:, : 2 * HD], "xh", swap) for block in blocks]
    part = attention(y_place, blocks, [blocks[n] for n in (0, 1, 3, 2)], None, False)
    attended = attention(y_place, blocks, [others[n] for n in (0, 1, 3, 2)], part, True)
    attended = attended.reshape(NY * NZ, 56, 128)
    attended = lax.all_to_all(attended, ("y", "z"), 0, 0, tiled=True)
    attended = attended.reshape(4, NZ, 56, 128)
    shapes = [shape(BF, D, 640), shape(BF, 12 * HD, D), shape(BF, half, D)]
    out_a, turned, out_b = once(prepare, [rest], [full(rest)], shapes, grant=24)
    swapped, _ = lax.optimization_barrier((out_a, attended))
    got_a = lax.ppermute(swapped, "c", swap)
    swapped, _ = lax.optimization_barrier((out_b, got_a))
    got_b = lax.ppermute(swapped, "c", swap)

    steps = []
    for clip in range(2):
        args = [place, attended, tok, modulation, out_a, got_a]
        specs = [SMEM, full(attended, 2, clip), full(tok, PATCH, clip)]
        specs += [full(a) for a in args[3:]]
        steps.append(once(spatial_end, args, specs, [shape(F32, PATCH, D), shape(BF, PATCH, D)]))
    diagonal = [(0, 3), (3, 0), (1, 2), (2, 1)]
    sent = []
    moved = [lax.ppermute(norm, "xl", swap) for _, norm in steps]
    moved = lax.optimization_barrier(moved)
    for (_, norm), norm_x in zip(steps, moved):
        args = [norm, lax.ppermute(norm, "c", swap), norm_x, lax.ppermute(norm_x, "c", swap)]
        args += [turned, gains]
        mixed = once(temporal, args, [full(a) for a in args], [shape(BF, 3 * HD, 128)] * 4)
        sent.append(
            [
                mixed[0],
                lax.ppermute(mixed[1], "c", swap),
                lax.ppermute(mixed[2], "xl", swap),
                lax.ppermute(mixed[3], ("xl", "c"), diagonal),
            ]
        )
    result = None
    for clip in range(2):
        args = sent[clip] + [steps[clip][0], modulation, out_b, got_b]
        specs = [SMEM] + [full(a) for a in args]
        aliases = None
        if result is not None:
            args, specs = args + [result], specs + [pl.BlockSpec(memory_space=pl.ANY)]
            aliases = {len(args): 0}
        whole = shape(BF, ROWS, D)
        out_specs = [full(whole, PATCH, clip)]
        scratch = [pltpu.VMEM((D, PATCH), F32)]
        args = [place] + args
        (result,) = once(temporal_end, args, specs, [whole], out_specs, aliases, scratch)
    return result.reshape(2, 1, PATCH, D)


def solution(mesh):
    fine = Mesh(mesh.devices.reshape(2, 2, 2, NY, NZ), ("xl", "c", "xh", "y", "z"))
    time, space = ("xl", "c"), ("xh", "y", "z")
    block = P(None, time, space, None)
    rows = P(space, None)
    return jax.shard_map(
        per_device,
        mesh=fine,
        in_specs=(block, P(), rows, rows, rows, rows, P()),
        out_specs=block,
        check_vma=False,
    )
```

```python
import functools
import math

import jax
import jax.numpy as jnp
from jax import lax
from jax.experimental import pallas as pl
from jax.experimental.pallas import tpu as pltpu
from jax.sharding import Mesh
from jax.sharding import PartitionSpec as P

D = 1152
HEADS = 16
HD = 72
HP = 80
PATCH = 96
ROWS = 2 * PATCH
NZ, NY = 8, 4
PLANE = NZ * PATCH
BF = jnp.bfloat16
F32 = jnp.float32
FACTOR = 1.0 / math.sqrt(HD)
TN = (((0,), (0,)), ((), ()))
NT = (((1,), (1,)), ((), ()))
SMEM = pl.BlockSpec(memory_space=pltpu.SMEM)
PARAMS = pltpu.CompilerParams(vmem_limit_bytes=32 * 1024 * 1024)


def normalise(values):
    mean_val = jnp.mean(values, -1, keepdims=True)
    centred = values - mean_val
    variance = jnp.mean(centred * centred, -1, keepdims=True)
    return centred * lax.rsqrt(variance + 1e-06)


def rms(values, gain):
    mean_sq = jnp.mean(values * values, 0, keepdims=True)
    return values * lax.rsqrt(mean_sq + 1e-06) * gain


def spatial_proj(y_ref, tok_ref, mod_ref, w_ref, gain_ref, s0, s1, s2, s3, turned):
    cols = 4 * PATCH
    zeros = jnp.zeros((HP - HD, cols), F32)

    @pl.when(pl.program_id(0) == 0)
    def _():
        turned[...] = w_ref[...].astype(F32).T.astype(BF)

    clips = []
    for clip in range(2):
        tok = tok_ref[:, clip * PATCH : (clip + 1) * PATCH, :].reshape(cols, D).astype(F32)
        normed = normalise(tok) * (1.0 + mod_ref[1:2, :]) + mod_ref[0:1, :]
        clips.append(normed.astype(BF))
    normed = jnp.concatenate(clips, 0)
    both = lax.dot_general(turned[: 6 * HD], normed, NT, preferred_element_type=F32)
    for clip in range(2):
        proj = both[:, clip * cols : (clip + 1) * cols]
        for head in range(2):
            query, key, value = (
                proj[part * 2 * HD + head * HD : part * 2 * HD + (head + 1) * HD] for part in range(3)
            )
            query = rms(query, gain_ref[:, 0:1]) * (FACTOR * math.log2(math.e))
            key = rms(key, gain_ref[:, 1:2])
            place = clip * 2 + head
            parts = [key, value, query, zeros]
            block = jnp.concatenate(parts, 0).astype(BF)
            slot = (place + NY - y_ref[0]) % NY
            for n, out_ref in enumerate((s0, s1, s2, s3)):

                @pl.when(slot == n)
                def _(out_ref=out_ref, block=block):
                    out_ref[0] = block


def pack(block, rows):
    strips = [block[rows:, n * 32 : (n + 1) * 32] for n in range(3)]
    spare = rows - 3 * strips[0].shape[0]
    if spare:
        strips.append(jnp.zeros((spare, 32), block.dtype))
    return jnp.concatenate([block[:rows], jnp.concatenate(strips, 0)], 1)


def unpack(packed, tall):
    strips = [packed[n * tall : (n + 1) * tall, PATCH:] for n in range(3)]
    return jnp.concatenate([packed[:, :PATCH], jnp.concatenate(strips, 1)], 0)


def attend(count, resume, finish, y_ref, *refs):
    q_refs, kv_refs = refs[:NY], refs[NY : NY + count]
    out_ref, query, keys, values = refs[-4:]
    place = pl.program_id(0)

    @pl.when(place == 0)
    def _():
        gap = jnp.zeros((128 - HD, PLANE), F32)
        first = lax.broadcasted_iota(jnp.int32, (HP - HD, PLANE), 0) == 0
        ones = jnp.where(first, 1.0, 0.0)
        for n, kv_ref in enumerate(kv_refs):
            both = kv_ref[0, : 2 * HD].astype(F32)
            keys[n] = jnp.concatenate([both[:HD], gap], 0).T.astype(BF)
            values[n] = jnp.concatenate([both[HD:], ones], 0).astype(BF)
        query[HP:] = jnp.zeros((128 - HP, PLANE), BF)

    for n, q_ref in enumerate(q_refs):

        @pl.when(place == n)
        def _(q_ref=q_ref):
            query[:HP] = q_ref[0, 2 * HD :]

    parts = [(n, slice(p, p + 256)) for n in range(count) for p in range(0, PLANE, 256)]

    def scores(n, here):
        return jnp.dot(keys[n, here, :], query[...], preferred_element_type=F32)

    done = refs[NY + count][0] if resume else None
    ahead = scores(*parts[0])
    for index, (n, here) in enumerate(parts):
        score = ahead
        if index + 1 < len(parts):
            ahead = scores(*parts[index + 1])
        expo = jnp.exp2(score).astype(BF)
        add = jnp.dot(values[n, :, here], expo, preferred_element_type=F32)
        done = add if done is None else done + add
    if not finish:
        out_ref[0] = done
        return
    done = done[:HD] * (1.0 / done[HD : HD + 1])
    home = (y_ref[0] + NY - place) % NY
    for z in range(NZ):
        out_ref[home, z] = pack(done[:, z * PATCH : (z + 1) * PATCH], 56).astype(BF)


def attention(y_place, queries, key_values, part, finish):
    count = len(key_values)
    sums = pl.BlockSpec((1, HP, PLANE), lambda q: (q, 0, 0))
    args = [y_place, *queries, *key_values]
    in_specs = [SMEM] + [pl.BlockSpec(a.shape, lambda q: (0, 0, 0)) for a in args[1:]]
    if part is not None:
        in_specs.append(sums)
        args.append(part)
    if finish:
        out_spec = pl.BlockSpec((NY, NZ, 56, 128), lambda q: (0, 0, 0, 0))
        out_shape = shape(BF, NY, NZ, 56, 128)
    else:
        out_spec = sums
        out_shape = shape(F32, NY, HP, PLANE)
    pairs = count * NY * PLANE * PLANE
    return pl.pallas_call(
        functools.partial(attend, count, part is not None, finish),
        grid=(NY,),
        in_specs=in_specs,
        out_specs=out_spec,
        out_shape=out_shape,
        scratch_shapes=[
            pltpu.VMEM((128, PLANE), BF),
            pltpu.VMEM((count, PLANE, 128), BF),
            pltpu.VMEM((count, HP, PLANE), BF),
        ],
        compiler_params=PARAMS,
        cost_estimate=pl.CostEstimate(
            flops=4 * pairs, bytes_accessed=1_000_000, transcendentals=0
        ),
        name="attend",
    )(*args)


def prepare(rest, out_a, turned, out_b):
    half, last = D // 2, D // 2 + 12 * HD
    out_a[:, :256] = rest[0]
    out_a[:, 256:512] = rest[1]
    out_a[:, 512:] = rest[2, :, :128]
    for n in range(2, NZ):
        chunk = rest[n].astype(F32).T.astype(BF)
        low, high = n * 256, (n + 1) * 256
        for ref, begin, end in ((turned, half, last), (out_b, last, last + half)):
            first, stop = max(low, begin), min(high, end)
            if first < stop:
                ref[first - begin : stop - begin] = chunk[first - low : stop - low]


def both_halves(second, own, got):
    return jnp.where(second, jnp.concatenate([got, own], 1), jnp.concatenate([own, got], 1))


def spatial_end(place_ref, att_ref, tok_ref, mod_ref, own, got, resid_ref, norm_ref):
    feats = [unpack(att_ref[n % 2, n // 2].astype(F32), 16) for n in range(HEADS)]
    attended = jnp.concatenate(feats, 0).T.astype(BF)
    halves = [jnp.dot(attended, w[...], preferred_element_type=F32) for w in (own, got)]
    branch = both_halves(place_ref[0] == 1, *(h[:, : D // 2] for h in halves))
    resid = tok_ref[...].astype(F32) + mod_ref[2:3, :] * branch
    resid_ref[...] = resid
    norm_ref[...] = (normalise(resid) * (1.0 + mod_ref[4:5, :]) + mod_ref[3:4, :]).astype(BF)


def temporal(n0, n1, n2, n3, weight, gain_ref, *out_refs):
    gap = jnp.zeros((128 - PATCH, D), BF)
    rows = jnp.concatenate([n0[...], gap, n1[...], gap, n2[...], gap, n3[...], gap], 0)
    proj = lax.dot_general(weight[...], rows, NT, preferred_element_type=F32)
    queries, keys, values = [], [], []
    for frame in range(4):
        here = slice(frame * 128, (frame + 1) * 128)
        heads = [proj[n * HD : (n + 1) * HD, here] for n in range(12)]
        queries.append([rms(v, gain_ref[:, 2:3]).astype(BF).astype(F32) for v in heads[:4]])
        keys.append([rms(v, gain_ref[:, 3:4]).astype(BF).astype(F32) for v in heads[4:8]])
        values.append([v.astype(BF).astype(F32) for v in heads[8:]])
    for f, out_ref in enumerate(out_refs):
        mixed = []
        for head in range(4):
            total, attended = 0.0, 0.0
            for g in range(4):
                score = jnp.sum(queries[f][head] * keys[g][head], 0, keepdims=True) * FACTOR
                expo = jnp.exp(score)
                total = total + expo
                attended = attended + expo.astype(BF).astype(F32) * values[g][head]
            mixed.append(attended / total)
        out_ref[...] = pack(jnp.concatenate(mixed, 0)[:, :PATCH], 3 * HD).astype(BF)


def temporal_end(place_ref, m0, m1, m2, m3, resid_ref, mod_ref, own, got, *refs):
    out_ref, feats = refs[-2:]
    for step, att_ref in enumerate((m0, m1, m2, m3)):
        here = pl.ds(pl.multiple_of((place_ref[1] ^ step) * (4 * HD), 4 * HD), 4 * HD)
        feats[here, :] = unpack(att_ref[...].astype(F32), HD)
    attended = feats[...].T.astype(BF)
    halves = [
        lax.dot_general(attended, w[...], NT, preferred_element_type=F32) for w in (own, got)
    ]
    branch = both_halves(place_ref[0] == 1, *halves)
    out_ref[...] = (resid_ref[...] + mod_ref[5:6, :] * branch).astype(BF)


def full(array, lead=None, n=0):
    block = array.shape if lead is None else (lead,) + array.shape[1:]
    place = (n,) + (0,) * (array.ndim - 1)
    return pl.BlockSpec(block, lambda i: place)


def once(kernel, args, specs, shapes, out_specs=None, aliases=None, scratch=(), grant=16):
    return pl.pallas_call(
        kernel,
        grid=(1,),
        in_specs=specs,
        out_specs=out_specs or [full(s) for s in shapes],
        out_shape=shapes,
        input_output_aliases=aliases or {},
        scratch_shapes=scratch,
        compiler_params=pltpu.CompilerParams(vmem_limit_bytes=grant * 1024 * 1024),
        cost_estimate=pl.CostEstimate(
            flops=2_000_000_000, bytes_accessed=8_000_000, transcendentals=0
        ),
        name=kernel.__name__,
    )(*args)


def shape(dtype, *sizes):
    return jax.ShapeDtypeStruct(sizes, dtype)


def per_device(tokens, modulation, spatial_qkv, spatial_out, temporal_qkv, temporal_out, norm_gains):
    core = lax.axis_index("c")
    frame = lax.axis_index("xl") * 2 + core
    place = jnp.stack([core, frame]).astype(jnp.int32)
    gains = norm_gains.T
    tok = tokens.reshape(ROWS, D)

    half = D // 2
    part_a = spatial_qkv.reshape(18, 3, NZ, 2 * HD).transpose(2, 0, 1, 3).reshape(NZ, 18, 6 * HD)
    part_a = jnp.pad(part_a, ((0, 0), (0, 0), (0, 512 - 6 * HD)))
    part_b = lax.dynamic_slice_in_dim(temporal_qkv.reshape(18, 3, D), frame * 4 * HD, 4 * HD, 2)
    rest = [
        jnp.where(core == 0, spatial_out[:, :half], spatial_out[:, half:]),
        part_b.reshape(18, 12 * HD),
        jnp.where(core == 0, temporal_out[:, :half], temporal_out[:, half:]),
    ]
    rest = jnp.pad(jnp.concatenate(rest, 1), ((0, 0), (0, 256 * NZ - D - 12 * HD)))
    rest = rest.reshape(18, NZ, 256).transpose(1, 0, 2)
    shard = jnp.concatenate([part_a, rest], 2)
    shard = lax.all_to_all(shard, "z", 0, 0, tiled=True).reshape(1, NZ * 18, 768)
    shard = jnp.broadcast_to(shard, (8, NZ * 18, 768))
    shard = lax.all_to_all(shard, ("xh", "y"), 0, 0, tiled=True).reshape(D, 768)

    column = lax.all_gather(tok, "z", axis=0)

    rest, column = lax.optimization_barrier((shard[:, 512:], column))
    rest = lax.all_gather(rest, "z", axis=0)

    y_place = lax.axis_index("y").astype(jnp.int32).reshape(1)
    slots = pl.pallas_call(
        spatial_proj,
        grid=(2,),
        in_specs=[
            SMEM,
            pl.BlockSpec((4, ROWS, D), lambda i: (i, 0, 0)),
            pl.BlockSpec((6, D), lambda i: (0, 0)),
            pl.BlockSpec((D, 512), lambda i: (0, 0)),
            pl.BlockSpec((HD, 4), lambda i: (0, 0)),
        ],
        out_specs=[pl.BlockSpec((1, 3 * HD + 8, 4 * PATCH), lambda i: (0, 0, i))] * NY,
        out_shape=[shape(BF, 1, 3 * HD + 8, PLANE)] * NY,
        scratch_shapes=[pltpu.VMEM((512, D), BF)],
        compiler_params=pltpu.CompilerParams(vmem_limit_bytes=48 * 1024 * 1024),
        name="spatial_proj",
    )(y_place, column, modulation, shard, gains)

    swap = [(0, 1), (1, 0)]
    blocks = list(slots)
    for n in (1, 3, 2):
        blocks[n] = lax.ppermute(slots[n], "y", [(i, (i + n) % NY) for i in range(NY)])
    others = [lax.ppermute(block[:, : 2 * HD], "xh", swap) for block in blocks]
    part = attention(y_place, blocks, [blocks[n] for n in (0, 1, 3, 2)], None, False)
    attended = attention(y_place, blocks, [others[n] for n in (0, 1, 3, 2)], part, True)
    attended = attended.reshape(NY * NZ, 56, 128)
    attended = lax.all_to_all(attended, ("y", "z"), 0, 0, tiled=True)
    attended = attended.reshape(4, NZ, 56, 128)
    shapes = [shape(BF, D, 640), shape(BF, 12 * HD, D), shape(BF, half, D)]
    out_a, turned, out_b = once(prepare, [rest], [full(rest)], shapes, grant=24)
    swapped, _ = lax.optimization_barrier((out_a, attended))
    got_a = lax.ppermute(swapped, "c", swap)
    swapped, _ = lax.optimization_barrier((out_b, got_a))
    got_b = lax.ppermute(swapped, "c", swap)

    steps = []
    for clip in range(2):
        args = [place, attended, tok, modulation, out_a, got_a]
        specs = [SMEM, full(attended, 2, clip), full(tok, PATCH, clip)]
        specs += [full(a) for a in args[3:]]
        steps.append(once(spatial_end, args, specs, [shape(F32, PATCH, D), shape(BF, PATCH, D)]))
    diagonal = [(0, 3), (3, 0), (1, 2), (2, 1)]
    sent = []
    moved = [lax.ppermute(norm, "xl", swap) for _, norm in steps]
    moved = lax.optimization_barrier(moved)
    for (_, norm), norm_x in zip(steps, moved):
        args = [norm, lax.ppermute(norm, "c", swap), norm_x, lax.ppermute(norm_x, "c", swap)]
        args += [turned, gains]
        sent.append(once(temporal, args, [full(a) for a in args], [shape(BF, 3 * HD, 128)] * 4))
    sent[0], _ = lax.optimization_barrier((sent[0], sent[1][0]))
    sent = [
        [
            mixed[0],
            lax.ppermute(mixed[1], "c", swap),
            lax.ppermute(mixed[2], "xl", swap),
            lax.ppermute(mixed[3], ("xl", "c"), diagonal),
        ]
        for mixed in sent
    ]
    result = None
    for clip in range(2):
        args = sent[clip] + [steps[clip][0], modulation, out_b, got_b]
        specs = [SMEM] + [full(a) for a in args]
        aliases = None
        if result is not None:
            args, specs = args + [result], specs + [pl.BlockSpec(memory_space=pl.ANY)]
            aliases = {len(args): 0}
        whole = shape(BF, ROWS, D)
        out_specs = [full(whole, PATCH, clip)]
        scratch = [pltpu.VMEM((D, PATCH), F32)]
        args = [place] + args
        (result,) = once(temporal_end, args, specs, [whole], out_specs, aliases, scratch)
    return result.reshape(2, 1, PATCH, D)


def solution(mesh):
    fine = Mesh(mesh.devices.reshape(2, 2, 2, NY, NZ), ("xl", "c", "xh", "y", "z"))
    time, space = ("xl", "c"), ("xh", "y", "z")
    block = P(None, time, space, None)
    rows = P(space, None)
    return jax.shard_map(
        per_device,
        mesh=fine,
        in_specs=(block, P(), rows, rows, rows, rows, P()),
        out_specs=block,
        check_vma=False,
    )
```

```python
import functools
import math

import jax
import jax.numpy as jnp
from jax import lax
from jax.experimental import pallas as pl
from jax.experimental.pallas import tpu as pltpu
from jax.sharding import Mesh
from jax.sharding import PartitionSpec as P

D = 1152
HEADS = 16
HD = 72
HP = 80
PATCH = 96
ROWS = 2 * PATCH
NZ, NY = 8, 4
PLANE = NZ * PATCH
BF = jnp.bfloat16
F32 = jnp.float32
FACTOR = 1.0 / math.sqrt(HD)
TN = (((0,), (0,)), ((), ()))
NT = (((1,), (1,)), ((), ()))
SMEM = pl.BlockSpec(memory_space=pltpu.SMEM)
PARAMS = pltpu.CompilerParams(vmem_limit_bytes=32 * 1024 * 1024)


def normalise(values):
    mean_val = jnp.mean(values, -1, keepdims=True)
    centred = values - mean_val
    variance = jnp.mean(centred * centred, -1, keepdims=True)
    return centred * lax.rsqrt(variance + 1e-06)


def rms(values, gain):
    mean_sq = jnp.mean(values * values, 0, keepdims=True)
    return values * lax.rsqrt(mean_sq + 1e-06) * gain


def spatial_proj(y_ref, tok_ref, mod_ref, w_ref, gain_ref, s0, s1, s2, s3, turned):
    cols = 4 * PATCH
    zeros = jnp.zeros((HP - HD, cols), F32)

    @pl.when(pl.program_id(0) == 0)
    def _():
        turned[...] = w_ref[...].astype(F32).T.astype(BF)

    clips = []
    for clip in range(2):
        tok = tok_ref[:, clip * PATCH : (clip + 1) * PATCH, :].reshape(cols, D).astype(F32)
        normed = normalise(tok) * (1.0 + mod_ref[1:2, :]) + mod_ref[0:1, :]
        clips.append(normed.astype(BF))
    normed = jnp.concatenate(clips, 0)
    both = lax.dot_general(turned[: 6 * HD], normed, NT, preferred_element_type=F32)
    for clip in range(2):
        proj = both[:, clip * cols : (clip + 1) * cols]
        for head in range(2):
            query, key, value = (
                proj[part * 2 * HD + head * HD : part * 2 * HD + (head + 1) * HD] for part in range(3)
            )
            query = rms(query, gain_ref[:, 0:1]) * (FACTOR * math.log2(math.e))
            key = rms(key, gain_ref[:, 1:2])
            place = clip * 2 + head
            parts = [key, value, query, zeros]
            block = jnp.concatenate(parts, 0).astype(BF)
            slot = (place + NY - y_ref[0]) % NY
            for n, out_ref in enumerate((s0, s1, s2, s3)):

                @pl.when(slot == n)
                def _(out_ref=out_ref, block=block):
                    out_ref[0] = block


def pack(block, rows):
    strips = [block[rows:, n * 32 : (n + 1) * 32] for n in range(3)]
    spare = rows - 3 * strips[0].shape[0]
    if spare:
        strips.append(jnp.zeros((spare, 32), block.dtype))
    return jnp.concatenate([block[:rows], jnp.concatenate(strips, 0)], 1)


def unpack(packed, tall):
    strips = [packed[n * tall : (n + 1) * tall, PATCH:] for n in range(3)]
    return jnp.concatenate([packed[:, :PATCH], jnp.concatenate(strips, 1)], 0)


def attend(count, resume, finish, y_ref, *refs):
    q_refs, kv_refs = refs[:NY], refs[NY : NY + count]
    out_ref, query, keys, values = refs[-4:]
    place = pl.program_id(0)

    @pl.when(place == 0)
    def _():
        gap = jnp.zeros((128 - HD, PLANE), F32)
        first = lax.broadcasted_iota(jnp.int32, (HP - HD, PLANE), 0) == 0
        ones = jnp.where(first, 1.0, 0.0)
        for n, kv_ref in enumerate(kv_refs):
            both = kv_ref[0, : 2 * HD].astype(F32)
            keys[n] = jnp.concatenate([both[:HD], gap], 0).T.astype(BF)
            values[n] = jnp.concatenate([both[HD:], ones], 0).astype(BF)
        query[HP:] = jnp.zeros((128 - HP, PLANE), BF)

    for n, q_ref in enumerate(q_refs):

        @pl.when(place == n)
        def _(q_ref=q_ref):
            query[:HP] = q_ref[0, 2 * HD :]

    parts = [(n, slice(p, p + 256)) for n in range(count) for p in range(0, PLANE, 256)]

    def scores(n, here):
        return jnp.dot(keys[n, here, :], query[...], preferred_element_type=F32)

    done = refs[NY + count][0] if resume else None
    ahead = scores(*parts[0])
    for index, (n, here) in enumerate(parts):
        score = ahead
        if index + 1 < len(parts):
            ahead = scores(*parts[index + 1])
        expo = jnp.exp2(score).astype(BF)
        add = jnp.dot(values[n, :, here], expo, preferred_element_type=F32)
        done = add if done is None else done + add
    if not finish:
        out_ref[0] = done
        return
    done = done[:HD] * (1.0 / done[HD : HD + 1])
    home = (y_ref[0] + NY - place) % NY
    for z in range(NZ):
        out_ref[home, z] = pack(done[:, z * PATCH : (z + 1) * PATCH], 56).astype(BF)


def attention(y_place, queries, key_values, part, finish):
    count = len(key_values)
    sums = pl.BlockSpec((1, HP, PLANE), lambda q: (q, 0, 0))
    args = [y_place, *queries, *key_values]
    in_specs = [SMEM] + [pl.BlockSpec(a.shape, lambda q: (0, 0, 0)) for a in args[1:]]
    if part is not None:
        in_specs.append(sums)
        args.append(part)
    if finish:
        out_spec = pl.BlockSpec((NY, NZ, 56, 128), lambda q: (0, 0, 0, 0))
        out_shape = shape(BF, NY, NZ, 56, 128)
    else:
        out_spec = sums
        out_shape = shape(F32, NY, HP, PLANE)
    pairs = count * NY * PLANE * PLANE
    return pl.pallas_call(
        functools.partial(attend, count, part is not None, finish),
        grid=(NY,),
        in_specs=in_specs,
        out_specs=out_spec,
        out_shape=out_shape,
        scratch_shapes=[
            pltpu.VMEM((128, PLANE), BF),
            pltpu.VMEM((count, PLANE, 128), BF),
            pltpu.VMEM((count, HP, PLANE), BF),
        ],
        compiler_params=PARAMS,
        cost_estimate=pl.CostEstimate(
            flops=4 * pairs, bytes_accessed=1_000_000, transcendentals=0
        ),
        name="attend",
    )(*args)


def prepare(rest, out_a, turned, out_b):
    half, last = D // 2, D // 2 + 12 * HD
    out_a[:, :256] = rest[0]
    out_a[:, 256:512] = rest[1]
    out_a[:, 512:] = rest[2, :, :128]
    for n in range(2, NZ):
        chunk = rest[n].astype(F32).T.astype(BF)
        low, high = n * 256, (n + 1) * 256
        for ref, begin, end in ((turned, half, last), (out_b, last, last + half)):
            first, stop = max(low, begin), min(high, end)
            if first < stop:
                ref[first - begin : stop - begin] = chunk[first - low : stop - low]


def both_halves(second, own, got):
    return jnp.where(second, jnp.concatenate([got, own], 1), jnp.concatenate([own, got], 1))


def spatial_end(place_ref, att_ref, tok_ref, mod_ref, own, got, resid_ref, norm_ref):
    feats = [unpack(att_ref[n % 2, n // 2].astype(F32), 16) for n in range(HEADS)]
    attended = jnp.concatenate(feats, 0).T.astype(BF)
    halves = [jnp.dot(attended, w[...], preferred_element_type=F32) for w in (own, got)]
    branch = both_halves(place_ref[0] == 1, *(h[:, : D // 2] for h in halves))
    resid = tok_ref[...].astype(F32) + mod_ref[2:3, :] * branch
    resid_ref[...] = resid
    norm_ref[...] = (normalise(resid) * (1.0 + mod_ref[4:5, :]) + mod_ref[3:4, :]).astype(BF)


def temporal(n0, n1, n2, n3, weight, gain_ref, *out_refs):
    gap = jnp.zeros((128 - PATCH, D), BF)
    rows = jnp.concatenate([n0[...], gap, n1[...], gap, n2[...], gap, n3[...], gap], 0)
    proj = lax.dot_general(weight[...], rows, NT, preferred_element_type=F32)
    queries, keys, values = [], [], []
    for frame in range(4):
        here = slice(frame * 128, (frame + 1) * 128)
        heads = [proj[n * HD : (n + 1) * HD, here] for n in range(12)]
        queries.append([rms(v, gain_ref[:, 2:3]).astype(BF).astype(F32) for v in heads[:4]])
        keys.append([rms(v, gain_ref[:, 3:4]).astype(BF).astype(F32) for v in heads[4:8]])
        values.append([v.astype(BF).astype(F32) for v in heads[8:]])
    for f, out_ref in enumerate(out_refs):
        mixed = []
        for head in range(4):
            total, attended = 0.0, 0.0
            for g in range(4):
                score = jnp.sum(queries[f][head] * keys[g][head], 0, keepdims=True) * FACTOR
                expo = jnp.exp(score)
                total = total + expo
                attended = attended + expo.astype(BF).astype(F32) * values[g][head]
            mixed.append(attended / total)
        out_ref[...] = pack(jnp.concatenate(mixed, 0)[:, :PATCH], 3 * HD).astype(BF)


def temporal_end(place_ref, m0, m1, m2, m3, resid_ref, mod_ref, own, got, *refs):
    out_ref, feats = refs[-2:]
    for step, att_ref in enumerate((m0, m1, m2, m3)):
        here = pl.ds(pl.multiple_of((place_ref[1] ^ step) * (4 * HD), 4 * HD), 4 * HD)
        feats[here, :] = unpack(att_ref[...].astype(F32), HD)
    attended = feats[...].T.astype(BF)
    halves = [
        lax.dot_general(attended, w[...], NT, preferred_element_type=F32) for w in (own, got)
    ]
    branch = both_halves(place_ref[0] == 1, *halves)
    out_ref[...] = (resid_ref[...] + mod_ref[5:6, :] * branch).astype(BF)


def full(array, lead=None, n=0):
    block = array.shape if lead is None else (lead,) + array.shape[1:]
    place = (n,) + (0,) * (array.ndim - 1)
    return pl.BlockSpec(block, lambda i: place)


def once(kernel, args, specs, shapes, out_specs=None, aliases=None, scratch=(), grant=16):
    return pl.pallas_call(
        kernel,
        grid=(1,),
        in_specs=specs,
        out_specs=out_specs or [full(s) for s in shapes],
        out_shape=shapes,
        input_output_aliases=aliases or {},
        scratch_shapes=scratch,
        compiler_params=pltpu.CompilerParams(vmem_limit_bytes=grant * 1024 * 1024),
        cost_estimate=pl.CostEstimate(
            flops=2_000_000_000, bytes_accessed=8_000_000, transcendentals=0
        ),
        name=kernel.__name__,
    )(*args)


def shape(dtype, *sizes):
    return jax.ShapeDtypeStruct(sizes, dtype)


def per_device(tokens, modulation, spatial_qkv, spatial_out, temporal_qkv, temporal_out, norm_gains):
    core = lax.axis_index("c")
    frame = lax.axis_index("xl") * 2 + core
    place = jnp.stack([core, frame]).astype(jnp.int32)
    gains = norm_gains.T
    tok = tokens.reshape(ROWS, D)

    half = D // 2
    part_a = spatial_qkv.reshape(18, 3, NZ, 2 * HD).transpose(2, 0, 1, 3).reshape(NZ, 18, 6 * HD)
    part_a = jnp.pad(part_a, ((0, 0), (0, 0), (0, 512 - 6 * HD)))
    part_b = lax.dynamic_slice_in_dim(temporal_qkv.reshape(18, 3, D), frame * 4 * HD, 4 * HD, 2)
    rest = [
        jnp.where(core == 0, spatial_out[:, :half], spatial_out[:, half:]),
        part_b.reshape(18, 12 * HD),
        jnp.where(core == 0, temporal_out[:, :half], temporal_out[:, half:]),
    ]
    rest = jnp.pad(jnp.concatenate(rest, 1), ((0, 0), (0, 256 * NZ - D - 12 * HD)))
    rest = rest.reshape(18, NZ, 256).transpose(1, 0, 2)
    shard = jnp.concatenate([part_a, rest], 2)
    shard = lax.all_to_all(shard, "z", 0, 0, tiled=True).reshape(1, NZ * 18, 768)
    shard = jnp.broadcast_to(shard, (8, NZ * 18, 768))
    shard = lax.all_to_all(shard, ("xh", "y"), 0, 0, tiled=True).reshape(D, 768)

    column = lax.all_gather(tok, "z", axis=0)

    rest, column = lax.optimization_barrier((shard[:, 512:], column))
    rest = lax.all_gather(rest, "z", axis=0)

    y_place = lax.axis_index("y").astype(jnp.int32).reshape(1)
    slots = pl.pallas_call(
        spatial_proj,
        grid=(2,),
        in_specs=[
            SMEM,
            pl.BlockSpec((4, ROWS, D), lambda i: (i, 0, 0)),
            pl.BlockSpec((6, D), lambda i: (0, 0)),
            pl.BlockSpec((D, 512), lambda i: (0, 0)),
            pl.BlockSpec((HD, 4), lambda i: (0, 0)),
        ],
        out_specs=[pl.BlockSpec((1, 3 * HD + 8, 4 * PATCH), lambda i: (0, 0, i))] * NY,
        out_shape=[shape(BF, 1, 3 * HD + 8, PLANE)] * NY,
        scratch_shapes=[pltpu.VMEM((512, D), BF)],
        compiler_params=pltpu.CompilerParams(vmem_limit_bytes=48 * 1024 * 1024),
        name="spatial_proj",
    )(y_place, column, modulation, shard, gains)

    swap = [(0, 1), (1, 0)]
    blocks = list(slots)
    for n in (1, 3, 2):
        blocks[n] = lax.ppermute(slots[n], "y", [(i, (i + n) % NY) for i in range(NY)])
    others = [lax.ppermute(block[:, : 2 * HD], "xh", swap) for block in blocks]
    part = attention(y_place, blocks, [blocks[n] for n in (0, 1, 3, 2)], None, False)
    attended = attention(y_place, blocks, [others[n] for n in (0, 1, 3, 2)], part, True)
    attended = attended.reshape(NY * NZ, 56, 128)
    attended = lax.all_to_all(attended, ("y", "z"), 0, 0, tiled=True)
    attended = attended.reshape(4, NZ, 56, 128)
    shapes = [shape(BF, D, 640), shape(BF, 12 * HD, D), shape(BF, half, D)]
    out_a, turned, out_b = once(prepare, [rest], [full(rest)], shapes, grant=44)
    swapped, _ = lax.optimization_barrier((out_a, attended))
    got_a = lax.ppermute(swapped, "c", swap)
    swapped, _ = lax.optimization_barrier((out_b, got_a))
    got_b = lax.ppermute(swapped, "c", swap)

    steps = []
    for clip in range(2):
        args = [place, attended, tok, modulation, out_a, got_a]
        specs = [SMEM, full(attended, 2, clip), full(tok, PATCH, clip)]
        specs += [full(a) for a in args[3:]]
        steps.append(once(spatial_end, args, specs, [shape(F32, PATCH, D), shape(BF, PATCH, D)]))
    diagonal = [(0, 3), (3, 0), (1, 2), (2, 1)]
    sent = []
    moved = [lax.ppermute(norm, "xl", swap) for _, norm in steps]
    moved = lax.optimization_barrier(moved)
    for (_, norm), norm_x in zip(steps, moved):
        args = [norm, lax.ppermute(norm, "c", swap), norm_x, lax.ppermute(norm_x, "c", swap)]
        args += [turned, gains]
        sent.append(once(temporal, args, [full(a) for a in args], [shape(BF, 3 * HD, 128)] * 4))
    sent[0], _ = lax.optimization_barrier((sent[0], sent[1][0]))
    sent = [
        [
            mixed[0],
            lax.ppermute(mixed[1], "c", swap),
            lax.ppermute(mixed[2], "xl", swap),
            lax.ppermute(mixed[3], ("xl", "c"), diagonal),
        ]
        for mixed in sent
    ]
    result = None
    for clip in range(2):
        args = sent[clip] + [steps[clip][0], modulation, out_b, got_b]
        specs = [SMEM] + [full(a) for a in args]
        aliases = None
        if result is not None:
            args, specs = args + [result], specs + [pl.BlockSpec(memory_space=pl.ANY)]
            aliases = {len(args): 0}
        whole = shape(BF, ROWS, D)
        out_specs = [full(whole, PATCH, clip)]
        scratch = [pltpu.VMEM((D, PATCH), F32)]
        args = [place] + args
        (result,) = once(temporal_end, args, specs, [whole], out_specs, aliases, scratch)
    return result.reshape(2, 1, PATCH, D)


def solution(mesh):
    fine = Mesh(mesh.devices.reshape(2, 2, 2, NY, NZ), ("xl", "c", "xh", "y", "z"))
    time, space = ("xl", "c"), ("xh", "y", "z")
    block = P(None, time, space, None)
    rows = P(space, None)
    return jax.shard_map(
        per_device,
        mesh=fine,
        in_specs=(block, P(), rows, rows, rows, rows, P()),
        out_specs=block,
        check_vma=False,
    )
```
